256 devices in a mesh: dom: 16 (over x, y), tp: 16 (over z, core).
Axes of the slice: x: 4, y: 4, z: 8, core: 2. Of those that a mesh axis runs over, the one named last changes fastest.
Arguments:
- latent: bfloat16 [1024, 65536], P('tp', 'dom'), may hold values from -6 to 6
- w_first: bfloat16 [1024, 1024], P(None, 'tp'), may hold values from -0.1875 to 0.1875
- w_second: bfloat16 [1024, 1024], P('tp'), may hold values from -0.1875 to 0.1875
- w_env: bfloat16 [1024, 256], P('tp'), may hold values from -0.1875 to 0.1875
- edge_vec: float32 [3, 65536], P(None, 'dom'), may hold values from -3 to 3, as said below
- centers: int32 [65536], P('dom'), may hold values from 0 to 127
- block_dest: int32 [512, 1], P('dom'), may hold values from 0 to 15; in each aligned block of 32 rows (0 to 31, 32 to 63, ...) at most 4 rows name the same one
- block_fill: int32 [512], P('dom'), may hold values from 64 to 128
- species: int32 [2048], P('dom'), may hold values from 0 to 3
- species_gain: float32 [4, 256], P(None, 'tp'), may hold values from 0.1 to 1.9
Outputs:
- latent_new: bfloat16 [1024, 65536], P('tp', 'dom')
- env_out: float32 [9, 256, 2048], P(None, 'tp', 'dom')
- invariants: float32 [3, 256, 65536], P(None, 'tp', 'dom')
The draws below stay inside these ranges and needn't reach their ends.
Inputs may be any that keep to these rules, and one draw needn't show every extreme that they name: `block_dest`: in the 32 blocks of one domain no destination domain is named more than 4 times, a bound that some block reaches. `edge_vec`: every component has magnitude 0.5 to 3.
All inputs are finite; a program needn't handle non-finite values.
Results may differ from the reference program's by a relative error of at most 0.0077.
Values may be sent and summed in bfloat16 or wider, within the bound.
A program may use at most 128 MiB of HBM per device.

```python
import math
import jax
import jax.numpy as jnp
import numpy as np
from jax import lax

LAT = 1024
C = 256
NSPEC = 4
NBLK = 32
ATOM_DEV = 128
EDGES = 65536
N_ATOMS = 2048
SLOTS = 4
N_DOM = 16


def draw_edge_vec(key, part):
    key_mag = jax.random.fold_in(key, 11)
    key_sign = jax.random.fold_in(key, 12)
    magnitude = jax.random.uniform(key_mag, (3, EDGES), jnp.float32, 0.5, 3.0)
    flips = jax.random.bernoulli(key_sign, 0.5, (3, EDGES))
    signed = jnp.where(flips, magnitude, -magnitude)
    return signed.astype(jnp.float32)


def set_ends(entries, own_key, low, largest):
    dims = entries.shape
    spot = [jax.random.randint(jax.random.fold_in(own_key, axis), (), 0, dims[axis]) for axis in range(len(dims))]
    entries = entries.at[tuple(spot)].set(low)
    longest = dims.index(max(dims))
    spot[longest] = (spot[longest] + 1) % dims[longest]
    return entries.at[tuple(spot)].set(largest)


def shard_levels(own_key, shape, split, smallest, largest):
    factor_of = 1.0
    for dim, shards_of in split:
        steps = jax.random.uniform(jax.random.fold_in(jax.random.fold_in(own_key, 6), dim), (shards_of,), jnp.float32, smallest / len(split), largest / len(split))
        factor_of = factor_of * jnp.repeat(jnp.exp(steps), shape[dim] // shards_of).reshape((-1,) + (1,) * (len(shape) - 1 - dim))
    return factor_of


def shared_out(rng, own, number, rows, number_of, top, bound, slope):
    sequence = jax.random.permutation(rng, number_of)
    heavy_load, ordinary = portions_of(number_of, rows * top, bound, slope, True), portions_of(number_of, rows * top, bound, slope, False)
    places = jnp.arange(number_of)

    def named(lengths, rotation):
        used = int((lengths > 0).sum())
        fixed = max(1, used // 4)
        shifted = fixed + (places - fixed + rotation * (used - fixed)) % max(1, number_of - fixed)
        return jnp.zeros((number_of,), jnp.int32).at[sequence[jnp.where(places < fixed, places, shifted)]].set(jnp.asarray(lengths, jnp.int32))

    lengths = jnp.where(number % 4 == 0, named(heavy_load, number // 4), named(ordinary, number - number // 4 - 1))
    mixed = jax.random.permutation(jax.random.fold_in(own, 3), number_of)
    donor, taker = mixed[0:number_of // 2 * 2:2], mixed[1:number_of // 2 * 2:2]
    room = jnp.minimum(lengths[donor] - 1, bound - lengths[taker]) // 2
    room = jnp.where((donor == sequence[0]) | (taker == sequence[0]) | (lengths[taker] == 0), 0, jnp.maximum(room, 0))
    shifted = jax.random.randint(jax.random.fold_in(own, 4), (number_of // 2,), 0, 1 << 20) % (room + 1)
    lengths = lengths.at[donor].add(-shifted).at[taker].add(shifted)
    labels = jnp.searchsorted(jnp.cumsum(lengths), jnp.arange(rows * top), side="right").astype(jnp.int32)
    listing = labels.reshape(top, rows).T
    listing = listing[jax.random.permutation(jax.random.fold_in(own, 1), rows)]
    rotation = jax.random.randint(jax.random.fold_in(own, 2), (rows, 1), 0, top)
    return jnp.take_along_axis(listing, (jnp.arange(top)[None, :] + rotation) % top, axis=1)


def portions_of(count, total, most, slope, full):
    portions = [(1 << 20) // math.isqrt(standing ** slope) + 1 for standing in range(1, count + 1)]
    largest = most if full else min(most, max(-(-total // count), total * portions[0] // sum(portions)))
    least = 1 if total - largest >= count - 1 else 0
    counts, spare = [largest] + [least] * (count - 1), total - largest - least * (count - 1)
    while spare > 0:
        free = [i for i in range(1, count) if counts[i] < largest] or [i for i in range(1, count) if counts[i] < most]
        mass, left = sum([portions[i] for i in free]), spare
        for i in free:
            more = min(most - counts[i], max(1, left * portions[i] // mass), spare)
            counts[i] = counts[i] + more
            spare = spare - more
    return np.array(counts)


def gaussian(rng, extent, spread, most, shards=(), held_as=jnp.bfloat16):
    entries = jax.random.normal(rng, extent, jnp.float32) * spread
    if len(shards) > 0:
        entries = shard_levels(rng, extent, shards, -0.22, 0.18) * entries
    return jnp.clip(entries, min=-most, max=most).astype(held_as)


def setup_inputs(seed: int = 0) -> dict:
    seeds = jax.random.split(jax.random.key(seed), 11)
    latent = gaussian(seeds[0], (LAT, EDGES), 1.0, 6.0, ((0, 16), (1, 16)))
    w_first = gaussian(seeds[1], (LAT, LAT), LAT ** -0.5, 0.1875, ((1, 16),))
    w_second = gaussian(seeds[2], (LAT, LAT), LAT ** -0.5, 0.1875, ((0, 16),))
    w_env = gaussian(seeds[3], (LAT, C), LAT ** -0.5, 0.1875, ((0, 16),))
    edge_vec = draw_edge_vec(jax.random.fold_in(seeds[10], 71), 0)
    centers = set_ends(jax.random.randint(seeds[5], (EDGES,), 0, ATOM_DEV), jax.random.fold_in(seeds[5], 1), 0, ATOM_DEV - 1).astype(jnp.int32)
    block_dest_keys = jax.random.split(jax.random.fold_in(seeds[6], 1), (N_DOM * NBLK) // NBLK)
    block_dest_turns = jax.random.permutation(jax.random.fold_in(seeds[6], 3), (N_DOM * NBLK) // NBLK)
    block_dest = jax.vmap(lambda own, number: shared_out(jax.random.fold_in(seeds[6], 2), own, number, NBLK, N_DOM, 1, SLOTS, 2))(block_dest_keys, block_dest_turns).reshape((N_DOM * NBLK, 1))
    block_fill = set_ends(jax.random.randint(seeds[7], (N_DOM * NBLK,), 64, 129), jax.random.fold_in(seeds[7], 1), 64, 128).astype(jnp.int32)
    species = set_ends(jax.random.randint(seeds[8], (N_ATOMS,), 0, NSPEC), jax.random.fold_in(seeds[8], 1), 0, NSPEC - 1).astype(jnp.int32)
    species_gain = jnp.clip(1.0 + 0.18 * jax.random.normal(seeds[9], (NSPEC, C), jnp.float32), 0.1, 1.9)
    return dict(latent=latent, w_first=w_first, w_second=w_second, w_env=w_env, edge_vec=edge_vec, centers=centers, block_dest=block_dest, block_fill=block_fill, species=species, species_gain=species_gain)


root_three = math.sqrt(3.0)
root_five = math.sqrt(5.0)
root_fifteen = math.sqrt(15.0)
cutoff_radius = 6.0
env_factor = 0.25

def harmonics(vectors):
    along_x = vectors[0]
    along_y = vectors[1]
    along_z = vectors[2]
    radius = jnp.sqrt(along_x * along_x + along_y * along_y + along_z * along_z)
    unit_x = along_x / radius
    unit_y = along_y / radius
    unit_z = along_z / radius
    ratio = radius / cutoff_radius
    envelope = (1.0 - ratio * ratio) ** 2
    parts = [jnp.ones_like(unit_x), root_three * unit_x, root_three * unit_y, root_three * unit_z, root_fifteen * unit_x * unit_y, root_fifteen * unit_y * unit_z, root_five / 2.0 * (3.0 * unit_z * unit_z - 1.0), root_fifteen * unit_x * unit_z, root_fifteen / 2.0 * (unit_x * unit_x - unit_y * unit_y)]
    return jnp.stack(parts) * envelope[None, :]

def reference(latent, w_first, w_second, w_env, edge_vec, centers, block_dest, block_fill, species, species_gain):
    hidden = jax.nn.silu(jnp.dot(w_first.T, latent, preferred_element_type=jnp.float32)).astype(jnp.bfloat16)
    update = jnp.dot(w_second.T, hidden, preferred_element_type=jnp.float32)
    latent_new = (latent.astype(jnp.float32) + update).astype(jnp.bfloat16)
    weights = jnp.dot(w_env.T, latent_new, preferred_element_type=jnp.float32).astype(jnp.bfloat16)
    weight_full = weights.astype(jnp.float32)
    harmonic = harmonics(edge_vec)
    edge_ids = jnp.arange(EDGES, dtype=jnp.int32)
    block_of = edge_ids // 128
    position = edge_ids % 128
    alive_mask = (position < block_fill[block_of]).astype(jnp.float32)
    atom = (block_dest[block_of, 0] * ATOM_DEV + centers).astype(jnp.int32)
    contrib = (harmonic[:, None, :] * weight_full[None, :, :] * alive_mask[None, None, :]).astype(jnp.bfloat16)
    flattened = contrib.reshape(9 * C, EDGES).T.astype(jnp.float32)
    summed = jax.ops.segment_sum(flattened, atom, num_segments=N_ATOMS)
    env_raw = summed.T.reshape(9, C, N_ATOMS)
    gain_sel = species_gain[species].T
    env_out = env_raw * gain_sel[None, :, :] * env_factor
    env_edge = env_out.astype(jnp.bfloat16)[:, :, atom].astype(jnp.float32)
    products = env_edge * harmonic[:, None, :]
    degree_sums = jnp.stack([products[0], lax.optimization_barrier(jnp.sum(products[1:4], axis=0)), lax.optimization_barrier(jnp.sum(products[4:9], axis=0))])
    invariants = degree_sums * weight_full[None, :, :] * alive_mask[None, None, :]
    return (latent_new, env_out, invariants)
```

```python
import math

import jax
import jax.numpy as jnp
from jax import lax
from jax.experimental import pallas as pl
from jax.experimental.pallas import tpu as pltpu
from jax.sharding import PartitionSpec as P

MESH = pl.DeviceIdType.MESH
F32 = jnp.float32
BF16 = jnp.bfloat16

root_three = math.sqrt(3.0)
root_five = math.sqrt(5.0)
root_fifteen = math.sqrt(15.0)
cutoff_radius = 6.0
env_factor = 0.25

SIDE = 4
NDOM = 16
NTP = 16


def dot(left, right, dims):
    return lax.dot_general(left, right, (dims, ((), ())), preferred_element_type=F32)


def kernel(
    dest_ref, fill_ref, latent, w1, w2, we, ev_ref, cen_ref, spec_ref, gain_ref,
    ln_out, env_out, inv_out,
    w1_part, pieces, ring, g1, g2, ge, x_in, x_t, hid, lnt, ln, ws, wt, hs, onehot, slots,
    sums, p_out, p_in, table,
    pre_sem, lat_send, lat_recv, one_send, one_recv, a_send, a_recv, b_send, b_recv,
    sib_send, sib_recv, w_send, w_recv, ln_send, ln_recv, q_send, q_recv, t_send, t_recv,
):
    dom = lax.axis_index("dom")
    me = lax.axis_index("tp")
    ax = dom // SIDE
    by = dom % SIDE
    core = me % 2
    sib = me + 1 - 2 * core

    def tp_peer(k):
        return (me + k) % NTP

    def dom_peer(k):
        return (dom + k) % NDOM

    def remote(src, dst, send, recv, to_dom, to_tp):
        return pltpu.make_async_remote_copy(
            src_ref=src, dst_ref=dst, send_sem=send, recv_sem=recv,
            device_id=(to_dom, to_tp), device_id_type=MESH,
        )

    pre = [
        pltpu.make_async_copy(w1.at[pl.ds(by * 256, 256), :], w1_part, pre_sem.at[0]),
        pltpu.make_async_copy(
            latent.at[:, pl.ds(pl.multiple_of(me * 256, 256), 256)], x_in.at[me], pre_sem.at[1]
        ),
    ]
    for half in range(2):
        lanes = pl.ds(pl.multiple_of(by * 256 + 128 * half, 128), 128)
        pre.append(
            pltpu.make_async_copy(
                w2.at[pl.ds(ax * 16, 16), lanes], pieces.at[half, 1], pre_sem.at[2 + half]
            )
        )
        pre.append(
            pltpu.make_async_copy(
                we.at[pl.ds(by * 16, 16), pl.ds(128 * half, 128)],
                pieces.at[half, 2], pre_sem.at[4 + half],
            )
        )
    for copy in pre:
        copy.start()

    barrier = pltpu.get_barrier_semaphore()

    def greet(k, carry):
        pl.semaphore_signal(barrier, inc=1, device_id=(dom, tp_peer(k)), device_id_type=MESH)
        pl.semaphore_signal(barrier, inc=1, device_id=(dom_peer(k), me), device_id_type=MESH)
        return carry

    lax.fori_loop(1, NTP, greet, 0)
    for copy in pre:
        copy.wait()
    pick = (
        lax.broadcasted_iota(jnp.int32, (16, 64), 1)
        == lax.broadcasted_iota(jnp.int32, (16, 64), 0) + ax * 16
    ).astype(F32).astype(BF16)
    turned = dot(pick, w1_part[...], ((1,), (1,))).astype(BF16)
    pieces[0, 0] = turned[:, :128]
    pieces[1, 0] = turned[:, 128:]
    pl.semaphore_wait(barrier, NTP - 1 + NDOM - 1)

    ring[pl.ds(me, 1)] = pieces[pl.ds(core, 1)]

    def one_copy(k):
        to = tp_peer(k)
        return remote(pieces.at[to % 2], ring.at[me], one_send.at[k], one_recv.at[k], dom, to)

    def lat_copy(k):
        to = tp_peer(k)
        return remote(
            latent.at[:, pl.ds(pl.multiple_of(to * 256, 256), 256)], x_in.at[me],
            lat_send.at[k], lat_recv.at[k], dom, to,
        )

    def w_copy(k):
        to = tp_peer(k)
        return remote(ws.at[to], wt.at[me], w_send.at[k], w_recv.at[k], dom, to)

    def ln_copy(k):
        to = tp_peer(k)
        return remote(
            ln.at[to], ln_out.at[:, pl.ds(pl.multiple_of(me * 256, 256), 256)],
            ln_send.at[k], ln_recv.at[k], dom, to,
        )

    def q_copy(k):
        to = dom_peer(k)
        return remote(p_out.at[to], p_in.at[dom], q_send.at[k], q_recv.at[k], to, me)

    def t_copy(k):
        to = dom_peer(k)
        return remote(table.at[dom], table.at[dom], t_send.at[k], t_recv.at[k], to, me)

    def start_all(make):
        def body(k, carry):
            make(k).start()
            return carry

        lax.fori_loop(1, 16, body, 0)

    def recv_all(make):
        def body(k, carry):
            make(k).wait_recv()
            return carry

        lax.fori_loop(1, 16, body, 0)

    def send_all(make):
        def body(k, carry):
            make(k).wait_send()
            return carry

        lax.fori_loop(1, 16, body, 0)

    start_all(one_copy)
    start_all(lat_copy)
    recv_all(one_copy)

    def x_peer(k):
        return ((ax + k) % SIDE) * SIDE + by

    def y_peer(k):
        return ax * SIDE + (by + k) % SIDE

    g1[pl.ds(core, 1), pl.ds(by, 1), pl.ds(ax, 1)] = ring[:, 0][None, None, None]
    g2[pl.ds(core, 1), pl.ds(ax, 1), pl.ds(by, 1)] = ring[:, 1][None, None, None]
    ge[pl.ds(core, 1), :, pl.ds(by, 1)] = ring[:, 2][None, :, None]
    first = []
    for k in range(1, SIDE):
        one = g1.at[core, by, ax]
        first.append(remote(one, one, a_send.at[0, k], a_recv.at[0, k], x_peer(k), me))
        two = g2.at[core, ax, by]
        first.append(remote(two, two, a_send.at[1, k], a_recv.at[1, k], y_peer(k), me))
        three = ge.at[core, :, by]
        first.append(
            remote(ring.at[:, 2], three, a_send.at[2, k], a_recv.at[2, k], y_peer(k), me)
        )
    for copy in first:
        copy.start()

    def harmonics(t, carry):
        v = ev_ref[:, pl.ds(pl.multiple_of(t * 256, 256), 256)]
        along_x, along_y, along_z = v[0:1], v[1:2], v[2:3]
        radius = jnp.sqrt(along_x * along_x + along_y * along_y + along_z * along_z)
        ux = along_x / radius
        uy = along_y / radius
        uz = along_z / radius
        ratio = radius / cutoff_radius
        flat = 1.0 - ratio * ratio
        envelope = flat * flat
        spot = lax.broadcasted_iota(jnp.int32, (1, 128), 1)
        alive = jnp.concatenate(
            [(spot < fill_ref[2 * t + j]).astype(F32) for j in range(2)], axis=1
        )
        rows = [
            envelope,
            root_three * ux * envelope,
            root_three * uy * envelope,
            root_three * uz * envelope,
            root_fifteen * ux * uy * envelope,
            root_fifteen * uy * uz * envelope,
            root_five / 2.0 * (3.0 * uz * uz - 1.0) * envelope,
            root_fifteen * ux * uz * envelope,
            root_fifteen / 2.0 * (ux * ux - uy * uy) * envelope,
            alive,
        ]
        for m, row in enumerate(rows):
            hs[t, m : m + 1, :] = row
        return carry

    lax.fori_loop(0, NTP, harmonics, 0)

    for k in range(SIDE - 1):
        first[3 * k].wait_recv()
        first[3 * k + 1].wait_recv()
    second = []
    for k in range(1, SIDE):
        one = g1.at[core, by]
        second.append(remote(one, one, b_send.at[0, k], b_recv.at[0, k], y_peer(k), me))
        two = g2.at[core, ax]
        second.append(remote(two, two, b_send.at[1, k], b_recv.at[1, k], x_peer(k), me))
    for copy in second:
        copy.start()

    def sib_copy(ref, kind, k):
        return remote(ref, ref, sib_send.at[kind, k], sib_recv.at[kind, k], dom, sib)

    across = [sib_copy(g1.at[core, by], 0, 0), sib_copy(g2.at[core, ax], 1, 0)]
    for copy in across:
        copy.start()

    def make_onehot(b, carry):
        atoms = lax.broadcasted_iota(jnp.int32, (128, 128), 0)
        onehot[b] = (atoms == cen_ref[pl.ds(b, 1), :]).astype(F32).astype(BF16)
        return carry

    lax.fori_loop(0, 32, make_onehot, 0)

    def make_slots(d, carry):
        found = [jnp.int32(32)] * 4
        for b in range(32):
            hit = dest_ref[b, 0] == d
            found = [jnp.where(hit, new, old) for new, old in zip([b] + found[:3], found)]
        for s in range(4):
            slots[4 * d + s] = found[s]
        return carry

    lax.fori_loop(0, NDOM, make_slots, 0)
    sums[32] = jnp.zeros((144, 128), F32)
    same = lax.broadcasted_iota(jnp.int32, (16, 16), 0) == lax.broadcasted_iota(
        jnp.int32, (16, 16), 1
    )
    gain = jnp.zeros((16, 128), F32)
    for s in range(4):
        column = jnp.sum(jnp.where(same, gain_ref[s : s + 1, :], 0.0), axis=1, keepdims=True)
        gain = gain + jnp.where(spec_ref[...] == s, column, 0.0)

    for k in range(SIDE - 1):
        first[3 * k + 2].wait_recv()
    last = sib_copy(ge.at[core], 2, 0)
    last.start()
    across.append(last)

    for k in range(1, SIDE):
        second[2 * k - 2].wait_recv()
        copy = sib_copy(g1.at[core, (by - k + SIDE) % SIDE], 0, k)
        copy.start()
        across.append(copy)
        second[2 * k - 1].wait_recv()
        copy = sib_copy(g2.at[core, (ax - k + SIDE) % SIDE], 1, k)
        copy.start()
        across.append(copy)

    recv_all(lat_copy)
    for n in range(4):
        block = x_in[4 * n : 4 * n + 4].reshape(256, 256).astype(F32)
        x_t[:, 256 * n : 256 * n + 256] = block.T.astype(BF16)

    other = 1 - core

    def sib_arrival(ref, kind, k):
        remote(ref, ref, sib_send.at[kind, k], sib_recv.at[kind, k], dom, sib).wait_recv()

    sib_arrival(g1.at[other, by], 0, 0)
    for k in range(1, SIDE):
        sib_arrival(g1.at[other, (by - k + SIDE) % SIDE], 0, k)

    def first_layer(r, carry):
        matrix = jnp.concatenate(
            [g1[c, b, r].reshape(256, 128) for b in range(SIDE) for c in range(2)], axis=1
        )
        v = dot(x_t[...], matrix, ((1,), (1,)))
        hid[r] = (v / (1.0 + jnp.exp(-v))).astype(BF16)
        return carry

    lax.fori_loop(0, SIDE, first_layer, 0)

    sib_arrival(g2.at[other, ax], 1, 0)
    for k in range(1, SIDE):
        sib_arrival(g2.at[other, (ax - k + SIDE) % SIDE], 1, k)

    for b in range(SIDE):
        update = jnp.zeros((256, 256), F32)
        for r in range(SIDE):
            matrix = jnp.concatenate([g2[c, r, b].reshape(256, 128) for c in range(2)], axis=1)
            update = update + dot(hid[r], matrix, ((1,), (0,)))
        lanes = slice(256 * b, 256 * b + 256)
        lnt[:, lanes] = (x_t[:, lanes].astype(F32) + update).astype(BF16)

    sib_arrival(ge.at[other], 2, 0)
    matrix = jnp.concatenate([ge[c].reshape(1024, 128) for c in range(2)], axis=1)
    env_weights = dot(lnt[...], matrix, ((1,), (0,)))
    ws[...] = env_weights.T.astype(BF16).reshape(16, 16, 256)
    wt[pl.ds(me, 1)] = ws[pl.ds(me, 1)]
    start_all(w_copy)

    for b in range(SIDE):
        block = lnt[:, 256 * b : 256 * b + 256].astype(F32).T.astype(BF16)
        ln[4 * b : 4 * b + 4] = block.reshape(4, 64, 256)
    own = pltpu.make_async_copy(
        ln.at[me], ln_out.at[:, pl.ds(pl.multiple_of(me * 256, 256), 256)], pre_sem.at[6]
    )
    own.start()
    start_all(ln_copy)

    recv_all(w_copy)

    def block_sums(t, carry):
        w = wt[t].astype(F32)
        h = hs[t]
        for j in range(2):
            lanes = slice(128 * j, 128 * j + 128)
            wj = w[:, lanes]
            alive = h[9:10, lanes]
            contrib = jnp.concatenate(
                [((h[m : m + 1, lanes] * wj) * alive).astype(BF16) for m in range(9)], axis=0
            )
            sums[2 * t + j] = dot(contrib, onehot[2 * t + j], ((1,), (1,)))
        return carry

    lax.fori_loop(0, NTP, block_sums, 0)

    def domain_sum(d):
        total = sums[slots[4 * d]] + sums[slots[4 * d + 1]]
        return total + (sums[slots[4 * d + 2]] + sums[slots[4 * d + 3]])

    def send_sums(k, carry):
        to = dom_peer(k)
        p_out[to] = domain_sum(to).astype(BF16)
        q_copy(k).start()
        return carry

    lax.fori_loop(1, NDOM, send_sums, 0)
    total = domain_sum(dom)
    recv_all(q_copy)

    def add(k, total):
        return total + p_in[(dom + k) % NDOM].astype(F32)

    total = lax.fori_loop(1, NDOM, add, total)
    env = total.reshape(9, 16, 128) * gain[None] * env_factor
    env_out[...] = env
    table[pl.ds(dom, 1)] = env.reshape(1, 144, 128).astype(BF16)
    start_all(t_copy)
    recv_all(t_copy)

    def finish(t, carry):
        w = wt[t].astype(F32)
        h = hs[t]
        parts = [[], [], []]
        for j in range(2):
            lanes = slice(128 * j, 128 * j + 128)
            env_edge = dot(table[dest_ref[2 * t + j, 0]], onehot[2 * t + j], ((1,), (0,)))
            terms = [
                env_edge[16 * m : 16 * m + 16] * h[m : m + 1, lanes] for m in range(9)
            ]
            degrees = [
                terms[0],
                terms[1] + terms[2] + terms[3],
                terms[4] + terms[5] + terms[6] + terms[7] + terms[8],
            ]
            for l in range(3):
                parts[l].append(degrees[l] * w[:, lanes] * h[9:10, lanes])
        for l in range(3):
            inv_out[l, :, pl.ds(pl.multiple_of(t * 256, 256), 256)] = jnp.concatenate(
                parts[l], axis=1
            )
        return carry

    lax.fori_loop(0, NTP, finish, 0)

    own.wait()
    recv_all(ln_copy)
    for copy in first + second + across:
        copy.wait_send()
    for make in (one_copy, lat_copy, w_copy, ln_copy, q_copy, t_copy):
        send_all(make)


def on_device(
    latent, w_first, w_second, w_env, edge_vec, centers, block_dest, block_fill, species,
    species_gain,
):
    smem = pl.BlockSpec(memory_space=pltpu.SMEM)
    vmem = pl.BlockSpec(memory_space=pltpu.VMEM)
    anywhere = pl.BlockSpec(memory_space=pl.ANY)
    dma = pltpu.SemaphoreType.DMA
    return pl.pallas_call(
        kernel,
        out_shape=(
            jax.ShapeDtypeStruct((64, 4096), BF16),
            jax.ShapeDtypeStruct((9, 16, 128), F32),
            jax.ShapeDtypeStruct((3, 16, 4096), F32),
        ),
        in_specs=[smem, smem, anywhere, anywhere, anywhere, anywhere, vmem, vmem, vmem, vmem],
        out_specs=(anywhere, vmem, vmem),
        scratch_shapes=[
            pltpu.VMEM((256, 64), BF16),
            pltpu.VMEM((2, 3, 16, 128), BF16),
            pltpu.VMEM((16, 3, 16, 128), BF16),
            pltpu.VMEM((2, 4, 4, 16, 16, 128), BF16),
            pltpu.VMEM((2, 4, 4, 16, 16, 128), BF16),
            pltpu.VMEM((2, 16, 4, 16, 128), BF16),
            pltpu.VMEM((16, 64, 256), BF16),
            pltpu.VMEM((256, 1024), BF16),
            pltpu.VMEM((4, 256, 256), BF16),
            pltpu.VMEM((256, 1024), BF16),
            pltpu.VMEM((16, 64, 256), BF16),
            pltpu.VMEM((16, 16, 256), BF16),
            pltpu.VMEM((16, 16, 256), BF16),
            pltpu.VMEM((16, 16, 256), F32),
            pltpu.VMEM((32, 128, 128), BF16),
            pltpu.SMEM((64,), jnp.int32),
            pltpu.VMEM((33, 144, 128), F32),
            pltpu.VMEM((16, 144, 128), BF16),
            pltpu.VMEM((16, 144, 128), BF16),
            pltpu.VMEM((16, 144, 128), BF16),
            dma((8,)),
            dma((16,)), dma((16,)), dma((16,)), dma((16,)),
            dma((3, 4)), dma((3, 4)), dma((2, 4)), dma((2, 4)), dma((3, 4)), dma((3, 4)),
            dma((16,)), dma((16,)), dma((16,)), dma((16,)),
            dma((16,)), dma((16,)), dma((16,)), dma((16,)),
        ],
        compiler_params=pltpu.CompilerParams(
            collective_id=0, has_side_effects=True, vmem_limit_bytes=40 * 1024 * 1024
        ),
        cost_estimate=pl.CostEstimate(
            flops=2 * 10**9, bytes_accessed=4 * 10**6, transcendentals=300000
        ),
        name="allegro",
    )(
        block_dest, block_fill, latent, w_first, w_second, w_env, edge_vec,
        centers.reshape(32, 128), species.reshape(1, 128), species_gain,
    )


def solution(mesh):
    in_specs = (
        P("tp", "dom"),
        P(None, "tp"),
        P("tp", None),
        P("tp", None),
        P(None, "dom"),
        P("dom"),
        P("dom", None),
        P("dom"),
        P("dom"),
        P(None, "tp"),
    )
    out_specs = (P("tp", "dom"), P(None, "tp", "dom"), P(None, "tp", "dom"))
    return jax.shard_map(
        on_device, mesh=mesh, in_specs=in_specs, out_specs=out_specs, check_vma=False
    )
```

```python
import math

import jax
import jax.numpy as jnp
from jax import lax
from jax.experimental import pallas as pl
from jax.experimental.pallas import tpu as pltpu
from jax.sharding import PartitionSpec as P

MESH = pl.DeviceIdType.MESH
F32 = jnp.float32
BF16 = jnp.bfloat16

root_three = math.sqrt(3.0)
root_five = math.sqrt(5.0)
root_fifteen = math.sqrt(15.0)
cutoff_radius = 6.0
env_factor = 0.25

SIDE = 4
NDOM = 16
NTP = 16
DEPTH = 8
HALF = DEPTH // 2
NEAR_Z = (7, 6, 2, 1, 5, 4, 3)
FAR = sorted(
    [(dx, dy) for dx in range(SIDE) for dy in range(SIDE) if dx or dy],
    key=lambda d: -min(d[0], SIDE - d[0]) - min(d[1], SIDE - d[1]),
)


def dot(left, right, dims):
    return lax.dot_general(left, right, (dims, ((), ())), preferred_element_type=F32)


def kernel(
    dest_ref, fill_ref, latent, w1, w2, we, ev_ref, cen_ref, spec_ref, gain_ref,
    ln_out, env_out, inv_out,
    pieces, ring, own1, own2, g1, g2, ge, x_in, x_t, hid, lnt, ln, ws, wt, hs, onehot, slots,
    sums, p_low, p_high, in_low, in_high, table_low, table_high,
    pre_sem, lat_send, lat_recv, one_send, one_recv, own_send, own_recv,
    a_send, a_recv, b_send, b_recv, e_send, e_recv,
    sib_send, sib_recv, w_send, w_recv, ln_send, ln_recv, q_send, q_recv, t_send, t_recv,
):
    dom = lax.axis_index("dom")
    me = lax.axis_index("tp")
    ax = dom // SIDE
    by = dom % SIDE
    core = me % 2
    other = 1 - core
    z = me // 2
    sib = 2 * z + other

    def tp_far(q):
        s = q // 2
        dz = HALF + (s + 1) // 2 * (1 - 2 * (s % 2))
        return 2 * ((z + dz) % DEPTH) + (core + 1 + q) % 2

    def tp_source(q):
        s = q // 2
        dz = HALF + (s + 1) // 2 * (1 - 2 * (s % 2))
        return 2 * ((z + DEPTH - dz) % DEPTH) + (core + 1 + q) % 2

    def dom_far(q):
        dx, dy = FAR[q]
        return (ax + dx) % SIDE * SIDE + (by + dy) % SIDE

    def x_peer(k):
        return (ax + k) % SIDE * SIDE + by

    def y_peer(k):
        return ax * SIDE + (by + k) % SIDE

    def remote(src, dst, send, recv, to_dom, to_tp):
        return pltpu.make_async_remote_copy(
            src_ref=src, dst_ref=dst, send_sem=send, recv_sem=recv,
            device_id=(to_dom, to_tp), device_id_type=MESH,
        )

    def each(count, act):
        def body(q, carry):
            act(q)
            return carry

        lax.fori_loop(0, count, body, 0)

    pre = [
        pltpu.make_async_copy(
            latent.at[:, pl.ds(pl.multiple_of(me * 256, 256), 256)], x_in.at[me], pre_sem.at[7]
        ),
        pltpu.make_async_copy(w1, own1.at[core], pre_sem.at[8]),
        pltpu.make_async_copy(w2, own2.at[core], pre_sem.at[9]),
    ]
    for half in range(2):
        lanes = pl.ds(pl.multiple_of(by * 256 + 128 * half, 128), 128)
        for i, matrix in enumerate([w1, w2]):
            pre.append(
                pltpu.make_async_copy(
                    matrix.at[pl.ds(ax * 16, 16), lanes],
                    pieces.at[half, i], pre_sem.at[2 * i + half],
                )
            )
        pre.append(
            pltpu.make_async_copy(
                we.at[pl.ds(by * 16, 16), pl.ds(128 * half, 128)],
                pieces.at[half, 2], pre_sem.at[4 + half],
            )
        )
    for copy in pre:
        copy.start()

    barrier = pltpu.get_barrier_semaphore()

    def greet_tp(q):
        pl.semaphore_signal(barrier, inc=1, device_id=(dom, tp_far(q)), device_id_type=MESH)

    each(NTP - 1, greet_tp)
    for q in range(NDOM - 1):
        pl.semaphore_signal(barrier, inc=1, device_id=(dom_far(q), me), device_id_type=MESH)
    for copy in pre:
        copy.wait()
    ring[pl.ds(14 + core, 1)] = pieces[pl.ds(core, 1)]
    pl.semaphore_wait(barrier, NTP - 1 + NDOM - 1)

    def one_copy(n, c):
        to = 2 * ((z + NEAR_Z[n]) % DEPTH) + c
        return remote(
            pieces.at[c], ring.at[2 * n + core], one_send.at[2 * n + c],
            one_recv.at[2 * n + core], dom, to,
        )

    def one_arrival(slot):
        remote(
            pieces.at[0], ring.at[slot], one_send.at[slot], one_recv.at[slot], dom, sib
        ).wait_recv()

    tile_copies = [one_copy(n, c) for n in range(7) for c in range(2)]
    tile_copies.append(
        remote(
            pieces.at[other], ring.at[14 + core], one_send.at[14], one_recv.at[14], dom, sib
        )
    )
    own_copies = [
        remote(ref.at[core], ref.at[core], own_send.at[i], own_recv.at[i], dom, sib)
        for i, ref in enumerate([own1, own2])
    ]
    for copy in tile_copies + own_copies:
        copy.start()

    def lat_copy(q):
        to = tp_far(q)
        return remote(
            latent.at[:, pl.ds(pl.multiple_of(to * 256, 256), 256)], x_in.at[me],
            lat_send.at[q], lat_recv.at[q], dom, to,
        )

    def w_copy(q):
        to = tp_far(q)
        return remote(ws.at[to], wt.at[me], w_send.at[q], w_recv.at[q], dom, to)

    def ln_copy(q):
        to = tp_far(q)
        return remote(
            ln.at[to], ln_out.at[:, pl.ds(pl.multiple_of(me * 256, 256), 256)],
            ln_send.at[q], ln_recv.at[q], dom, to,
        )

    each(15, lambda q: lat_copy(q).start())

    groups = [slice(0, 8), slice(8, 14)]
    spans = [pl.ds(0, 8), pl.ds(8, 6)]
    first = []
    for g in range(2):
        for slot in range(groups[g].start, groups[g].stop):
            one_arrival(slot)
        tiles = ring[groups[g]]
        g1[pl.ds(core, 1), pl.ds(by, 1), pl.ds(ax, 1), groups[g]] = tiles[:, 0][None, None, None]
        g2[pl.ds(core, 1), pl.ds(ax, 1), pl.ds(by, 1), groups[g]] = tiles[:, 1][None, None, None]
        copies = []
        for k in (2, 1, 3):
            one = g1.at[core, by, ax, spans[g]]
            copies.append(remote(one, one, a_send.at[g, 0, k], a_recv.at[g, 0, k], x_peer(k), me))
            two = g2.at[core, ax, by, spans[g]]
            copies.append(remote(two, two, a_send.at[g, 1, k], a_recv.at[g, 1, k], y_peer(k), me))
        for copy in copies:
            copy.start()
        first.append(copies)
    tile_copies[14].wait_recv()
    for n in range(7):
        for c in range(2):
            chip = (z + DEPTH - NEAR_Z[n]) % DEPTH
            ge[pl.ds(core, 1), pl.ds(2 * chip + c, 1), pl.ds(by, 1)] = ring[2 * n + c, 2][
                None, None, None
            ]
    for c in range(2):
        ge[pl.ds(core, 1), pl.ds(2 * z + c, 1), pl.ds(by, 1)] = ring[14 + c, 2][None, None, None]
    env_copies = []
    for k in (2, 1, 3):
        three = ge.at[core, :, by]
        env_copies.append(remote(three, three, e_send.at[k], e_recv.at[k], y_peer(k), me))
    for copy in env_copies:
        copy.start()

    def sib_copy(g, kind, k):
        ref = (
            g1.at[core, (by + SIDE - k) % SIDE, :, spans[g]]
            if kind == 0
            else g2.at[core, (ax + SIDE - k) % SIDE, :, spans[g]]
        )
        return remote(
            ref, ref, sib_send.at[g, kind, k], sib_recv.at[g, kind, k], dom, sib
        )

    second = []
    across = []
    for g in range(2):
        for copy in first[g]:
            copy.wait_recv()
        copies = []
        for k in (2, 1, 3):
            one = g1.at[core, by, :, spans[g]]
            copies.append(remote(one, one, b_send.at[g, 0, k], b_recv.at[g, 0, k], y_peer(k), me))
            two = g2.at[core, ax, :, spans[g]]
            copies.append(remote(two, two, b_send.at[g, 1, k], b_recv.at[g, 1, k], x_peer(k), me))
        for copy in copies:
            copy.start()
        second.append(copies)
        for kind in range(2):
            copy = sib_copy(g, kind, 0)
            copy.start()
            across.append(copy)

    def harmonics(t):
        v = ev_ref[:, pl.ds(pl.multiple_of(t * 256, 256), 256)]
        along_x, along_y, along_z = v[0:1], v[1:2], v[2:3]
        radius = jnp.sqrt(along_x * along_x + along_y * along_y + along_z * along_z)
        ux = along_x / radius
        uy = along_y / radius
        uz = along_z / radius
        ratio = radius / cutoff_radius
        flat = 1.0 - ratio * ratio
        envelope = flat * flat
        spot = lax.broadcasted_iota(jnp.int32, (1, 128), 1)
        alive = jnp.concatenate(
            [(spot < fill_ref[2 * t + j]).astype(F32) for j in range(2)], axis=1
        )
        rows = [
            envelope,
            root_three * ux * envelope,
            root_three * uy * envelope,
            root_three * uz * envelope,
            root_fifteen * ux * uy * envelope,
            root_fifteen * uy * uz * envelope,
            root_five / 2.0 * (3.0 * uz * uz - 1.0) * envelope,
            root_fifteen * ux * uz * envelope,
            root_fifteen / 2.0 * (ux * ux - uy * uy) * envelope,
            alive,
        ]
        for m, row in enumerate(rows):
            hs[t, m : m + 1, :] = row

    each(NTP, harmonics)

    def make_onehot(b):
        atoms = lax.broadcasted_iota(jnp.int32, (128, 128), 0)
        onehot[b] = (atoms == cen_ref[pl.ds(b, 1), :]).astype(F32).astype(BF16)

    each(32, make_onehot)

    def make_slots(d):
        found = [jnp.int32(32)] * 4
        for b in range(32):
            hit = dest_ref[b] == d
            found = [jnp.where(hit, new, old) for new, old in zip([b] + found[:3], found)]
        for s in range(4):
            slots[4 * d + s] = found[s]

    each(NDOM, make_slots)
    sums[32] = jnp.zeros((144, 128), F32)
    same = lax.broadcasted_iota(jnp.int32, (16, 16), 0) == lax.broadcasted_iota(
        jnp.int32, (16, 16), 1
    )
    gain = jnp.zeros((16, 128), F32)
    for s in range(4):
        column = jnp.sum(jnp.where(same, gain_ref[s : s + 1, :], 0.0), axis=1, keepdims=True)
        gain = gain + jnp.where(spec_ref[...] == s, column, 0.0)

    for copy in env_copies:
        copy.wait_recv()
    last = remote(ge.at[core], ge.at[core], own_send.at[2], own_recv.at[2], dom, sib)
    last.start()
    across.append(last)
    for g in range(2):
        for i, k in enumerate((2, 1, 3)):
            for kind in range(2):
                second[g][2 * i + kind].wait_recv()
                copy = sib_copy(g, kind, k)
                copy.start()
                across.append(copy)
        if g == 0:
            each(15, lambda q: lat_copy(q).wait_recv())
            for n in range(4):
                block = x_in[4 * n : 4 * n + 4].reshape(256, 256).astype(F32)
                x_t[:, 256 * n : 256 * n + 256] = block.T.astype(BF16)

    def sib_arrivals(kind):
        own_copies[kind].wait_recv()
        for g in range(2):
            for k in range(SIDE):
                sib_copy(g, kind, k).wait_recv()

    sib_arrivals(0)

    def first_layer(r):
        tiles = jnp.concatenate(
            [g1[c, b, r].reshape(224, 128) for b in range(SIDE) for c in range(2)], axis=1
        )
        rows = pl.ds(pl.multiple_of(16 * r, 16), 16)
        matrix = jnp.concatenate([tiles, own1[0, rows, :], own1[1, rows, :]], axis=0)
        v = dot(x_t[...], matrix, ((1,), (1,)))
        hid[r] = (v / (1.0 + jnp.exp(-v))).astype(BF16)

    each(SIDE, first_layer)
    sib_arrivals(1)
    for b in range(SIDE):
        lanes = slice(256 * b, 256 * b + 256)
        update = jnp.zeros((256, 256), F32)
        for r in range(SIDE):
            tiles = jnp.concatenate([g2[c, r, b].reshape(224, 128) for c in range(2)], axis=1)
            rows = slice(16 * r, 16 * r + 16)
            matrix = jnp.concatenate([tiles, own2[0, rows, lanes], own2[1, rows, lanes]], axis=0)
            update = update + dot(hid[r], matrix, ((1,), (0,)))
        lnt[:, lanes] = (x_t[:, lanes].astype(F32) + update).astype(BF16)

    last.wait_recv()
    matrix = jnp.concatenate([ge[c].reshape(1024, 128) for c in range(2)], axis=1)
    env_weights = dot(lnt[...], matrix, ((1,), (0,)))
    ws[...] = env_weights.T.astype(BF16).reshape(16, 16, 256)
    each(15, lambda q: w_copy(q).start())
    wt[pl.ds(me, 1)] = ws[pl.ds(me, 1)]

    for b in range(SIDE):
        block = lnt[:, 256 * b : 256 * b + 256].astype(F32).T.astype(BF16)
        ln[4 * b : 4 * b + 4] = block.reshape(4, 64, 256)
    own = pltpu.make_async_copy(
        ln.at[me], ln_out.at[:, pl.ds(pl.multiple_of(me * 256, 256), 256)], pre_sem.at[6]
    )
    own.start()
    each(15, lambda q: ln_copy(q).start())

    def block_sums(t):
        w = wt[t].astype(F32)
        h = hs[t]
        for j in range(2):
            lanes = slice(128 * j, 128 * j + 128)
            wj = w[:, lanes]
            alive = h[9:10, lanes]
            contrib = jnp.concatenate(
                [((h[m : m + 1, lanes] * wj) * alive).astype(BF16) for m in range(9)], axis=0
            )
            sums[2 * t + j] = dot(contrib, onehot[2 * t + j], ((1,), (1,)))

    block_sums(me)

    def arrived_sums(q):
        w_copy(14 - q).wait_recv()
        block_sums(tp_source(14 - q))

    each(15, arrived_sums)

    def domain_sum(d):
        total = sums[slots[4 * d]] + sums[slots[4 * d + 1]]
        return total + (sums[slots[4 * d + 2]] + sums[slots[4 * d + 3]])

    def q_copy(part, q):
        out, into = ((p_low, in_low), (p_high, in_high))[part]
        to = dom_far(q)
        return remote(
            out.at[to], into.at[dom], q_send.at[part, q], q_recv.at[part, q], to, me
        )

    def t_copy(part, q):
        ref = (table_low, table_high)[part]
        return remote(
            ref.at[dom], ref.at[dom], t_send.at[part, q], t_recv.at[part, q], dom_far(q), me
        )

    for q in range(NDOM - 1):
        to = dom_far(q)
        total = domain_sum(to).astype(BF16)
        p_low[pl.ds(to, 1)] = total[None, :64]
        p_high[pl.ds(to, 1)] = total[None, 64:]
        q_copy(0, q).start()
    for q in range(NDOM - 1):
        q_copy(1, q).start()
    total = domain_sum(dom)
    for part in range(2):
        into, ref = ((in_low, table_low), (in_high, table_high))[part]
        rows = (slice(0, 64), slice(64, 144))[part]
        comps = (slice(0, 4), slice(4, 9))[part]
        for q in range(NDOM - 1):
            q_copy(part, q).wait_recv()

        def add(k, acc):
            return acc + into[(dom + k) % NDOM].astype(F32)

        acc = lax.fori_loop(1, NDOM, add, total[rows])
        env = acc.reshape(-1, 16, 128) * gain[None] * env_factor
        ref[pl.ds(dom, 1)] = env.reshape(1, -1, 128).astype(BF16)
        for q in range(NDOM - 1):
            t_copy(part, q).start()
        env_out[comps] = env

    def finish(t, part):
        w = wt[t].astype(F32)
        h = hs[t]
        ref = (table_low, table_high)[part]
        base = (0, 4)[part]
        spans_of = (((0,), (1, 2, 3)), ((4, 5, 6, 7, 8),))[part]
        parts = [[] for _ in spans_of]
        for j in range(2):
            lanes = slice(128 * j, 128 * j + 128)
            env_edge = dot(ref[dest_ref[2 * t + j]], onehot[2 * t + j], ((1,), (0,)))
            for l, comps in enumerate(spans_of):
                degree = None
                for m in comps:
                    term = env_edge[16 * (m - base) : 16 * (m - base) + 16] * h[m : m + 1, lanes]
                    degree = term if degree is None else degree + term
                parts[l].append(degree * w[:, lanes] * h[9:10, lanes])
        for l in range(len(spans_of)):
            inv_out[(0, 2)[part] + l, :, pl.ds(pl.multiple_of(t * 256, 256), 256)] = (
                jnp.concatenate(parts[l], axis=1)
            )

    for part in range(2):
        for q in range(NDOM - 1):
            t_copy(part, q).wait_recv()
        each(NTP, lambda t: finish(t, part))

    own.wait()
    each(15, lambda q: ln_copy(q).wait_recv())
    for copy in tile_copies + own_copies + first[0] + first[1] + env_copies:
        copy.wait_send()
    for copy in second[0] + second[1] + across:
        copy.wait_send()
    for make in (lat_copy, w_copy, ln_copy):
        each(15, lambda q: make(q).wait_send())
    for part in range(2):
        for q in range(NDOM - 1):
            q_copy(part, q).wait_send()
            t_copy(part, q).wait_send()


def on_device(
    latent, w_first, w_second, w_env, edge_vec, centers, block_dest, block_fill, species,
    species_gain,
):
    smem = pl.BlockSpec(memory_space=pltpu.SMEM)
    vmem = pl.BlockSpec(memory_space=pltpu.VMEM)
    hbm = pl.BlockSpec(memory_space=pltpu.HBM)
    dma = pltpu.SemaphoreType.DMA
    return pl.pallas_call(
        kernel,
        out_shape=(
            jax.ShapeDtypeStruct((64, 4096), BF16),
            jax.ShapeDtypeStruct((9, 16, 128), F32),
            jax.ShapeDtypeStruct((3, 16, 4096), F32),
        ),
        in_specs=[smem, smem, hbm, hbm, hbm, hbm, vmem, vmem, vmem, vmem],
        out_specs=(vmem, vmem, vmem),
        scratch_shapes=[
            pltpu.VMEM((2, 3, 16, 128), BF16),
            pltpu.VMEM((16, 3, 16, 128), BF16),
            pltpu.VMEM((2, 64, 1024), BF16),
            pltpu.VMEM((2, 64, 1024), BF16),
            pltpu.VMEM((2, 4, 4, 14, 16, 128), BF16),
            pltpu.VMEM((2, 4, 4, 14, 16, 128), BF16),
            pltpu.VMEM((2, 16, 4, 16, 128), BF16),
            pltpu.VMEM((16, 64, 256), BF16),
            pltpu.VMEM((256, 1024), BF16),
            pltpu.VMEM((4, 256, 256), BF16),
            pltpu.VMEM((256, 1024), BF16),
            pltpu.VMEM((16, 64, 256), BF16),
            pltpu.VMEM((16, 16, 256), BF16),
            pltpu.VMEM((16, 16, 256), BF16),
            pltpu.VMEM((16, 16, 256), F32),
            pltpu.VMEM((32, 128, 128), BF16),
            pltpu.SMEM((64,), jnp.int32),
            pltpu.VMEM((33, 144, 128), F32),
            pltpu.VMEM((16, 64, 128), BF16),
            pltpu.VMEM((16, 80, 128), BF16),
            pltpu.VMEM((16, 64, 128), BF16),
            pltpu.VMEM((16, 80, 128), BF16),
            pltpu.VMEM((16, 64, 128), BF16),
            pltpu.VMEM((16, 80, 128), BF16),
            dma((10,)),
            dma((15,)), dma((15,)), dma((15,)), dma((15,)), dma((3,)), dma((3,)),
            dma((2, 2, 4)), dma((2, 2, 4)), dma((2, 2, 4)), dma((2, 2, 4)), dma((4,)), dma((4,)),
            dma((2, 2, 4)), dma((2, 2, 4)),
            dma((15,)), dma((15,)), dma((15,)), dma((15,)),
            dma((2, 15)), dma((2, 15)), dma((2, 15)), dma((2, 15)),
        ],
        compiler_params=pltpu.CompilerParams(
            collective_id=0, has_side_effects=True, vmem_limit_bytes=60 * 1024 * 1024
        ),
        cost_estimate=pl.CostEstimate(
            flops=2 * 10**9, bytes_accessed=4 * 10**6, transcendentals=300000
        ),
        name="allegro",
    )(
        block_dest.reshape(32), block_fill, latent, w_first.T, w_second, w_env, edge_vec,
        centers.reshape(32, 128), species.reshape(1, 128), species_gain,
    )


def solution(mesh):
    in_specs = (
        P("tp", "dom"),
        P(None, "tp"),
        P("tp", None),
        P("tp", None),
        P(None, "dom"),
        P("dom"),
        P("dom", None),
        P("dom"),
        P("dom"),
        P(None, "tp"),
    )
    out_specs = (P("tp", "dom"), P(None, "tp", "dom"), P(None, "tp", "dom"))
    return jax.shard_map(
        on_device, mesh=mesh, in_specs=in_specs, out_specs=out_specs, check_vma=False
    )
```

```python
import math

import jax
import jax.numpy as jnp
from jax import lax
from jax.experimental import pallas as pl
from jax.experimental.pallas import tpu as pltpu
from jax.sharding import PartitionSpec as P

MESH = pl.DeviceIdType.MESH
F32 = jnp.float32
BF16 = jnp.bfloat16

root_three = math.sqrt(3.0)
root_five = math.sqrt(5.0)
root_fifteen = math.sqrt(15.0)
cutoff_radius = 6.0
env_factor = 0.25

SIDE = 4
NDOM = 16
NTP = 16
DEPTH = 8
HALF = DEPTH // 2
NEAR_Z = (6, 2, 7, 1, 4, 5, 3)
FAR = sorted(
    [(dx, dy) for dx in range(SIDE) for dy in range(SIDE) if dx or dy],
    key=lambda d: -min(d[0], SIDE - d[0]) - min(d[1], SIDE - d[1]),
)


def dot(left, right, dims):
    return lax.dot_general(left, right, (dims, ((), ())), preferred_element_type=F32)


def kernel(
    dest, fill, latent, w1, w2, we, ev, cen, spec, gains,
    ln_out, env_out, inv_out,
    dest_ref, fill_ref, ev_ref, cen_ref, spec_ref, gain_ref,
    pieces, ring, own1, own2, g1, g2, ge, x_in, x_t, hid, lnt, ln, ws, wt, hs, onehot, slots,
    sums, p_low, p_high, in_low, in_high, table_low, table_high,
    pre_sem, lat_send, lat_recv, one_send, one_recv, own_send, own_recv,
    a_send, a_recv, b_send, b_recv, e_send, e_recv,
    sib_send, sib_recv, w_send, w_recv, ln_send, ln_recv, q_send, q_recv, t_send, t_recv,
):
    dom = lax.axis_index("dom")
    me = lax.axis_index("tp")
    ax = dom // SIDE
    by = dom % SIDE
    core = me % 2
    other = 1 - core
    z = me // 2
    sib = 2 * z + other

    def tp_far(q):
        s = q // 2
        dz = HALF + (s + 1) // 2 * (1 - 2 * (s % 2))
        return 2 * ((z + dz) % DEPTH) + (core + 1 + q) % 2

    def tp_source(q):
        s = q // 2
        dz = HALF + (s + 1) // 2 * (1 - 2 * (s % 2))
        return 2 * ((z + DEPTH - dz) % DEPTH) + (core + 1 + q) % 2

    def dom_far(q):
        dx, dy = FAR[q]
        return (ax + dx) % SIDE * SIDE + (by + dy) % SIDE

    def x_peer(k):
        return (ax + k) % SIDE * SIDE + by

    def y_peer(k):
        return ax * SIDE + (by + k) % SIDE

    def remote(src, dst, send, recv, to_dom, to_tp):
        return pltpu.make_async_remote_copy(
            src_ref=src, dst_ref=dst, send_sem=send, recv_sem=recv,
            device_id=(to_dom, to_tp), device_id_type=MESH,
        )

    def each(count, act, unroll=1):
        def body(q, carry):
            act(q)
            return carry

        lax.fori_loop(0, count, body, 0, unroll=unroll)

    pre = [
        pltpu.make_async_copy(
            latent.at[:, pl.ds(pl.multiple_of(me * 256, 256), 256)], x_in.at[me], pre_sem.at[7]
        ),
        pltpu.make_async_copy(w1, own1.at[core], pre_sem.at[8]),
        pltpu.make_async_copy(w2, own2.at[core], pre_sem.at[9]),
    ]
    for half in range(2):
        lanes = pl.ds(pl.multiple_of(by * 256 + 128 * half, 128), 128)
        for i, matrix in enumerate([w1, w2]):
            pre.append(
                pltpu.make_async_copy(
                    matrix.at[pl.ds(ax * 16, 16), lanes],
                    pieces.at[half, i], pre_sem.at[2 * i + half],
                )
            )
        pre.append(
            pltpu.make_async_copy(
                we.at[pl.ds(by * 16, 16), pl.ds(128 * half, 128)],
                pieces.at[half, 2], pre_sem.at[4 + half],
            )
        )
    for copy in pre:
        copy.start()

    small = [
        pltpu.make_async_copy(src, dst, pre_sem.at[10 + i])
        for i, (src, dst) in enumerate(
            [
                (dest, dest_ref), (fill, fill_ref), (ev, ev_ref), (cen, cen_ref),
                (spec, spec_ref), (gains, gain_ref),
            ]
        )
    ]
    for copy in small:
        copy.start()
    barrier = pltpu.get_barrier_semaphore()

    def greet_tp(q):
        pl.semaphore_signal(barrier, inc=1, device_id=(dom, tp_far(q)), device_id_type=MESH)

    each(NTP - 1, greet_tp)
    for q in range(NDOM - 1):
        pl.semaphore_signal(barrier, inc=1, device_id=(dom_far(q), me), device_id_type=MESH)
    for copy in pre:
        copy.wait()
    ring[pl.ds(14 + core, 1)] = pieces[pl.ds(core, 1)]
    pl.semaphore_wait(barrier, NTP - 1 + NDOM - 1)

    def one_copy(n, c):
        to = 2 * ((z + NEAR_Z[n]) % DEPTH) + c
        return remote(
            pieces.at[c], ring.at[2 * n + core], one_send.at[2 * n + c],
            one_recv.at[2 * n + core], dom, to,
        )

    def one_arrival(slot):
        remote(
            pieces.at[0], ring.at[slot], one_send.at[slot], one_recv.at[slot], dom, sib
        ).wait_recv()

    tile_copies = [one_copy(n, c) for n in range(7) for c in range(2)]
    tile_copies.append(
        remote(
            pieces.at[other], ring.at[14 + core], one_send.at[14], one_recv.at[14], dom, sib
        )
    )
    own_copies = [
        remote(ref.at[core], ref.at[core], own_send.at[i], own_recv.at[i], dom, sib)
        for i, ref in enumerate([own1, own2])
    ]
    for copy in tile_copies + own_copies:
        copy.start()

    def lat_copy(q):
        to = tp_far(q)
        return remote(
            latent.at[:, pl.ds(pl.multiple_of(to * 256, 256), 256)], x_in.at[me],
            lat_send.at[q], lat_recv.at[q], dom, to,
        )

    def w_copy(q):
        to = tp_far(q)
        return remote(ws.at[to], wt.at[me], w_send.at[q], w_recv.at[q], dom, to)

    def ln_copy(q):
        to = tp_far(q)
        return remote(
            ln.at[to], ln_out.at[:, pl.ds(pl.multiple_of(me * 256, 256), 256)],
            ln_send.at[q], ln_recv.at[q], dom, to,
        )

    groups = [slice(0, 8), slice(8, 14)]
    spans = [pl.ds(0, 8), pl.ds(8, 6)]

    def sib_copy(g, kind, k):
        ref = (
            g1.at[core, (by + SIDE - k) % SIDE, :, spans[g]]
            if kind == 0
            else g2.at[core, (ax + SIDE - k) % SIDE, :, spans[g]]
        )
        return remote(
            ref, ref, sib_send.at[g, kind, k], sib_recv.at[g, kind, k], dom, sib
        )

    first = []
    second = []
    across = []
    for g in range(2):
        for slot in range(groups[g].start, groups[g].stop):
            one_arrival(slot)
        tiles = ring[groups[g]]
        g1[pl.ds(core, 1), pl.ds(by, 1), pl.ds(ax, 1), groups[g]] = tiles[:, 0][None, None, None]
        g2[pl.ds(core, 1), pl.ds(ax, 1), pl.ds(by, 1), groups[g]] = tiles[:, 1][None, None, None]
        copies = []
        for k in (2, 1, 3):
            one = g1.at[core, by, ax, spans[g]]
            copies.append(remote(one, one, a_send.at[g, 0, k], a_recv.at[g, 0, k], x_peer(k), me))
            two = g2.at[core, ax, by, spans[g]]
            copies.append(remote(two, two, a_send.at[g, 1, k], a_recv.at[g, 1, k], y_peer(k), me))
        for copy in copies:
            copy.start()
        first.append(copies)
        if g == 1:
            each(15, lambda q: lat_copy(q).start())
        for copy in copies:
            copy.wait_recv()
        copies = []
        for k in (2, 1, 3):
            one = g1.at[core, by, :, spans[g]]
            copies.append(remote(one, one, b_send.at[g, 0, k], b_recv.at[g, 0, k], y_peer(k), me))
            two = g2.at[core, ax, :, spans[g]]
            copies.append(remote(two, two, b_send.at[g, 1, k], b_recv.at[g, 1, k], x_peer(k), me))
        for copy in copies:
            copy.start()
        second.append(copies)
        for kind in range(2):
            copy = sib_copy(g, kind, 0)
            copy.start()
            across.append(copy)

    tile_copies[14].wait_recv()
    for n in range(7):
        for c in range(2):
            chip = (z + DEPTH - NEAR_Z[n]) % DEPTH
            ge[pl.ds(core, 1), pl.ds(2 * chip + c, 1), pl.ds(by, 1)] = ring[2 * n + c, 2][
                None, None, None
            ]
    for c in range(2):
        ge[pl.ds(core, 1), pl.ds(2 * z + c, 1), pl.ds(by, 1)] = ring[14 + c, 2][None, None, None]
    env_copies = []
    for k in (2, 1, 3):
        three = ge.at[core, :, by]
        env_copies.append(remote(three, three, e_send.at[k], e_recv.at[k], y_peer(k), me))
    for copy in env_copies:
        copy.start()

    for copy in small:
        copy.wait()

    def harmonics(t):
        v = ev_ref[:, pl.ds(pl.multiple_of(t * 256, 256), 256)]
        along_x, along_y, along_z = v[0:1], v[1:2], v[2:3]
        radius = jnp.sqrt(along_x * along_x + along_y * along_y + along_z * along_z)
        ux = along_x / radius
        uy = along_y / radius
        uz = along_z / radius
        ratio = radius / cutoff_radius
        flat = 1.0 - ratio * ratio
        envelope = flat * flat
        spot = lax.broadcasted_iota(jnp.int32, (1, 128), 1)
        alive = jnp.concatenate(
            [(spot < fill_ref[2 * t + j]).astype(F32) for j in range(2)], axis=1
        )
        rows = [
            envelope,
            root_three * ux * envelope,
            root_three * uy * envelope,
            root_three * uz * envelope,
            root_fifteen * ux * uy * envelope,
            root_fifteen * uy * uz * envelope,
            root_five / 2.0 * (3.0 * uz * uz - 1.0) * envelope,
            root_fifteen * ux * uz * envelope,
            root_fifteen / 2.0 * (ux * ux - uy * uy) * envelope,
            alive,
        ]
        for m, row in enumerate(rows):
            hs[t, m : m + 1, :] = row

    each(NTP, harmonics)

    def make_onehot(b):
        atoms = lax.broadcasted_iota(jnp.int32, (128, 128), 0)
        onehot[b] = (atoms == cen_ref[pl.ds(b, 1), :]).astype(F32).astype(BF16)

    each(32, make_onehot)

    def make_slots(d):
        found = [jnp.int32(32)] * 4
        for b in range(32):
            hit = dest_ref[b] == d
            found = [jnp.where(hit, new, old) for new, old in zip([b] + found[:3], found)]
        for s in range(4):
            slots[4 * d + s] = found[s]

    each(NDOM, make_slots)
    sums[32] = jnp.zeros((144, 128), F32)
    same = lax.broadcasted_iota(jnp.int32, (16, 16), 0) == lax.broadcasted_iota(
        jnp.int32, (16, 16), 1
    )
    gain = jnp.zeros((16, 128), F32)
    for s in range(4):
        column = jnp.sum(jnp.where(same, gain_ref[s : s + 1, :], 0.0), axis=1, keepdims=True)
        gain = gain + jnp.where(spec_ref[...] == s, column, 0.0)

    for copy in env_copies:
        copy.wait_recv()
    last = remote(ge.at[core], ge.at[core], own_send.at[2], own_recv.at[2], dom, sib)
    last.start()
    across.append(last)
    for g in range(2):
        for i, k in enumerate((2, 1, 3)):
            for kind in range(2):
                second[g][2 * i + kind].wait_recv()
                copy = sib_copy(g, kind, k)
                copy.start()
                across.append(copy)
        if g == 0:
            each(15, lambda q: lat_copy(q).wait_recv())
            for n in range(4):
                block = x_in[4 * n : 4 * n + 4].reshape(256, 256).astype(F32)
                x_t[:, 256 * n : 256 * n + 256] = block.T.astype(BF16)

    def sib_arrivals(kind):
        own_copies[kind].wait_recv()
        for g in range(2):
            for k in range(SIDE):
                sib_copy(g, kind, k).wait_recv()

    sib_arrivals(0)

    def first_layer(r):
        tiles = jnp.concatenate(
            [g1[c, b, r].reshape(224, 128) for b in range(SIDE) for c in range(2)], axis=1
        )
        rows = pl.ds(pl.multiple_of(16 * r, 16), 16)
        matrix = jnp.concatenate([tiles, own1[0, rows, :], own1[1, rows, :]], axis=0)
        v = dot(x_t[...], matrix, ((1,), (1,)))
        hid[r] = (v / (1.0 + jnp.exp(-v))).astype(BF16)

    each(SIDE, first_layer)
    sib_arrivals(1)
    for b in range(SIDE):
        lanes = slice(256 * b, 256 * b + 256)
        update = jnp.zeros((256, 256), F32)
        for r in range(SIDE):
            tiles = jnp.concatenate([g2[c, r, b].reshape(224, 128) for c in range(2)], axis=1)
            rows = slice(16 * r, 16 * r + 16)
            matrix = jnp.concatenate([tiles, own2[0, rows, lanes], own2[1, rows, lanes]], axis=0)
            update = update + dot(hid[r], matrix, ((1,), (0,)))
        lnt[:, lanes] = (x_t[:, lanes].astype(F32) + update).astype(BF16)

    last.wait_recv()
    matrix = jnp.concatenate([ge[c].reshape(1024, 128) for c in range(2)], axis=1)
    env_weights = dot(lnt[...], matrix, ((1,), (0,)))
    ws[...] = env_weights.T.astype(BF16).reshape(16, 16, 256)
    each(15, lambda q: w_copy(q).start())
    wt[pl.ds(me, 1)] = ws[pl.ds(me, 1)]

    for b in range(SIDE):
        block = lnt[:, 256 * b : 256 * b + 256].astype(F32).T.astype(BF16)
        ln[4 * b : 4 * b + 4] = block.reshape(4, 64, 256)
    def block_sums(t):
        w = wt[t].astype(F32)
        h = hs[t]
        for j in range(2):
            lanes = slice(128 * j, 128 * j + 128)
            wj = w[:, lanes]
            alive = h[9:10, lanes]
            contrib = jnp.concatenate(
                [((h[m : m + 1, lanes] * wj) * alive).astype(BF16) for m in range(9)], axis=0
            )
            sums[2 * t + j] = dot(contrib, onehot[2 * t + j], ((1,), (1,)))

    block_sums(me)

    def arrived_sums(q):
        w_copy(14 - q).wait_recv()
        block_sums(tp_source(14 - q))

    each(15, arrived_sums)

    def domain_sum(d):
        total = sums[slots[4 * d]] + sums[slots[4 * d + 1]]
        return total + (sums[slots[4 * d + 2]] + sums[slots[4 * d + 3]])

    def q_copy(part, q):
        out, into = ((p_low, in_low), (p_high, in_high))[part]
        to = dom_far(q)
        return remote(
            out.at[to], into.at[dom], q_send.at[part, q], q_recv.at[part, q], to, me
        )

    def t_copy(part, q):
        ref = (table_low, table_high)[part]
        return remote(
            ref.at[dom], ref.at[dom], t_send.at[part, q], t_recv.at[part, q], dom_far(q), me
        )

    for q in range(NDOM - 1):
        to = dom_far(q)
        total = domain_sum(to).astype(BF16)
        p_low[pl.ds(to, 1)] = total[None, :64]
        p_high[pl.ds(to, 1)] = total[None, 64:]
        q_copy(0, q).start()
    for q in range(NDOM - 1):
        q_copy(1, q).start()
    own = pltpu.make_async_copy(
        ln.at[me], ln_out.at[:, pl.ds(pl.multiple_of(me * 256, 256), 256)], pre_sem.at[6]
    )
    own.start()
    each(15, lambda q: ln_copy(q).start())
    total = domain_sum(dom)
    for part in range(2):
        into, ref = ((in_low, table_low), (in_high, table_high))[part]
        rows = (slice(0, 64), slice(64, 144))[part]
        comps = (slice(0, 4), slice(4, 9))[part]
        for q in range(NDOM - 1):
            q_copy(part, q).wait_recv()

        def add(k, acc):
            return acc + into[(dom + k) % NDOM].astype(F32)

        acc = lax.fori_loop(1, NDOM, add, total[rows])
        env = acc.reshape(-1, 16, 128) * gain[None] * env_factor
        ref[pl.ds(dom, 1)] = env.reshape(1, -1, 128).astype(BF16)
        for q in range(NDOM - 1):
            t_copy(part, q).start()
        env_out[comps] = env

    def finish(t, part):
        w = wt[t].astype(F32)
        h = hs[t]
        ref = (table_low, table_high)[part]
        base = (0, 4)[part]
        spans_of = (((0,), (1, 2, 3)), ((4, 5, 6, 7, 8),))[part]
        parts = [[] for _ in spans_of]
        for j in range(2):
            lanes = slice(128 * j, 128 * j + 128)
            env_edge = dot(ref[dest_ref[2 * t + j]], onehot[2 * t + j], ((1,), (0,)))
            for l, comps in enumerate(spans_of):
                degree = None
                for m in comps:
                    term = env_edge[16 * (m - base) : 16 * (m - base) + 16] * h[m : m + 1, lanes]
                    degree = term if degree is None else degree + term
                parts[l].append(degree * w[:, lanes] * h[9:10, lanes])
        for l in range(len(spans_of)):
            inv_out[(0, 2)[part] + l, :, pl.ds(pl.multiple_of(t * 256, 256), 256)] = (
                jnp.concatenate(parts[l], axis=1)
            )

    for part in range(2):
        for q in range(NDOM - 1):
            t_copy(part, q).wait_recv()
        each(NTP, lambda t: finish(t, part), unroll=4)

    own.wait()
    each(15, lambda q: ln_copy(q).wait_recv())
    for copy in tile_copies + own_copies + first[0] + first[1] + env_copies:
        copy.wait_send()
    for copy in second[0] + second[1] + across:
        copy.wait_send()
    for make in (lat_copy, w_copy, ln_copy):
        each(15, lambda q: make(q).wait_send())
    for part in range(2):
        for q in range(NDOM - 1):
            q_copy(part, q).wait_send()
            t_copy(part, q).wait_send()


def write_out(ln_in, env_in, inv_in, ln_out, env_out, inv_out, ln, env, inv, sem_in, sem_out):
    parts = [(env_in, env, env_out)]
    for n in range(2):
        rows = pl.ds(32 * n, 32)
        parts.append((ln_in.at[rows], ln.at[rows], ln_out.at[rows]))
    for l in range(3):
        parts.append((inv_in.at[l], inv.at[l], inv_out.at[l]))
    reads = [
        pltpu.make_async_copy(src, mid, sem_in.at[n]) for n, (src, mid, _) in enumerate(parts)
    ]
    writes = [
        pltpu.make_async_copy(mid, dst, sem_out.at[n]) for n, (_, mid, dst) in enumerate(parts)
    ]
    for copy in reads:
        copy.start()
    for read, write in zip(reads, writes):
        read.wait()
        write.start()
    for copy in writes:
        copy.wait()


def on_device(
    latent, w_first, w_second, w_env, edge_vec, centers, block_dest, block_fill, species,
    species_gain,
):
    vmem = pl.BlockSpec(memory_space=pltpu.VMEM)
    hbm = pl.BlockSpec(memory_space=pltpu.HBM)
    dma = pltpu.SemaphoreType.DMA
    shapes = (
        jax.ShapeDtypeStruct((64, 4096), BF16),
        jax.ShapeDtypeStruct((9, 16, 128), F32),
        jax.ShapeDtypeStruct((3, 16, 4096), F32),
    )
    results = pl.pallas_call(
        kernel,
        out_shape=shapes,
        in_specs=[hbm] * 10,
        out_specs=(vmem, vmem, vmem),
        scratch_shapes=[
            pltpu.SMEM((32,), jnp.int32),
            pltpu.SMEM((32,), jnp.int32),
            pltpu.VMEM((3, 4096), F32),
            pltpu.VMEM((32, 128), jnp.int32),
            pltpu.VMEM((1, 128), jnp.int32),
            pltpu.VMEM((4, 16), F32),
            pltpu.VMEM((2, 3, 16, 128), BF16),
            pltpu.VMEM((16, 3, 16, 128), BF16),
            pltpu.VMEM((2, 64, 1024), BF16),
            pltpu.VMEM((2, 64, 1024), BF16),
            pltpu.VMEM((2, 4, 4, 14, 16, 128), BF16),
            pltpu.VMEM((2, 4, 4, 14, 16, 128), BF16),
            pltpu.VMEM((2, 16, 4, 16, 128), BF16),
            pltpu.VMEM((16, 64, 256), BF16),
            pltpu.VMEM((256, 1024), BF16),
            pltpu.VMEM((4, 256, 256), BF16),
            pltpu.VMEM((256, 1024), BF16),
            pltpu.VMEM((16, 64, 256), BF16),
            pltpu.VMEM((16, 16, 256), BF16),
            pltpu.VMEM((16, 16, 256), BF16),
            pltpu.VMEM((16, 16, 256), F32),
            pltpu.VMEM((32, 128, 128), BF16),
            pltpu.SMEM((64,), jnp.int32),
            pltpu.VMEM((33, 144, 128), F32),
            pltpu.VMEM((16, 64, 128), BF16),
            pltpu.VMEM((16, 80, 128), BF16),
            pltpu.VMEM((16, 64, 128), BF16),
            pltpu.VMEM((16, 80, 128), BF16),
            pltpu.VMEM((16, 64, 128), BF16),
            pltpu.VMEM((16, 80, 128), BF16),
            dma((16,)),
            dma((15,)), dma((15,)), dma((15,)), dma((15,)), dma((3,)), dma((3,)),
            dma((2, 2, 4)), dma((2, 2, 4)), dma((2, 2, 4)), dma((2, 2, 4)), dma((4,)), dma((4,)),
            dma((2, 2, 4)), dma((2, 2, 4)),
            dma((15,)), dma((15,)), dma((15,)), dma((15,)),
            dma((2, 15)), dma((2, 15)), dma((2, 15)), dma((2, 15)),
        ],
        compiler_params=pltpu.CompilerParams(
            collective_id=0, has_side_effects=True, vmem_limit_bytes=60 * 1024 * 1024
        ),
        cost_estimate=pl.CostEstimate(
            flops=2 * 10**9, bytes_accessed=4 * 10**6, transcendentals=300000
        ),
        name="allegro",
    )(
        block_dest.reshape(32), block_fill, latent, w_first.T, w_second, w_env, edge_vec,
        centers.reshape(32, 128), species.reshape(1, 128), species_gain,
    )
    return pl.pallas_call(
        write_out,
        out_shape=shapes,
        in_specs=[hbm] * 3,
        out_specs=(hbm,) * 3,
        scratch_shapes=[
            pltpu.VMEM((64, 4096), BF16),
            pltpu.VMEM((9, 16, 128), F32),
            pltpu.VMEM((3, 16, 4096), F32),
            dma((6,)),
            dma((6,)),
        ],
        compiler_params=pltpu.CompilerParams(vmem_limit_bytes=60 * 1024 * 1024),
        name="write_out",
    )(*results)


def solution(mesh):
    in_specs = (
        P("tp", "dom"),
        P(None, "tp"),
        P("tp", None),
        P("tp", None),
        P(None, "dom"),
        P("dom"),
        P("dom", None),
        P("dom"),
        P("dom"),
        P(None, "tp"),
    )
    out_specs = (P("tp", "dom"), P(None, "tp", "dom"), P(None, "tp", "dom"))
    return jax.shard_map(
        on_device, mesh=mesh, in_specs=in_specs, out_specs=out_specs, check_vma=False
    )
```

```python
import math

import jax
import jax.numpy as jnp
from jax import lax
from jax.experimental import pallas as pl
from jax.experimental.pallas import tpu as pltpu
from jax.sharding import PartitionSpec as P

MESH = pl.DeviceIdType.MESH
F32 = jnp.float32
BF16 = jnp.bfloat16

root_three = math.sqrt(3.0)
root_five = math.sqrt(5.0)
root_fifteen = math.sqrt(15.0)
cutoff_radius = 6.0
env_factor = 0.25

SIDE = 4
NDOM = 16
NTP = 16
DEPTH = 8
HALF = DEPTH // 2
NEAR_Z = (6, 2, 7, 1, 4, 5, 3)
FAR = sorted(
    [(dx, dy) for dx in range(SIDE) for dy in range(SIDE) if dx or dy],
    key=lambda d: -min(d[0], SIDE - d[0]) - min(d[1], SIDE - d[1]),
)


def dot(left, right, dims):
    return lax.dot_general(left, right, (dims, ((), ())), preferred_element_type=F32)


def kernel(
    dest, fill, latent, w1, w2, we, ev, cen, spec, gains,
    ln_out, env_out, inv_out,
    dest_ref, fill_ref, ev_ref, cen_ref, spec_ref, gain_ref,
    pieces, ring, own1, own2, g1, g2, ge, x_in, x_t, hid, lnt, ln, ws, wt, hs, onehot, slots,
    sums, p_low, p_high, in_low, in_high, table_low, table_high,
    pre_sem, lat_send, lat_recv, one_send, one_recv, own_send, own_recv,
    a_send, a_recv, b_send, b_recv, e_send, e_recv,
    sib_send, sib_recv, w_send, w_recv, ln_send, ln_recv, q_send, q_recv, t_send, t_recv,
):
    dom = lax.axis_index("dom")
    me = lax.axis_index("tp")
    ax = dom // SIDE
    by = dom % SIDE
    core = me % 2
    other = 1 - core
    z = me // 2
    sib = 2 * z + other

    def tp_far(q):
        s = q // 2
        dz = HALF + (s + 1) // 2 * (1 - 2 * (s % 2))
        return 2 * ((z + dz) % DEPTH) + (core + 1 + q) % 2

    def dom_far(q):
        dx, dy = FAR[q]
        return (ax + dx) % SIDE * SIDE + (by + dy) % SIDE

    def x_peer(k):
        return (ax + k) % SIDE * SIDE + by

    def y_peer(k):
        return ax * SIDE + (by + k) % SIDE

    def remote(src, dst, send, recv, to_dom, to_tp):
        return pltpu.make_async_remote_copy(
            src_ref=src, dst_ref=dst, send_sem=send, recv_sem=recv,
            device_id=(to_dom, to_tp), device_id_type=MESH,
        )

    def each(count, act, unroll=1):
        def body(q, carry):
            act(q)
            return carry

        lax.fori_loop(0, count, body, 0, unroll=unroll)

    pre = [
        pltpu.make_async_copy(
            latent.at[:, pl.ds(pl.multiple_of(me * 256, 256), 256)], x_in.at[me], pre_sem.at[7]
        ),
        pltpu.make_async_copy(w1, own1.at[core], pre_sem.at[8]),
        pltpu.make_async_copy(w2, own2.at[core], pre_sem.at[9]),
    ]
    for half in range(2):
        lanes = pl.ds(pl.multiple_of(by * 256 + 128 * half, 128), 128)
        for i, matrix in enumerate([w1, w2]):
            pre.append(
                pltpu.make_async_copy(
                    matrix.at[pl.ds(ax * 16, 16), lanes],
                    pieces.at[half, i], pre_sem.at[2 * i + half],
                )
            )
        pre.append(
            pltpu.make_async_copy(
                we.at[pl.ds((by, ax)[half] * 16, 16), pl.ds(128 * half, 128)],
                pieces.at[half, 2], pre_sem.at[4 + half],
            )
        )
    for copy in pre:
        copy.start()

    small = [
        pltpu.make_async_copy(src, dst, pre_sem.at[10 + i])
        for i, (src, dst) in enumerate(
            [
                (dest, dest_ref), (fill, fill_ref), (ev, ev_ref), (cen, cen_ref),
                (spec, spec_ref), (gains, gain_ref),
            ]
        )
    ]
    for copy in small:
        copy.start()
    barrier = pltpu.get_barrier_semaphore()

    def greet_tp(q):
        pl.semaphore_signal(barrier, inc=1, device_id=(dom, tp_far(q)), device_id_type=MESH)

    each(NTP - 1, greet_tp)
    for q in range(NDOM - 1):
        pl.semaphore_signal(barrier, inc=1, device_id=(dom_far(q), me), device_id_type=MESH)
    for copy in pre:
        copy.wait()
    ring[pl.ds(14 + core, 1)] = pieces[pl.ds(core, 1)]
    pl.semaphore_wait(barrier, NTP - 1 + NDOM - 1)

    def one_copy(n, c):
        to = 2 * ((z + NEAR_Z[n]) % DEPTH) + c
        return remote(
            pieces.at[c], ring.at[2 * n + core], one_send.at[2 * n + c],
            one_recv.at[2 * n + core], dom, to,
        )

    def one_arrival(slot):
        remote(
            pieces.at[0], ring.at[slot], one_send.at[slot], one_recv.at[slot], dom, sib
        ).wait_recv()

    tile_copies = [one_copy(n, c) for n in range(7) for c in range(2)]
    tile_copies.append(
        remote(
            pieces.at[other], ring.at[14 + core], one_send.at[14], one_recv.at[14], dom, sib
        )
    )
    own_copies = [
        remote(ref.at[core], ref.at[core], own_send.at[i], own_recv.at[i], dom, sib)
        for i, ref in enumerate([own1, own2])
    ]
    for copy in tile_copies + own_copies:
        copy.start()

    def lat_copy(q):
        to = tp_far(q)
        return remote(
            latent.at[:, pl.ds(pl.multiple_of(to * 256, 256), 256)], x_in.at[me],
            lat_send.at[q], lat_recv.at[q], dom, to,
        )

    def w_copy(q):
        to = tp_far(q)
        return remote(ws.at[to], wt.at[me], w_send.at[q], w_recv.at[q], dom, to)

    def ln_copy(q):
        to = tp_far(q)
        return remote(
            ln.at[to], ln_out.at[:, pl.ds(pl.multiple_of(me * 256, 256), 256)],
            ln_send.at[q], ln_recv.at[q], dom, to,
        )

    for copy in small:
        copy.wait()

    def harmonics(t):
        v = ev_ref[:, pl.ds(pl.multiple_of(t * 256, 256), 256)]
        along_x, along_y, along_z = v[0:1], v[1:2], v[2:3]
        radius = jnp.sqrt(along_x * along_x + along_y * along_y + along_z * along_z)
        ux = along_x / radius
        uy = along_y / radius
        uz = along_z / radius
        ratio = radius / cutoff_radius
        flat = 1.0 - ratio * ratio
        envelope = flat * flat
        spot = lax.broadcasted_iota(jnp.int32, (1, 128), 1)
        alive = jnp.concatenate(
            [(spot < fill_ref[2 * t + j]).astype(F32) for j in range(2)], axis=1
        )
        rows = [
            envelope,
            root_three * ux * envelope,
            root_three * uy * envelope,
            root_three * uz * envelope,
            root_fifteen * ux * uy * envelope,
            root_fifteen * uy * uz * envelope,
            root_five / 2.0 * (3.0 * uz * uz - 1.0) * envelope,
            root_fifteen * ux * uz * envelope,
            root_fifteen / 2.0 * (ux * ux - uy * uy) * envelope,
            alive,
        ]
        for m, row in enumerate(rows):
            hs[t, m : m + 1, :] = row

    each(NTP, harmonics)

    def make_onehot(b):
        atoms = lax.broadcasted_iota(jnp.int32, (128, 128), 0)
        onehot[b] = (atoms == cen_ref[pl.ds(b, 1), :]).astype(F32).astype(BF16)

    each(32, make_onehot)

    groups = [slice(0, 8), slice(8, 14)]
    spans = [pl.ds(0, 8), pl.ds(8, 6)]

    def quad(g, kind, k, half=None):
        part = slice(None) if half is None else pl.ds(2 * half, 2)
        if kind == 0:
            return g1.at[core, (by + SIDE - k) % SIDE, part, spans[g]]
        return g2.at[core, (ax + SIDE - k) % SIDE, part, spans[g]]

    def sib_copy(g, kind, k, half=None):
        ref = quad(g, kind, k, half)
        slot = k if half is None else 2 + 2 * half
        return remote(
            ref, ref, sib_send.at[g, kind, slot], sib_recv.at[g, kind, slot], dom, sib
        )

    def second_peer(kind, k):
        return (y_peer, x_peer)[kind](k)

    first = []
    second = []
    across = []
    env_row = by * other + ax * core
    env_copies = []
    for g in range(2):
        for slot in range(groups[g].start, groups[g].stop):
            one_arrival(slot)
        tiles = ring[groups[g]]
        g1[pl.ds(core, 1), pl.ds(by, 1), pl.ds(ax, 1), groups[g]] = tiles[:, 0][None, None, None]
        g2[pl.ds(core, 1), pl.ds(ax, 1), pl.ds(by, 1), groups[g]] = tiles[:, 1][None, None, None]
        copies = []
        for k in (2, 1, 3):
            one = g1.at[core, by, ax, spans[g]]
            copies.append(remote(one, one, a_send.at[g, 0, k], a_recv.at[g, 0, k], x_peer(k), me))
            two = g2.at[core, ax, by, spans[g]]
            copies.append(remote(two, two, a_send.at[g, 1, k], a_recv.at[g, 1, k], y_peer(k), me))
        for copy in copies:
            copy.start()
        first.append(copies)
        if g == 1:
            each(15, lambda q: lat_copy(q).start())
            tile_copies[14].wait_recv()
            for n in range(7):
                for c in range(2):
                    chip = (z + DEPTH - NEAR_Z[n]) % DEPTH
                    ge[pl.ds(core, 1), pl.ds(2 * chip + c, 1), pl.ds(env_row, 1)] = ring[
                        2 * n + c, 2
                    ][None, None, None]
            for c in range(2):
                ge[pl.ds(core, 1), pl.ds(2 * z + c, 1), pl.ds(env_row, 1)] = ring[14 + c, 2][
                    None, None, None
                ]
            for k in (2, 1, 3):
                three = ge.at[core, :, env_row]
                to = (ax + k * core) % SIDE * SIDE + (by + k * other) % SIDE
                env_copies.append(remote(three, three, e_send.at[k], e_recv.at[k], to, me))
            for copy in env_copies:
                copy.start()
        for copy in copies:
            copy.wait_recv()
        copies = {}
        for k in (1, 3):
            for kind in range(2):
                mine = quad(g, kind, 0)
                copies[kind, k] = remote(
                    mine, mine, b_send.at[g, kind, k], b_recv.at[g, kind, k],
                    second_peer(kind, k), me,
                )
                copies[kind, k].start()
        second.append(copies)
        for kind in range(2):
            copy = sib_copy(g, kind, 0)
            copy.start()
            across.append(copy)

    def make_slots(d):
        found = [jnp.int32(32)] * 4
        for b in range(32):
            hit = dest_ref[b] == d
            found = [jnp.where(hit, new, old) for new, old in zip([b] + found[:3], found)]
        for s in range(4):
            slots[4 * d + s] = found[s]

    relays = []
    for g in range(2):
        copies = {}
        for half, k in enumerate((1, 3)):
            for kind in range(2):
                second[g][kind, k].wait_recv()
                theirs = quad(g, kind, k, half)
                copies[kind, half] = remote(
                    theirs, theirs, b_send.at[g, kind, 2 * half], b_recv.at[g, kind, 2 * half],
                    second_peer(kind, k), me,
                )
                copies[kind, half].start()
        relays.append(copies)
        for k in (1, 3):
            for kind in range(2):
                copy = sib_copy(g, kind, k)
                copy.start()
                across.append(copy)
        if g == 0:
            each(NDOM, make_slots)
            sums[32] = jnp.zeros((144, 128), F32)
            same = lax.broadcasted_iota(jnp.int32, (16, 16), 0) == lax.broadcasted_iota(
                jnp.int32, (16, 16), 1
            )
            gain = jnp.zeros((16, 128), F32)
            for s in range(4):
                column = jnp.sum(jnp.where(same, gain_ref[s : s + 1, :], 0.0), axis=1, keepdims=True)
                gain = gain + jnp.where(spec_ref[...] == s, column, 0.0)
    for copy in env_copies:
        copy.wait_recv()
    last = remote(ge.at[core], ge.at[core], own_send.at[2], own_recv.at[2], dom, sib)
    last.start()
    across.append(last)
    each(15, lambda q: lat_copy(q).wait_recv())
    for n in range(4):
        block = x_in[4 * n : 4 * n + 4].reshape(256, 256).astype(F32)
        x_t[:, 256 * n : 256 * n + 256] = block.T.astype(BF16)
    for g in range(2):
        for half in range(2):
            for kind in range(2):
                relays[g][kind, half].wait_recv()
                copy = sib_copy(g, kind, 2, half)
                copy.start()
                across.append(copy)

    def sib_arrivals(kind):
        own_copies[kind].wait_recv()
        for g in range(2):
            for k in (0, 1, 3):
                sib_copy(g, kind, k).wait_recv()
            for half in range(2):
                sib_copy(g, kind, 2, half).wait_recv()

    sib_arrivals(0)

    def first_layer(r):
        tiles = jnp.concatenate(
            [g1[c, b, r].reshape(224, 128) for b in range(SIDE) for c in range(2)], axis=1
        )
        rows = pl.ds(pl.multiple_of(16 * r, 16), 16)
        matrix = jnp.concatenate([tiles, own1[0, rows, :], own1[1, rows, :]], axis=0)
        v = dot(x_t[...], matrix, ((1,), (1,)))
        hid[r] = (v / (1.0 + jnp.exp(-v))).astype(BF16)

    each(SIDE, first_layer)
    sib_arrivals(1)
    for b in range(SIDE):
        lanes = slice(256 * b, 256 * b + 256)
        update = jnp.zeros((256, 256), F32)
        for r in range(SIDE):
            tiles = jnp.concatenate([g2[c, r, b].reshape(224, 128) for c in range(2)], axis=1)
            rows = slice(16 * r, 16 * r + 16)
            matrix = jnp.concatenate([tiles, own2[0, rows, lanes], own2[1, rows, lanes]], axis=0)
            update = update + dot(hid[r], matrix, ((1,), (0,)))
        lnt[:, lanes] = (x_t[:, lanes].astype(F32) + update).astype(BF16)

    last.wait_recv()
    matrix = jnp.concatenate([ge[c].reshape(1024, 128) for c in range(2)], axis=1)
    env_weights = dot(lnt[...], matrix, ((1,), (0,)))
    ws[...] = env_weights.T.astype(BF16).reshape(16, 16, 256)
    each(15, lambda q: w_copy(q).start())
    wt[pl.ds(me, 1)] = ws[pl.ds(me, 1)]

    for b in range(SIDE):
        block = lnt[:, 256 * b : 256 * b + 256].astype(F32).T.astype(BF16)
        ln[4 * b : 4 * b + 4] = block.reshape(4, 64, 256)
    def block_sums(t):
        w = wt[t].astype(F32)
        h = hs[t]
        for j in range(2):
            lanes = slice(128 * j, 128 * j + 128)
            wj = w[:, lanes]
            alive = h[9:10, lanes]
            contrib = jnp.concatenate(
                [((h[m : m + 1, lanes] * wj) * alive).astype(BF16) for m in range(9)], axis=0
            )
            sums[2 * t + j] = dot(contrib, onehot[2 * t + j], ((1,), (1,)))

    each(15, lambda q: w_copy(q).wait_recv())
    each(NTP, block_sums, unroll=4)

    def domain_sum(d):
        total = sums[slots[4 * d]] + sums[slots[4 * d + 1]]
        return total + (sums[slots[4 * d + 2]] + sums[slots[4 * d + 3]])

    def q_copy(part, q):
        out, into = ((p_low, in_low), (p_high, in_high))[part]
        to = dom_far(q)
        return remote(
            out.at[to], into.at[dom], q_send.at[part, q], q_recv.at[part, q], to, me
        )

    def t_copy(part, q):
        ref = (table_low, table_high)[part]
        return remote(
            ref.at[dom], ref.at[dom], t_send.at[part, q], t_recv.at[part, q], dom_far(q), me
        )

    for q in range(NDOM - 1):
        to = dom_far(q)
        total = domain_sum(to).astype(BF16)
        p_low[pl.ds(to, 1)] = total[None, :64]
        p_high[pl.ds(to, 1)] = total[None, 64:]
        q_copy(0, q).start()
    for q in range(NDOM - 1):
        q_copy(1, q).start()
    own = pltpu.make_async_copy(
        ln.at[me], ln_out.at[:, pl.ds(pl.multiple_of(me * 256, 256), 256)], pre_sem.at[6]
    )
    own.start()
    each(15, lambda q: ln_copy(q).start())
    total = domain_sum(dom)
    for part in range(2):
        into, ref = ((in_low, table_low), (in_high, table_high))[part]
        rows = (slice(0, 64), slice(64, 144))[part]
        comps = (slice(0, 4), slice(4, 9))[part]
        for q in range(NDOM - 1):
            q_copy(part, q).wait_recv()

        def add(k, acc):
            return acc + into[(dom + k) % NDOM].astype(F32)

        acc = lax.fori_loop(1, NDOM, add, total[rows])
        env = acc.reshape(-1, 16, 128) * gain[None] * env_factor
        ref[pl.ds(dom, 1)] = env.reshape(1, -1, 128).astype(BF16)
        for q in range(NDOM - 1):
            t_copy(part, q).start()
        env_out[comps] = env

    def finish(t, part):
        w = wt[t].astype(F32)
        h = hs[t]
        ref = (table_low, table_high)[part]
        base = (0, 4)[part]
        spans_of = (((0,), (1, 2, 3)), ((4, 5, 6, 7, 8),))[part]
        parts = [[] for _ in spans_of]
        for j in range(2):
            lanes = slice(128 * j, 128 * j + 128)
            env_edge = dot(ref[dest_ref[2 * t + j]], onehot[2 * t + j], ((1,), (0,)))
            for l, comps in enumerate(spans_of):
                degree = None
                for m in comps:
                    term = env_edge[16 * (m - base) : 16 * (m - base) + 16] * h[m : m + 1, lanes]
                    degree = term if degree is None else degree + term
                parts[l].append(degree * w[:, lanes] * h[9:10, lanes])
        for l in range(len(spans_of)):
            inv_out[(0, 2)[part] + l, :, pl.ds(pl.multiple_of(t * 256, 256), 256)] = (
                jnp.concatenate(parts[l], axis=1)
            )

    for part in range(2):
        for q in range(NDOM - 1):
            t_copy(part, q).wait_recv()
        each(NTP, lambda t: finish(t, part), unroll=4)

    own.wait()
    each(15, lambda q: ln_copy(q).wait_recv())
    for copy in tile_copies + own_copies + first[0] + first[1] + env_copies:
        copy.wait_send()
    for copy in across:
        copy.wait_send()
    for copies in second + relays:
        for copy in copies.values():
            copy.wait_send()
    for make in (lat_copy, w_copy, ln_copy):
        each(15, lambda q: make(q).wait_send())
    for part in range(2):
        for q in range(NDOM - 1):
            q_copy(part, q).wait_send()
            t_copy(part, q).wait_send()


def write_out(ln_in, env_in, inv_in, ln_out, env_out, inv_out, ln, env, inv, sem_in, sem_out):
    parts = [(env_in, env, env_out)]
    for n in range(2):
        rows = pl.ds(32 * n, 32)
        parts.append((ln_in.at[rows], ln.at[rows], ln_out.at[rows]))
    for l in range(3):
        parts.append((inv_in.at[l], inv.at[l], inv_out.at[l]))
    reads = [
        pltpu.make_async_copy(src, mid, sem_in.at[n]) for n, (src, mid, _) in enumerate(parts)
    ]
    writes = [
        pltpu.make_async_copy(mid, dst, sem_out.at[n]) for n, (_, mid, dst) in enumerate(parts)
    ]
    for copy in reads:
        copy.start()
    for read, write in zip(reads, writes):
        read.wait()
        write.start()
    for copy in writes:
        copy.wait()


def on_device(
    latent, w_first, w_second, w_env, edge_vec, centers, block_dest, block_fill, species,
    species_gain,
):
    vmem = pl.BlockSpec(memory_space=pltpu.VMEM)
    hbm = pl.BlockSpec(memory_space=pltpu.HBM)
    dma = pltpu.SemaphoreType.DMA
    shapes = (
        jax.ShapeDtypeStruct((64, 4096), BF16),
        jax.ShapeDtypeStruct((9, 16, 128), F32),
        jax.ShapeDtypeStruct((3, 16, 4096), F32),
    )
    results = pl.pallas_call(
        kernel,
        out_shape=shapes,
        in_specs=[hbm] * 10,
        out_specs=(vmem, vmem, vmem),
        scratch_shapes=[
            pltpu.SMEM((32,), jnp.int32),
            pltpu.SMEM((32,), jnp.int32),
            pltpu.VMEM((3, 4096), F32),
            pltpu.VMEM((32, 128), jnp.int32),
            pltpu.VMEM((1, 128), jnp.int32),
            pltpu.VMEM((4, 16), F32),
            pltpu.VMEM((2, 3, 16, 128), BF16),
            pltpu.VMEM((16, 3, 16, 128), BF16),
            pltpu.VMEM((2, 64, 1024), BF16),
            pltpu.VMEM((2, 64, 1024), BF16),
            pltpu.VMEM((2, 4, 4, 14, 16, 128), BF16),
            pltpu.VMEM((2, 4, 4, 14, 16, 128), BF16),
            pltpu.VMEM((2, 16, 4, 16, 128), BF16),
            pltpu.VMEM((16, 64, 256), BF16),
            pltpu.VMEM((256, 1024), BF16),
            pltpu.VMEM((4, 256, 256), BF16),
            pltpu.VMEM((256, 1024), BF16),
            pltpu.VMEM((16, 64, 256), BF16),
            pltpu.VMEM((16, 16, 256), BF16),
            pltpu.VMEM((16, 16, 256), BF16),
            pltpu.VMEM((16, 16, 256), F32),
            pltpu.VMEM((32, 128, 128), BF16),
            pltpu.SMEM((64,), jnp.int32),
            pltpu.VMEM((33, 144, 128), F32),
            pltpu.VMEM((16, 64, 128), BF16),
            pltpu.VMEM((16, 80, 128), BF16),
            pltpu.VMEM((16, 64, 128), BF16),
            pltpu.VMEM((16, 80, 128), BF16),
            pltpu.VMEM((16, 64, 128), BF16),
            pltpu.VMEM((16, 80, 128), BF16),
            dma((16,)),
            dma((15,)), dma((15,)), dma((15,)), dma((15,)), dma((3,)), dma((3,)),
            dma((2, 2, 4)), dma((2, 2, 4)), dma((2, 2, 4)), dma((2, 2, 4)), dma((4,)), dma((4,)),
            dma((2, 2, 5)), dma((2, 2, 5)),
            dma((15,)), dma((15,)), dma((15,)), dma((15,)),
            dma((2, 15)), dma((2, 15)), dma((2, 15)), dma((2, 15)),
        ],
        compiler_params=pltpu.CompilerParams(
            collective_id=0, has_side_effects=True, vmem_limit_bytes=60 * 1024 * 1024
        ),
        cost_estimate=pl.CostEstimate(
            flops=2 * 10**9, bytes_accessed=4 * 10**6, transcendentals=300000
        ),
        name="allegro",
    )(
        block_dest.reshape(32), block_fill, latent, w_first.T, w_second, w_env, edge_vec,
        centers.reshape(32, 128), species.reshape(1, 128), species_gain,
    )
    return pl.pallas_call(
        write_out,
        out_shape=shapes,
        in_specs=[hbm] * 3,
        out_specs=(hbm,) * 3,
        scratch_shapes=[
            pltpu.VMEM((64, 4096), BF16),
            pltpu.VMEM((9, 16, 128), F32),
            pltpu.VMEM((3, 16, 4096), F32),
            dma((6,)),
            dma((6,)),
        ],
        compiler_params=pltpu.CompilerParams(vmem_limit_bytes=60 * 1024 * 1024),
        name="write_out",
    )(*results)


def solution(mesh):
    in_specs = (
        P("tp", "dom"),
        P(None, "tp"),
        P("tp", None),
        P("tp", None),
        P(None, "dom"),
        P("dom"),
        P("dom", None),
        P("dom"),
        P("dom"),
        P(None, "tp"),
    )
    out_specs = (P("tp", "dom"), P(None, "tp", "dom"), P(None, "tp", "dom"))
    return jax.shard_map(
        on_device, mesh=mesh, in_specs=in_specs, out_specs=out_specs, check_vma=False
    )
```

```python
import math

import jax
import jax.numpy as jnp
from jax import lax
from jax.experimental import pallas as pl
from jax.experimental.pallas import tpu as pltpu
from jax.sharding import PartitionSpec as P

MESH = pl.DeviceIdType.MESH
F32 = jnp.float32
BF16 = jnp.bfloat16

root_three = math.sqrt(3.0)
root_five = math.sqrt(5.0)
root_fifteen = math.sqrt(15.0)
cutoff_radius = 6.0
env_factor = 0.25

SIDE = 4
NDOM = 16
NTP = 16
DEPTH = 8
HALF = DEPTH // 2
NEAR_Z = (6, 2, 7, 1, 4, 5, 3)
ENV_Z = (4, 5, 3, 6, 2, 7, 1)
FAR = sorted(
    [(dx, dy) for dx in range(SIDE) for dy in range(SIDE) if dx or dy],
    key=lambda d: -min(d[0], SIDE - d[0]) - min(d[1], SIDE - d[1]),
)


def dot(left, right, dims):
    return lax.dot_general(left, right, (dims, ((), ())), preferred_element_type=F32)


def kernel(
    dest, fill, latent, w1, w2, we, ev, cen, spec, gains,
    ln_out, env_out, inv_out,
    dest_ref, fill_ref, ev_ref, cen_ref, spec_ref, gain_ref,
    pieces, ring, own1, own2, g1, g2, ge, x_in, x_t, hid, lnt, ln, ws, wt, hs, onehot, slots,
    sums, p_low, p_high, in_low, in_high, table_low, table_high,
    pre_sem, lat_send, lat_recv, one_send, one_recv, own_send, own_recv,
    a_send, a_recv, b_send, b_recv, e_send, e_recv,
    sib_send, sib_recv, w_send, w_recv, ln_send, ln_recv, q_send, q_recv, t_send, t_recv,
):
    dom = lax.axis_index("dom")
    me = lax.axis_index("tp")
    ax = dom // SIDE
    by = dom % SIDE
    core = me % 2
    other = 1 - core
    z = me // 2
    sib = 2 * z + other

    def tp_far(q):
        s = q // 2
        dz = HALF + (s + 1) // 2 * (1 - 2 * (s % 2))
        return 2 * ((z + dz) % DEPTH) + (core + 1 + q) % 2

    def dom_far(q):
        dx, dy = FAR[q]
        return (ax + dx) % SIDE * SIDE + (by + dy) % SIDE

    def x_peer(k):
        return (ax + k) % SIDE * SIDE + by

    def y_peer(k):
        return ax * SIDE + (by + k) % SIDE

    def remote(src, dst, send, recv, to_dom, to_tp):
        return pltpu.make_async_remote_copy(
            src_ref=src, dst_ref=dst, send_sem=send, recv_sem=recv,
            device_id=(to_dom, to_tp), device_id_type=MESH,
        )

    def each(count, act, unroll=1):
        def body(q, carry):
            act(q)
            return carry

        lax.fori_loop(0, count, body, 0, unroll=unroll)

    pre = [
        pltpu.make_async_copy(
            latent.at[:, pl.ds(pl.multiple_of(me * 256, 256), 256)], x_in.at[me], pre_sem.at[7]
        ),
        pltpu.make_async_copy(w1, own1.at[core], pre_sem.at[8]),
        pltpu.make_async_copy(w2, own2.at[core], pre_sem.at[9]),
        pltpu.make_async_copy(we, ge.at[z, core], pre_sem.at[4]),
    ]
    for half in range(2):
        lanes = pl.ds(pl.multiple_of(by * 256 + 128 * half, 128), 128)
        for i, matrix in enumerate([w1, w2]):
            pre.append(
                pltpu.make_async_copy(
                    matrix.at[pl.ds(ax * 16, 16), lanes],
                    pieces.at[half, i], pre_sem.at[2 * i + half],
                )
            )
    for copy in pre:
        copy.start()

    small = [
        pltpu.make_async_copy(src, dst, pre_sem.at[10 + i])
        for i, (src, dst) in enumerate(
            [
                (dest, dest_ref), (fill, fill_ref), (ev, ev_ref), (cen, cen_ref),
                (spec, spec_ref), (gains, gain_ref),
            ]
        )
    ]
    for copy in small:
        copy.start()
    barrier = pltpu.get_barrier_semaphore()

    def greet_tp(q):
        pl.semaphore_signal(barrier, inc=1, device_id=(dom, tp_far(q)), device_id_type=MESH)

    each(NTP - 1, greet_tp)
    for q in range(NDOM - 1):
        pl.semaphore_signal(barrier, inc=1, device_id=(dom_far(q), me), device_id_type=MESH)
    for copy in pre:
        copy.wait()
    pl.semaphore_wait(barrier, NTP - 1 + NDOM - 1)

    def one_copy(n, c):
        to = 2 * ((z + NEAR_Z[n]) % DEPTH) + c
        return remote(
            pieces.at[c], ring.at[2 * n + core], one_send.at[2 * n + c],
            one_recv.at[2 * n + core], dom, to,
        )

    def one_arrival(slot):
        remote(
            pieces.at[0], ring.at[slot], one_send.at[slot], one_recv.at[slot], dom, sib
        ).wait_recv()

    tile_copies = [one_copy(n, c) for n in range(7) for c in range(2)]
    own_copies = [
        remote(ref.at[core], ref.at[core], own_send.at[i], own_recv.at[i], dom, sib)
        for i, ref in enumerate([own1, own2])
    ]
    for copy in tile_copies + own_copies:
        copy.start()

    def lat_copy(q):
        to = tp_far(q)
        return remote(
            latent.at[:, pl.ds(pl.multiple_of(to * 256, 256), 256)], x_in.at[me],
            lat_send.at[q], lat_recv.at[q], dom, to,
        )

    def w_copy(q):
        to = tp_far(q)
        return remote(ws.at[to], wt.at[me], w_send.at[q], w_recv.at[q], dom, to)

    def ln_copy(q):
        to = tp_far(q)
        return remote(
            ln.at[to], ln_out.at[:, pl.ds(pl.multiple_of(me * 256, 256), 256)],
            ln_send.at[q], ln_recv.at[q], dom, to,
        )

    for copy in small:
        copy.wait()

    def harmonics(t):
        v = ev_ref[:, pl.ds(pl.multiple_of(t * 256, 256), 256)]
        along_x, along_y, along_z = v[0:1], v[1:2], v[2:3]
        radius = jnp.sqrt(along_x * along_x + along_y * along_y + along_z * along_z)
        ux = along_x / radius
        uy = along_y / radius
        uz = along_z / radius
        ratio = radius / cutoff_radius
        flat = 1.0 - ratio * ratio
        envelope = flat * flat
        spot = lax.broadcasted_iota(jnp.int32, (1, 128), 1)
        alive = jnp.concatenate(
            [(spot < fill_ref[2 * t + j]).astype(F32) for j in range(2)], axis=1
        )
        rows = [
            envelope,
            root_three * ux * envelope,
            root_three * uy * envelope,
            root_three * uz * envelope,
            root_fifteen * ux * uy * envelope,
            root_fifteen * uy * uz * envelope,
            root_five / 2.0 * (3.0 * uz * uz - 1.0) * envelope,
            root_fifteen * ux * uz * envelope,
            root_fifteen / 2.0 * (ux * ux - uy * uy) * envelope,
            alive,
        ]
        for m, row in enumerate(rows):
            hs[t, m : m + 1, :] = row

    each(NTP, harmonics)

    def make_onehot(b):
        atoms = lax.broadcasted_iota(jnp.int32, (128, 128), 0)
        onehot[b] = (atoms == cen_ref[pl.ds(b, 1), :]).astype(F32).astype(BF16)

    each(32, make_onehot)

    groups = [slice(0, 8), slice(8, 14)]
    spans = [pl.ds(0, 8), pl.ds(8, 6)]

    def quad(g, kind, k, half=None):
        part = slice(None) if half is None else pl.ds(2 * half, 2)
        if kind == 0:
            return g1.at[core, (by + SIDE - k) % SIDE, part, spans[g]]
        return g2.at[core, (ax + SIDE - k) % SIDE, part, spans[g]]

    def sib_copy(g, kind, k, half=None):
        ref = quad(g, kind, k, half)
        slot = k if half is None else 2 + 2 * half
        return remote(
            ref, ref, sib_send.at[g, kind, slot], sib_recv.at[g, kind, slot], dom, sib
        )

    def second_peer(kind, k):
        return (y_peer, x_peer)[kind](k)

    first = []
    second = []
    across = []
    env_copies = []
    for g in range(2):
        for slot in range(groups[g].start, groups[g].stop):
            one_arrival(slot)
        tiles = ring[groups[g]]
        g1[pl.ds(core, 1), pl.ds(by, 1), pl.ds(ax, 1), groups[g]] = tiles[:, 0][None, None, None]
        g2[pl.ds(core, 1), pl.ds(ax, 1), pl.ds(by, 1), groups[g]] = tiles[:, 1][None, None, None]
        copies = []
        for k in (2, 1, 3):
            one = g1.at[core, by, ax, spans[g]]
            copies.append(remote(one, one, a_send.at[g, 0, k], a_recv.at[g, 0, k], x_peer(k), me))
            two = g2.at[core, ax, by, spans[g]]
            copies.append(remote(two, two, a_send.at[g, 1, k], a_recv.at[g, 1, k], y_peer(k), me))
        for copy in copies:
            copy.start()
        first.append(copies)
        if g == 1:
            each(15, lambda q: lat_copy(q).start())
            for n in range(7):
                mine = ge.at[z, core]
                to = 2 * ((z + ENV_Z[n]) % DEPTH) + core
                env_copies.append(
                    remote(mine, mine, e_send.at[n], e_recv.at[n], dom, to)
                )
            for copy in env_copies:
                copy.start()
        for copy in copies:
            copy.wait_recv()
        copies = {}
        for k in (1, 3):
            for kind in range(2):
                mine = quad(g, kind, 0)
                copies[kind, k] = remote(
                    mine, mine, b_send.at[g, kind, k], b_recv.at[g, kind, k],
                    second_peer(kind, k), me,
                )
                copies[kind, k].start()
        second.append(copies)
        for kind in range(2):
            copy = sib_copy(g, kind, 0)
            copy.start()
            across.append(copy)

    def make_slots(d):
        found = [jnp.int32(32)] * 4
        for b in range(32):
            hit = dest_ref[b] == d
            found = [jnp.where(hit, new, old) for new, old in zip([b] + found[:3], found)]
        for s in range(4):
            slots[4 * d + s] = found[s]

    relays = []
    for g in range(2):
        copies = {}
        for half, k in enumerate((1, 3)):
            for kind in range(2):
                second[g][kind, k].wait_recv()
                theirs = quad(g, kind, k, half)
                copies[kind, half] = remote(
                    theirs, theirs, b_send.at[g, kind, 2 * half], b_recv.at[g, kind, 2 * half],
                    second_peer(kind, k), me,
                )
                copies[kind, half].start()
        relays.append(copies)
        for k in (1, 3):
            for kind in range(2):
                copy = sib_copy(g, kind, k)
                copy.start()
                across.append(copy)
        if g == 0:
            each(NDOM, make_slots)
            sums[32] = jnp.zeros((144, 128), F32)
            same = lax.broadcasted_iota(jnp.int32, (16, 16), 0) == lax.broadcasted_iota(
                jnp.int32, (16, 16), 1
            )
            gain = jnp.zeros((16, 128), F32)
            for s in range(4):
                column = jnp.sum(jnp.where(same, gain_ref[s : s + 1, :], 0.0), axis=1, keepdims=True)
                gain = gain + jnp.where(spec_ref[...] == s, column, 0.0)
    each(15, lambda q: lat_copy(q).wait_recv())
    for n in range(4):
        block = x_in[4 * n : 4 * n + 4].reshape(256, 256).astype(F32)
        x_t[:, 256 * n : 256 * n + 256] = block.T.astype(BF16)
    for g in range(2):
        for half in range(2):
            for kind in range(2):
                relays[g][kind, half].wait_recv()
                copy = sib_copy(g, kind, 2, half)
                copy.start()
                across.append(copy)

    for copy in env_copies:
        copy.wait_recv()
    last = remote(ge.at[:, core], ge.at[:, core], own_send.at[2], own_recv.at[2], dom, sib)
    last.start()
    across.append(last)

    def sib_arrivals(kind):
        own_copies[kind].wait_recv()
        for g in range(2):
            for k in (0, 1, 3):
                sib_copy(g, kind, k).wait_recv()
            for half in range(2):
                sib_copy(g, kind, 2, half).wait_recv()

    sib_arrivals(0)

    def first_layer(r):
        tiles = jnp.concatenate(
            [g1[c, b, r].reshape(224, 128) for b in range(SIDE) for c in range(2)], axis=1
        )
        rows = pl.ds(pl.multiple_of(16 * r, 16), 16)
        matrix = jnp.concatenate([tiles, own1[0, rows, :], own1[1, rows, :]], axis=0)
        v = dot(x_t[...], matrix, ((1,), (1,)))
        hid[r] = (v / (1.0 + jnp.exp(-v))).astype(BF16)

    each(SIDE, first_layer)
    sib_arrivals(1)
    for b in range(SIDE):
        lanes = slice(256 * b, 256 * b + 256)
        update = jnp.zeros((256, 256), F32)
        for r in range(SIDE):
            tiles = jnp.concatenate([g2[c, r, b].reshape(224, 128) for c in range(2)], axis=1)
            rows = slice(16 * r, 16 * r + 16)
            matrix = jnp.concatenate([tiles, own2[0, rows, lanes], own2[1, rows, lanes]], axis=0)
            update = update + dot(hid[r], matrix, ((1,), (0,)))
        lnt[:, lanes] = (x_t[:, lanes].astype(F32) + update).astype(BF16)

    last.wait_recv()
    env_weights = dot(lnt[...], ge[...].reshape(1024, 256), ((1,), (0,)))
    ws[...] = env_weights.T.astype(BF16).reshape(16, 16, 256)
    each(15, lambda q: w_copy(q).start())
    wt[pl.ds(me, 1)] = ws[pl.ds(me, 1)]

    for b in range(SIDE):
        block = lnt[:, 256 * b : 256 * b + 256].astype(F32).T.astype(BF16)
        ln[4 * b : 4 * b + 4] = block.reshape(4, 64, 256)
    def block_sums(t):
        w = wt[t].astype(F32)
        h = hs[t]
        for j in range(2):
            lanes = slice(128 * j, 128 * j + 128)
            wj = w[:, lanes]
            alive = h[9:10, lanes]
            contrib = jnp.concatenate(
                [((h[m : m + 1, lanes] * wj) * alive).astype(BF16) for m in range(9)], axis=0
            )
            sums[2 * t + j] = dot(contrib, onehot[2 * t + j], ((1,), (1,)))

    each(15, lambda q: w_copy(q).wait_recv())
    each(NTP, block_sums, unroll=4)

    def domain_sum(d):
        total = sums[slots[4 * d]] + sums[slots[4 * d + 1]]
        return total + (sums[slots[4 * d + 2]] + sums[slots[4 * d + 3]])

    def q_copy(part, q):
        out, into = ((p_low, in_low), (p_high, in_high))[part]
        to = dom_far(q)
        return remote(
            out.at[to], into.at[dom], q_send.at[part, q], q_recv.at[part, q], to, me
        )

    def t_copy(part, q):
        ref = (table_low, table_high)[part]
        return remote(
            ref.at[dom], ref.at[dom], t_send.at[part, q], t_recv.at[part, q], dom_far(q), me
        )

    for q in range(NDOM - 1):
        to = dom_far(q)
        total = domain_sum(to).astype(BF16)
        p_low[pl.ds(to, 1)] = total[None, :64]
        p_high[pl.ds(to, 1)] = total[None, 64:]
        q_copy(0, q).start()
    for q in range(NDOM - 1):
        q_copy(1, q).start()
    own = pltpu.make_async_copy(
        ln.at[me], ln_out.at[:, pl.ds(pl.multiple_of(me * 256, 256), 256)], pre_sem.at[6]
    )
    own.start()
    each(15, lambda q: ln_copy(q).start())
    total = domain_sum(dom)
    in_low[pl.ds(dom, 1)] = jnp.zeros((1, 64, 128), BF16)
    in_high[pl.ds(dom, 1)] = jnp.zeros((1, 80, 128), BF16)
    for part in range(2):
        into, ref = ((in_low, table_low), (in_high, table_high))[part]
        rows = (slice(0, 64), slice(64, 144))[part]
        comps = (slice(0, 4), slice(4, 9))[part]
        for q in range(NDOM - 1):
            q_copy(part, q).wait_recv()

        acc = total[rows]
        for d in range(NDOM):
            acc = acc + into[d].astype(F32)
        env = acc.reshape(-1, 16, 128) * gain[None] * env_factor
        ref[pl.ds(dom, 1)] = env.reshape(1, -1, 128).astype(BF16)
        for q in range(NDOM - 1):
            t_copy(part, q).start()
        env_out[comps] = env

    def finish(t, part):
        w = wt[t].astype(F32)
        h = hs[t]
        ref = (table_low, table_high)[part]
        base = (0, 4)[part]
        spans_of = (((0,), (1, 2, 3)), ((4, 5, 6, 7, 8),))[part]
        parts = [[] for _ in spans_of]
        for j in range(2):
            lanes = slice(128 * j, 128 * j + 128)
            env_edge = dot(ref[dest_ref[2 * t + j]], onehot[2 * t + j], ((1,), (0,)))
            for l, comps in enumerate(spans_of):
                degree = None
                for m in comps:
                    term = env_edge[16 * (m - base) : 16 * (m - base) + 16] * h[m : m + 1, lanes]
                    degree = term if degree is None else degree + term
                parts[l].append(degree * w[:, lanes] * h[9:10, lanes])
        for l in range(len(spans_of)):
            inv_out[(0, 2)[part] + l, :, pl.ds(pl.multiple_of(t * 256, 256), 256)] = (
                jnp.concatenate(parts[l], axis=1)
            )

    for part in range(2):
        for q in range(NDOM - 1):
            t_copy(part, q).wait_recv()
        each(NTP, lambda t: finish(t, part), unroll=4)

    own.wait()
    each(15, lambda q: ln_copy(q).wait_recv())
    for copy in tile_copies + own_copies + first[0] + first[1] + env_copies:
        copy.wait_send()
    for copy in across:
        copy.wait_send()
    for copies in second + relays:
        for copy in copies.values():
            copy.wait_send()
    for make in (lat_copy, w_copy, ln_copy):
        each(15, lambda q: make(q).wait_send())
    for part in range(2):
        for q in range(NDOM - 1):
            q_copy(part, q).wait_send()
            t_copy(part, q).wait_send()


def write_out(ln_in, env_in, inv_in, ln_out, env_out, inv_out, ln, env, inv, sem_in, sem_out):
    parts = [(env_in, env, env_out)]
    for n in range(2):
        rows = pl.ds(32 * n, 32)
        parts.append((ln_in.at[rows], ln.at[rows], ln_out.at[rows]))
    for l in range(3):
        parts.append((inv_in.at[l], inv.at[l], inv_out.at[l]))
    reads = [
        pltpu.make_async_copy(src, mid, sem_in.at[n]) for n, (src, mid, _) in enumerate(parts)
    ]
    writes = [
        pltpu.make_async_copy(mid, dst, sem_out.at[n]) for n, (_, mid, dst) in enumerate(parts)
    ]
    for copy in reads:
        copy.start()
    for read, write in zip(reads, writes):
        read.wait()
        write.start()
    for copy in writes:
        copy.wait()


def on_device(
    latent, w_first, w_second, w_env, edge_vec, centers, block_dest, block_fill, species,
    species_gain,
):
    vmem = pl.BlockSpec(memory_space=pltpu.VMEM)
    hbm = pl.BlockSpec(memory_space=pltpu.HBM)
    dma = pltpu.SemaphoreType.DMA
    shapes = (
        jax.ShapeDtypeStruct((64, 4096), BF16),
        jax.ShapeDtypeStruct((9, 16, 128), F32),
        jax.ShapeDtypeStruct((3, 16, 4096), F32),
    )
    results = pl.pallas_call(
        kernel,
        out_shape=shapes,
        in_specs=[hbm] * 10,
        out_specs=(vmem, vmem, vmem),
        scratch_shapes=[
            pltpu.SMEM((32,), jnp.int32),
            pltpu.SMEM((32,), jnp.int32),
            pltpu.VMEM((3, 4096), F32),
            pltpu.VMEM((32, 128), jnp.int32),
            pltpu.VMEM((1, 128), jnp.int32),
            pltpu.VMEM((4, 16), F32),
            pltpu.VMEM((2, 2, 16, 128), BF16),
            pltpu.VMEM((14, 2, 16, 128), BF16),
            pltpu.VMEM((2, 64, 1024), BF16),
            pltpu.VMEM((2, 64, 1024), BF16),
            pltpu.VMEM((2, 4, 4, 14, 16, 128), BF16),
            pltpu.VMEM((2, 4, 4, 14, 16, 128), BF16),
            pltpu.VMEM((8, 2, 64, 256), BF16),
            pltpu.VMEM((16, 64, 256), BF16),
            pltpu.VMEM((256, 1024), BF16),
            pltpu.VMEM((4, 256, 256), BF16),
            pltpu.VMEM((256, 1024), BF16),
            pltpu.VMEM((16, 64, 256), BF16),
            pltpu.VMEM((16, 16, 256), BF16),
            pltpu.VMEM((16, 16, 256), BF16),
            pltpu.VMEM((16, 16, 256), F32),
            pltpu.VMEM((32, 128, 128), BF16),
            pltpu.SMEM((64,), jnp.int32),
            pltpu.VMEM((33, 144, 128), F32),
            pltpu.VMEM((16, 64, 128), BF16),
            pltpu.VMEM((16, 80, 128), BF16),
            pltpu.VMEM((16, 64, 128), BF16),
            pltpu.VMEM((16, 80, 128), BF16),
            pltpu.VMEM((16, 64, 128), BF16),
            pltpu.VMEM((16, 80, 128), BF16),
            dma((16,)),
            dma((15,)), dma((15,)), dma((15,)), dma((15,)), dma((3,)), dma((3,)),
            dma((2, 2, 4)), dma((2, 2, 4)), dma((2, 2, 4)), dma((2, 2, 4)), dma((7,)), dma((7,)),
            dma((2, 2, 5)), dma((2, 2, 5)),
            dma((15,)), dma((15,)), dma((15,)), dma((15,)),
            dma((2, 15)), dma((2, 15)), dma((2, 15)), dma((2, 15)),
        ],
        compiler_params=pltpu.CompilerParams(
            collective_id=0, has_side_effects=True, vmem_limit_bytes=60 * 1024 * 1024
        ),
        cost_estimate=pl.CostEstimate(
            flops=2 * 10**9, bytes_accessed=4 * 10**6, transcendentals=300000
        ),
        name="allegro",
    )(
        block_dest.reshape(32), block_fill, latent, w_first.T, w_second, w_env, edge_vec,
        centers.reshape(32, 128), species.reshape(1, 128), species_gain,
    )
    return pl.pallas_call(
        write_out,
        out_shape=shapes,
        in_specs=[hbm] * 3,
        out_specs=(hbm,) * 3,
        scratch_shapes=[
            pltpu.VMEM((64, 4096), BF16),
            pltpu.VMEM((9, 16, 128), F32),
            pltpu.VMEM((3, 16, 4096), F32),
            dma((6,)),
            dma((6,)),
        ],
        compiler_params=pltpu.CompilerParams(vmem_limit_bytes=60 * 1024 * 1024),
        name="write_out",
    )(*results)


def solution(mesh):
    in_specs = (
        P("tp", "dom"),
        P(None, "tp"),
        P("tp", None),
        P("tp", None),
        P(None, "dom"),
        P("dom"),
        P("dom", None),
        P("dom"),
        P("dom"),
        P(None, "tp"),
    )
    out_specs = (P("tp", "dom"), P(None, "tp", "dom"), P(None, "tp", "dom"))
    return jax.shard_map(
        on_device, mesh=mesh, in_specs=in_specs, out_specs=out_specs, check_vma=False
    )
```

```python
import math

import jax
import jax.numpy as jnp
from jax import lax
from jax.experimental import pallas as pl
from jax.experimental.pallas import tpu as pltpu
from jax.sharding import PartitionSpec as P

MESH = pl.DeviceIdType.MESH
F32 = jnp.float32
BF16 = jnp.bfloat16

root_three = math.sqrt(3.0)
root_five = math.sqrt(5.0)
root_fifteen = math.sqrt(15.0)
cutoff_radius = 6.0
env_factor = 0.25

SIDE = 4
NDOM = 16
NTP = 16
DEPTH = 8
HALF = DEPTH // 2
NEAR_Z = (6, 2, 7, 1, 4, 5, 3)
FAR = sorted(
    [(dx, dy) for dx in range(SIDE) for dy in range(SIDE) if dx or dy],
    key=lambda d: -min(d[0], SIDE - d[0]) - min(d[1], SIDE - d[1]),
)


def dot(left, right, dims):
    return lax.dot_general(left, right, (dims, ((), ())), preferred_element_type=F32)


def kernel(
    dest, fill, latent, w1, w2, we, ev, cen, spec, gains,
    ln_out, env_out, inv_out,
    dest_ref, fill_ref, ev_ref, cen_ref, spec_ref, gain_ref,
    pieces, ring, own1, own2, g1, g2, ge, x_in, x_t, hid, update, lnt, ln, ws, wt, hs, onehot, slots,
    sums, p_low, p_high, in_low, in_high, table_low, table_high,
    pre_sem, lat_send, lat_recv, one_send, one_recv, own_send, own_recv,
    a_send, a_recv, b_send, b_recv, e_send, e_recv,
    sib_send, sib_recv, w_send, w_recv, ln_send, ln_recv, q_send, q_recv, t_send, t_recv,
):
    dom = lax.axis_index("dom")
    me = lax.axis_index("tp")
    ax = dom // SIDE
    by = dom % SIDE
    core = me % 2
    other = 1 - core
    z = me // 2
    sib = 2 * z + other

    def tp_far(q):
        s = q // 2
        dz = HALF + (s + 1) // 2 * (1 - 2 * (s % 2))
        return 2 * ((z + dz) % DEPTH) + (core + 1 + q) % 2

    def dom_far(q):
        dx, dy = FAR[q]
        return (ax + dx) % SIDE * SIDE + (by + dy) % SIDE

    def x_peer(k):
        return (ax + k) % SIDE * SIDE + by

    def y_peer(k):
        return ax * SIDE + (by + k) % SIDE

    def remote(src, dst, send, recv, to_dom, to_tp):
        return pltpu.make_async_remote_copy(
            src_ref=src, dst_ref=dst, send_sem=send, recv_sem=recv,
            device_id=(to_dom, to_tp), device_id_type=MESH,
        )

    def each(count, act, unroll=1):
        def body(q, carry):
            act(q)
            return carry

        lax.fori_loop(0, count, body, 0, unroll=unroll)

    pre = [
        pltpu.make_async_copy(
            latent.at[:, pl.ds(pl.multiple_of(me * 256, 256), 256)], x_in.at[me], pre_sem.at[7]
        ),
        pltpu.make_async_copy(w1, own1.at[core], pre_sem.at[8]),
        pltpu.make_async_copy(w2, own2.at[core], pre_sem.at[9]),
    ]
    for half in range(2):
        lanes = pl.ds(pl.multiple_of(by * 256 + 128 * half, 128), 128)
        for i, matrix in enumerate([w1, w2]):
            pre.append(
                pltpu.make_async_copy(
                    matrix.at[pl.ds(ax * 16, 16), lanes],
                    pieces.at[half, i], pre_sem.at[2 * i + half],
                )
            )
        pre.append(
            pltpu.make_async_copy(
                we.at[pl.ds((by, ax)[half] * 16, 16), pl.ds(128 * half, 128)],
                pieces.at[half, 2], pre_sem.at[4 + half],
            )
        )
    for copy in pre:
        copy.start()

    small = [
        pltpu.make_async_copy(src, dst, pre_sem.at[10 + i])
        for i, (src, dst) in enumerate(
            [
                (dest, dest_ref), (fill, fill_ref), (ev, ev_ref), (cen, cen_ref),
                (spec, spec_ref), (gains, gain_ref),
            ]
        )
    ]
    for copy in small:
        copy.start()
    barrier = pltpu.get_barrier_semaphore()

    def greet_tp(q):
        pl.semaphore_signal(barrier, inc=1, device_id=(dom, tp_far(q)), device_id_type=MESH)

    each(NTP - 1, greet_tp)
    for q in range(NDOM - 1):
        pl.semaphore_signal(barrier, inc=1, device_id=(dom_far(q), me), device_id_type=MESH)
    for copy in pre:
        copy.wait()
    ring[pl.ds(14 + core, 1)] = pieces[pl.ds(core, 1)]
    pl.semaphore_wait(barrier, NTP - 1 + NDOM - 1)

    def one_copy(n, c):
        to = 2 * ((z + NEAR_Z[n]) % DEPTH) + c
        return remote(
            pieces.at[c], ring.at[2 * n + core], one_send.at[2 * n + c],
            one_recv.at[2 * n + core], dom, to,
        )

    def one_arrival(slot):
        remote(
            pieces.at[0], ring.at[slot], one_send.at[slot], one_recv.at[slot], dom, sib
        ).wait_recv()

    tile_copies = [one_copy(n, c) for n in range(7) for c in range(2)]
    tile_copies.append(
        remote(
            pieces.at[other], ring.at[14 + core], one_send.at[14], one_recv.at[14], dom, sib
        )
    )
    own_copies = [
        remote(ref.at[core], ref.at[core], own_send.at[i], own_recv.at[i], dom, sib)
        for i, ref in enumerate([own1, own2])
    ]
    for copy in tile_copies + own_copies:
        copy.start()

    def lat_copy(q):
        to = tp_far(q)
        return remote(
            latent.at[:, pl.ds(pl.multiple_of(to * 256, 256), 256)], x_in.at[me],
            lat_send.at[q], lat_recv.at[q], dom, to,
        )

    def w_copy(q):
        to = tp_far(q)
        return remote(ws.at[to], wt.at[me], w_send.at[q], w_recv.at[q], dom, to)

    def ln_copy(q):
        to = tp_far(q)
        return remote(
            ln.at[to], ln_out.at[:, pl.ds(pl.multiple_of(me * 256, 256), 256)],
            ln_send.at[q], ln_recv.at[q], dom, to,
        )

    for copy in small:
        copy.wait()

    def harmonics(t):
        v = ev_ref[:, pl.ds(pl.multiple_of(t * 256, 256), 256)]
        along_x, along_y, along_z = v[0:1], v[1:2], v[2:3]
        radius = jnp.sqrt(along_x * along_x + along_y * along_y + along_z * along_z)
        ux = along_x / radius
        uy = along_y / radius
        uz = along_z / radius
        ratio = radius / cutoff_radius
        flat = 1.0 - ratio * ratio
        envelope = flat * flat
        spot = lax.broadcasted_iota(jnp.int32, (1, 128), 1)
        alive = jnp.concatenate(
            [(spot < fill_ref[2 * t + j]).astype(F32) for j in range(2)], axis=1
        )
        rows = [
            envelope,
            root_three * ux * envelope,
            root_three * uy * envelope,
            root_three * uz * envelope,
            root_fifteen * ux * uy * envelope,
            root_fifteen * uy * uz * envelope,
            root_five / 2.0 * (3.0 * uz * uz - 1.0) * envelope,
            root_fifteen * ux * uz * envelope,
            root_fifteen / 2.0 * (ux * ux - uy * uy) * envelope,
            alive,
        ]
        for m, row in enumerate(rows):
            hs[t, m : m + 1, :] = row

    each(NTP, harmonics)

    def make_onehot(b):
        atoms = lax.broadcasted_iota(jnp.int32, (128, 128), 0)
        onehot[b] = (atoms == cen_ref[pl.ds(b, 1), :]).astype(F32).astype(BF16)

    each(32, make_onehot)

    groups = [slice(0, 8), slice(8, 14)]
    spans = [pl.ds(0, 8), pl.ds(8, 6)]

    def quad(g, kind, k, half=None):
        part = slice(None) if half is None else pl.ds(2 * half, 2)
        if kind == 0:
            return g1.at[core, (by + SIDE - k) % SIDE, part, spans[g]]
        return g2.at[core, (ax + SIDE - k) % SIDE, part, spans[g]]

    def sib_copy(g, kind, k, half=None):
        ref = quad(g, kind, k, half)
        slot = k if half is None else 2 + 2 * half
        return remote(
            ref, ref, sib_send.at[g, kind, slot], sib_recv.at[g, kind, slot], dom, sib
        )

    def second_peer(kind, k):
        return (y_peer, x_peer)[kind](k)

    first = []
    second = []
    across = []
    env_row = by * other + ax * core
    env_copies = []
    for g in range(2):
        for slot in range(groups[g].start, groups[g].stop):
            one_arrival(slot)
        tiles = ring[groups[g]]
        g1[pl.ds(core, 1), pl.ds(by, 1), pl.ds(ax, 1), groups[g]] = tiles[:, 0][None, None, None]
        g2[pl.ds(core, 1), pl.ds(ax, 1), pl.ds(by, 1), groups[g]] = tiles[:, 1][None, None, None]
        copies = []
        for k in (2, 1, 3):
            one = g1.at[core, by, ax, spans[g]]
            copies.append(remote(one, one, a_send.at[g, 0, k], a_recv.at[g, 0, k], x_peer(k), me))
            two = g2.at[core, ax, by, spans[g]]
            copies.append(remote(two, two, a_send.at[g, 1, k], a_recv.at[g, 1, k], y_peer(k), me))
        for copy in copies:
            copy.start()
        first.append(copies)
        if g == 1:
            each(15, lambda q: lat_copy(q).start())
            tile_copies[14].wait_recv()
            for n in range(7):
                for c in range(2):
                    chip = (z + DEPTH - NEAR_Z[n]) % DEPTH
                    ge[pl.ds(core, 1), pl.ds(2 * chip + c, 1), pl.ds(env_row, 1)] = ring[
                        2 * n + c, 2
                    ][None, None, None]
            for c in range(2):
                ge[pl.ds(core, 1), pl.ds(2 * z + c, 1), pl.ds(env_row, 1)] = ring[14 + c, 2][
                    None, None, None
                ]
            for k in (2, 1, 3):
                three = ge.at[core, :, env_row]
                to = (ax + k * core) % SIDE * SIDE + (by + k * other) % SIDE
                env_copies.append(remote(three, three, e_send.at[k], e_recv.at[k], to, me))
            for copy in env_copies:
                copy.start()
        for copy in copies:
            copy.wait_recv()
        copies = {}
        for k in (1, 3):
            for kind in range(2):
                mine = quad(g, kind, 0)
                copies[kind, k] = remote(
                    mine, mine, b_send.at[g, kind, k], b_recv.at[g, kind, k],
                    second_peer(kind, k), me,
                )
                copies[kind, k].start()
        second.append(copies)
        for kind in range(2):
            copy = sib_copy(g, kind, 0)
            copy.start()
            across.append(copy)

    def make_slots(d):
        found = [jnp.int32(32)] * 4
        for b in range(32):
            hit = dest_ref[b] == d
            found = [jnp.where(hit, new, old) for new, old in zip([b] + found[:3], found)]
        for s in range(4):
            slots[4 * d + s] = found[s]

    relays = []
    for g in range(2):
        copies = {}
        for half, k in enumerate((1, 3)):
            for kind in range(2):
                second[g][kind, k].wait_recv()
                theirs = quad(g, kind, k, half)
                copies[kind, half] = remote(
                    theirs, theirs, b_send.at[g, kind, 2 * half], b_recv.at[g, kind, 2 * half],
                    second_peer(kind, k), me,
                )
                copies[kind, half].start()
        relays.append(copies)
        for k in (1, 3):
            for kind in range(2):
                copy = sib_copy(g, kind, k)
                copy.start()
                across.append(copy)
        if g == 0:
            each(NDOM, make_slots)
            sums[32] = jnp.zeros((144, 128), F32)
            same = lax.broadcasted_iota(jnp.int32, (16, 16), 0) == lax.broadcasted_iota(
                jnp.int32, (16, 16), 1
            )
            gain = jnp.zeros((16, 128), F32)
            for s in range(4):
                column = jnp.sum(jnp.where(same, gain_ref[s : s + 1, :], 0.0), axis=1, keepdims=True)
                gain = gain + jnp.where(spec_ref[...] == s, column, 0.0)
    for copy in env_copies:
        copy.wait_recv()
    last = remote(ge.at[core], ge.at[core], own_send.at[2], own_recv.at[2], dom, sib)
    last.start()
    across.append(last)
    each(15, lambda q: lat_copy(q).wait_recv())
    for n in range(4):
        block = x_in[4 * n : 4 * n + 4].reshape(256, 256).astype(F32)
        x_t[:, 256 * n : 256 * n + 256] = block.T.astype(BF16)
    def pass_relays(g):
        for half in range(2):
            for kind in range(2):
                relays[g][kind, half].wait_recv()
                copy = sib_copy(g, kind, 2, half)
                copy.start()
                across.append(copy)

    def sib_arrivals(g, kind):
        for k in (0, 1, 3):
            sib_copy(g, kind, k).wait_recv()
        for half in range(2):
            sib_copy(g, kind, 2, half).wait_recv()

    def first_layer(g):
        def layer(r):
            rows = pl.ds(pl.multiple_of(16 * r, 16), 16)
            tiles = jnp.concatenate(
                [
                    g1[c, b, r, groups[g]].reshape(-1, 128)
                    for b in range(SIDE)
                    for c in range(2)
                ],
                axis=1,
            )
            if g == 1:
                tiles = jnp.concatenate([tiles, own1[0, rows, :], own1[1, rows, :]], axis=0)
            v = dot(x_t[...], tiles, ((1,), (1,)))
            hid[g, r] = (v / (1.0 + jnp.exp(-v))).astype(BF16)

        each(SIDE, layer)

    def second_layer(g, b):
        lanes = slice(256 * b, 256 * b + 256)
        matrix = []
        for r in range(SIDE):
            tiles = jnp.concatenate(
                [g2[c, r, b, groups[g]].reshape(-1, 128) for c in range(2)], axis=1
            )
            matrix.append(tiles)
            if g == 1:
                rows = slice(16 * r, 16 * r + 16)
                matrix += [own2[0, rows, lanes], own2[1, rows, lanes]]
        hidden = jnp.concatenate([hid[g, r] for r in range(SIDE)], axis=1)
        return dot(hidden, jnp.concatenate(matrix, axis=0), ((1,), (0,)))

    pass_relays(0)
    sib_arrivals(0, 0)
    first_layer(0)
    sib_arrivals(0, 1)
    for b in range(SIDE):
        update[:, 256 * b : 256 * b + 256] = second_layer(0, b)
    pass_relays(1)
    own_copies[0].wait_recv()
    sib_arrivals(1, 0)
    first_layer(1)
    own_copies[1].wait_recv()
    sib_arrivals(1, 1)
    for b in range(SIDE):
        lanes = slice(256 * b, 256 * b + 256)
        total = update[:, lanes] + second_layer(1, b)
        lnt[:, lanes] = (x_t[:, lanes].astype(F32) + total).astype(BF16)

    last.wait_recv()
    matrix = jnp.concatenate([ge[c].reshape(1024, 128) for c in range(2)], axis=1)
    env_weights = dot(lnt[...], matrix, ((1,), (0,)))
    ws[...] = env_weights.T.astype(BF16).reshape(16, 16, 256)
    each(15, lambda q: w_copy(q).start())
    wt[pl.ds(me, 1)] = ws[pl.ds(me, 1)]

    for b in range(SIDE):
        block = lnt[:, 256 * b : 256 * b + 256].astype(F32).T.astype(BF16)
        ln[4 * b : 4 * b + 4] = block.reshape(4, 64, 256)
    def block_sums(t):
        w = wt[t].astype(F32)
        h = hs[t]
        for j in range(2):
            lanes = slice(128 * j, 128 * j + 128)
            wj = w[:, lanes]
            alive = h[9:10, lanes]
            contrib = jnp.concatenate(
                [((h[m : m + 1, lanes] * wj) * alive).astype(BF16) for m in range(9)], axis=0
            )
            sums[2 * t + j] = dot(contrib, onehot[2 * t + j], ((1,), (1,)))

    each(15, lambda q: w_copy(q).wait_recv())
    each(NTP, block_sums, unroll=4)

    def domain_sum(d):
        total = sums[slots[4 * d]] + sums[slots[4 * d + 1]]
        return total + (sums[slots[4 * d + 2]] + sums[slots[4 * d + 3]])

    def q_copy(part, q):
        out, into = ((p_low, in_low), (p_high, in_high))[part]
        to = dom_far(q)
        return remote(
            out.at[to], into.at[dom], q_send.at[part, q], q_recv.at[part, q], to, me
        )

    def t_copy(part, q):
        ref = (table_low, table_high)[part]
        return remote(
            ref.at[dom], ref.at[dom], t_send.at[part, q], t_recv.at[part, q], dom_far(q), me
        )

    for q in range(NDOM - 1):
        to = dom_far(q)
        total = domain_sum(to).astype(BF16)
        p_low[pl.ds(to, 1)] = total[None, :64]
        p_high[pl.ds(to, 1)] = total[None, 64:]
        q_copy(0, q).start()
    for q in range(NDOM - 1):
        q_copy(1, q).start()
    own = pltpu.make_async_copy(
        ln.at[me], ln_out.at[:, pl.ds(pl.multiple_of(me * 256, 256), 256)], pre_sem.at[6]
    )
    own.start()
    each(15, lambda q: ln_copy(q).start())
    total = domain_sum(dom)
    in_low[pl.ds(dom, 1)] = jnp.zeros((1, 64, 128), BF16)
    in_high[pl.ds(dom, 1)] = jnp.zeros((1, 80, 128), BF16)
    for part in range(2):
        into, ref = ((in_low, table_low), (in_high, table_high))[part]
        rows = (slice(0, 64), slice(64, 144))[part]
        comps = (slice(0, 4), slice(4, 9))[part]
        for q in range(NDOM - 1):
            q_copy(part, q).wait_recv()

        acc = total[rows]
        for d in range(NDOM):
            acc = acc + into[d].astype(F32)
        env = acc.reshape(-1, 16, 128) * gain[None] * env_factor
        ref[pl.ds(dom, 1)] = env.reshape(1, -1, 128).astype(BF16)
        for q in range(NDOM - 1):
            t_copy(part, q).start()
        env_out[comps] = env

    def finish(t, part):
        w = wt[t].astype(F32)
        h = hs[t]
        ref = (table_low, table_high)[part]
        base = (0, 4)[part]
        spans_of = (((0,), (1, 2, 3)), ((4, 5, 6, 7, 8),))[part]
        parts = [[] for _ in spans_of]
        for j in range(2):
            lanes = slice(128 * j, 128 * j + 128)
            env_edge = dot(ref[dest_ref[2 * t + j]], onehot[2 * t + j], ((1,), (0,)))
            for l, comps in enumerate(spans_of):
                degree = None
                for m in comps:
                    term = env_edge[16 * (m - base) : 16 * (m - base) + 16] * h[m : m + 1, lanes]
                    degree = term if degree is None else degree + term
                parts[l].append(degree * w[:, lanes] * h[9:10, lanes])
        for l in range(len(spans_of)):
            inv_out[(0, 2)[part] + l, :, pl.ds(pl.multiple_of(t * 256, 256), 256)] = (
                jnp.concatenate(parts[l], axis=1)
            )

    for part in range(2):
        for q in range(NDOM - 1):
            t_copy(part, q).wait_recv()
        each(NTP, lambda t: finish(t, part), unroll=4)

    own.wait()
    each(15, lambda q: ln_copy(q).wait_recv())
    for copy in tile_copies + own_copies + first[0] + first[1] + env_copies:
        copy.wait_send()
    for copy in across:
        copy.wait_send()
    for copies in second + relays:
        for copy in copies.values():
            copy.wait_send()
    for make in (lat_copy, w_copy, ln_copy):
        each(15, lambda q: make(q).wait_send())
    for part in range(2):
        for q in range(NDOM - 1):
            q_copy(part, q).wait_send()
            t_copy(part, q).wait_send()


def write_out(ln_in, env_in, inv_in, ln_out, env_out, inv_out, ln, env, inv, sem_in, sem_out):
    parts = [(env_in, env, env_out)]
    for n in range(2):
        rows = pl.ds(32 * n, 32)
        parts.append((ln_in.at[rows], ln.at[rows], ln_out.at[rows]))
    for l in range(3):
        parts.append((inv_in.at[l], inv.at[l], inv_out.at[l]))
    reads = [
        pltpu.make_async_copy(src, mid, sem_in.at[n]) for n, (src, mid, _) in enumerate(parts)
    ]
    writes = [
        pltpu.make_async_copy(mid, dst, sem_out.at[n]) for n, (_, mid, dst) in enumerate(parts)
    ]
    for copy in reads:
        copy.start()
    for read, write in zip(reads, writes):
        read.wait()
        write.start()
    for copy in writes:
        copy.wait()


def on_device(
    latent, w_first, w_second, w_env, edge_vec, centers, block_dest, block_fill, species,
    species_gain,
):
    vmem = pl.BlockSpec(memory_space=pltpu.VMEM)
    hbm = pl.BlockSpec(memory_space=pltpu.HBM)
    dma = pltpu.SemaphoreType.DMA
    shapes = (
        jax.ShapeDtypeStruct((64, 4096), BF16),
        jax.ShapeDtypeStruct((9, 16, 128), F32),
        jax.ShapeDtypeStruct((3, 16, 4096), F32),
    )
    results = pl.pallas_call(
        kernel,
        out_shape=shapes,
        in_specs=[hbm] * 10,
        out_specs=(vmem, vmem, vmem),
        scratch_shapes=[
            pltpu.SMEM((32,), jnp.int32),
            pltpu.SMEM((32,), jnp.int32),
            pltpu.VMEM((3, 4096), F32),
            pltpu.VMEM((32, 128), jnp.int32),
            pltpu.VMEM((1, 128), jnp.int32),
            pltpu.VMEM((4, 16), F32),
            pltpu.VMEM((2, 3, 16, 128), BF16),
            pltpu.VMEM((16, 3, 16, 128), BF16),
            pltpu.VMEM((2, 64, 1024), BF16),
            pltpu.VMEM((2, 64, 1024), BF16),
            pltpu.VMEM((2, 4, 4, 14, 16, 128), BF16),
            pltpu.VMEM((2, 4, 4, 14, 16, 128), BF16),
            pltpu.VMEM((2, 16, 4, 16, 128), BF16),
            pltpu.VMEM((16, 64, 256), BF16),
            pltpu.VMEM((256, 1024), BF16),
            pltpu.VMEM((2, 4, 256, 128), BF16),
            pltpu.VMEM((256, 1024), F32),
            pltpu.VMEM((256, 1024), BF16),
            pltpu.VMEM((16, 64, 256), BF16),
            pltpu.VMEM((16, 16, 256), BF16),
            pltpu.VMEM((16, 16, 256), BF16),
            pltpu.VMEM((16, 16, 256), F32),
            pltpu.VMEM((32, 128, 128), BF16),
            pltpu.SMEM((64,), jnp.int32),
            pltpu.VMEM((33, 144, 128), F32),
            pltpu.VMEM((16, 64, 128), BF16),
            pltpu.VMEM((16, 80, 128), BF16),
            pltpu.VMEM((16, 64, 128), BF16),
            pltpu.VMEM((16, 80, 128), BF16),
            pltpu.VMEM((16, 64, 128), BF16),
            pltpu.VMEM((16, 80, 128), BF16),
            dma((16,)),
            dma((15,)), dma((15,)), dma((15,)), dma((15,)), dma((3,)), dma((3,)),
            dma((2, 2, 4)), dma((2, 2, 4)), dma((2, 2, 4)), dma((2, 2, 4)), dma((4,)), dma((4,)),
            dma((2, 2, 5)), dma((2, 2, 5)),
            dma((15,)), dma((15,)), dma((15,)), dma((15,)),
            dma((2, 15)), dma((2, 15)), dma((2, 15)), dma((2, 15)),
        ],
        compiler_params=pltpu.CompilerParams(
            collective_id=0, has_side_effects=True, vmem_limit_bytes=60 * 1024 * 1024
        ),
        cost_estimate=pl.CostEstimate(
            flops=2 * 10**9, bytes_accessed=4 * 10**6, transcendentals=300000
        ),
        name="allegro",
    )(
        block_dest.reshape(32), block_fill, latent, w_first.T, w_second, w_env, edge_vec,
        centers.reshape(32, 128), species.reshape(1, 128), species_gain,
    )
    return pl.pallas_call(
        write_out,
        out_shape=shapes,
        in_specs=[hbm] * 3,
        out_specs=(hbm,) * 3,
        scratch_shapes=[
            pltpu.VMEM((64, 4096), BF16),
            pltpu.VMEM((9, 16, 128), F32),
            pltpu.VMEM((3, 16, 4096), F32),
            dma((6,)),
            dma((6,)),
        ],
        compiler_params=pltpu.CompilerParams(vmem_limit_bytes=60 * 1024 * 1024),
        name="write_out",
    )(*results)


def solution(mesh):
    in_specs = (
        P("tp", "dom"),
        P(None, "tp"),
        P("tp", None),
        P("tp", None),
        P(None, "dom"),
        P("dom"),
        P("dom", None),
        P("dom"),
        P("dom"),
        P(None, "tp"),
    )
    out_specs = (P("tp", "dom"), P(None, "tp", "dom"), P(None, "tp", "dom"))
    return jax.shard_map(
        on_device, mesh=mesh, in_specs=in_specs, out_specs=out_specs, check_vma=False
    )
```

```python
import math

import jax
import jax.numpy as jnp
from jax import lax
from jax.experimental import pallas as pl
from jax.experimental.pallas import tpu as pltpu
from jax.sharding import PartitionSpec as P

MESH = pl.DeviceIdType.MESH
F32 = jnp.float32
BF16 = jnp.bfloat16

root_three = math.sqrt(3.0)
root_five = math.sqrt(5.0)
root_fifteen = math.sqrt(15.0)
cutoff_radius = 6.0
env_factor = 0.25

SIDE = 4
NDOM = 16
NTP = 16
DEPTH = 8
HALF = DEPTH // 2
NEAR_Z = (6, 2, 7, 1, 4, 5, 3)
FAR = sorted(
    [(dx, dy) for dx in range(SIDE) for dy in range(SIDE) if dx or dy],
    key=lambda d: -min(d[0], SIDE - d[0]) - min(d[1], SIDE - d[1]),
)


def dot(left, right, dims):
    return lax.dot_general(left, right, (dims, ((), ())), preferred_element_type=F32)


def kernel(
    dest, fill, latent, w1, w2, we, ev, cen, spec, gains,
    ln_out, env_out, inv_out,
    dest_ref, fill_ref, ev_ref, cen_ref, spec_ref, gain_ref,
    pieces, ring, own1, own2, g1, g2, ge, x_in, x_t, hid, lnt, ln, ws, wt, hs, onehot, slots,
    sums, p_low, p_high, in_low, in_high, table_low, table_high,
    pre_sem, lat_send, lat_recv, one_send, one_recv, own_send, own_recv,
    a_send, a_recv, b_send, b_recv, e_send, e_recv,
    sib_send, sib_recv, w_send, w_recv, ln_send, ln_recv, q_send, q_recv, t_send, t_recv,
):
    dom = lax.axis_index("dom")
    me = lax.axis_index("tp")
    ax = dom // SIDE
    by = dom % SIDE
    core = me % 2
    other = 1 - core
    z = me // 2
    sib = 2 * z + other

    def tp_far(q):
        s = q // 2
        dz = HALF + (s + 1) // 2 * (1 - 2 * (s % 2))
        return 2 * ((z + dz) % DEPTH) + (core + 1 + q) % 2

    def dom_far(q):
        dx, dy = FAR[q]
        return (ax + dx) % SIDE * SIDE + (by + dy) % SIDE

    def x_peer(k):
        return (ax + k) % SIDE * SIDE + by

    def y_peer(k):
        return ax * SIDE + (by + k) % SIDE

    def remote(src, dst, send, recv, to_dom, to_tp):
        return pltpu.make_async_remote_copy(
            src_ref=src, dst_ref=dst, send_sem=send, recv_sem=recv,
            device_id=(to_dom, to_tp), device_id_type=MESH,
        )

    def each(count, act, unroll=1):
        def body(q, carry):
            act(q)
            return carry

        lax.fori_loop(0, count, body, 0, unroll=unroll)

    pre = [
        pltpu.make_async_copy(
            latent.at[:, pl.ds(pl.multiple_of(me * 256, 256), 256)], x_in.at[me], pre_sem.at[7]
        ),
        pltpu.make_async_copy(w1, own1.at[core], pre_sem.at[8]),
        pltpu.make_async_copy(w2, own2.at[core], pre_sem.at[9]),
    ]
    for half in range(2):
        lanes = pl.ds(pl.multiple_of(by * 256 + 128 * half, 128), 128)
        for i, matrix in enumerate([w1, w2]):
            pre.append(
                pltpu.make_async_copy(
                    matrix.at[pl.ds(ax * 16, 16), lanes],
                    pieces.at[half, i], pre_sem.at[2 * i + half],
                )
            )
        pre.append(
            pltpu.make_async_copy(
                we.at[pl.ds((by, ax)[half] * 16, 16), pl.ds(128 * half, 128)],
                pieces.at[half, 2], pre_sem.at[4 + half],
            )
        )
    for copy in pre:
        copy.start()

    small = [
        pltpu.make_async_copy(src, dst, pre_sem.at[10 + i])
        for i, (src, dst) in enumerate(
            [
                (dest, dest_ref), (fill, fill_ref), (ev, ev_ref), (cen, cen_ref),
                (spec, spec_ref), (gains, gain_ref),
            ]
        )
    ]
    for copy in small:
        copy.start()
    barrier = pltpu.get_barrier_semaphore()

    def greet_tp(q):
        pl.semaphore_signal(barrier, inc=1, device_id=(dom, tp_far(q)), device_id_type=MESH)

    each(NTP - 1, greet_tp)
    for q in range(NDOM - 1):
        pl.semaphore_signal(barrier, inc=1, device_id=(dom_far(q), me), device_id_type=MESH)
    for copy in pre:
        copy.wait()
    ring[pl.ds(14 + core, 1)] = pieces[pl.ds(core, 1)]
    pl.semaphore_wait(barrier, NTP - 1 + NDOM - 1)

    def one_copy(n, c):
        to = 2 * ((z + NEAR_Z[n]) % DEPTH) + c
        return remote(
            pieces.at[c], ring.at[2 * n + core], one_send.at[2 * n + c],
            one_recv.at[2 * n + core], dom, to,
        )

    def one_arrival(slot):
        remote(
            pieces.at[0], ring.at[slot], one_send.at[slot], one_recv.at[slot], dom, sib
        ).wait_recv()

    tile_copies = [one_copy(n, c) for n in range(7) for c in range(2)]
    tile_copies.append(
        remote(
            pieces.at[other], ring.at[14 + core], one_send.at[14], one_recv.at[14], dom, sib
        )
    )
    own_copies = [
        remote(ref.at[core], ref.at[core], own_send.at[i], own_recv.at[i], dom, sib)
        for i, ref in enumerate([own1, own2])
    ]
    for copy in tile_copies + own_copies:
        copy.start()

    def lat_copy(q):
        to = tp_far(q)
        return remote(
            latent.at[:, pl.ds(pl.multiple_of(to * 256, 256), 256)], x_in.at[me],
            lat_send.at[q], lat_recv.at[q], dom, to,
        )

    def w_copy(q):
        to = tp_far(q)
        return remote(ws.at[to], wt.at[me], w_send.at[q], w_recv.at[q], dom, to)

    def ln_copy(q):
        to = tp_far(q)
        return remote(
            ln.at[to], ln_out.at[:, pl.ds(pl.multiple_of(me * 256, 256), 256)],
            ln_send.at[q], ln_recv.at[q], dom, to,
        )

    for copy in small:
        copy.wait()

    def harmonics(t):
        v = ev_ref[:, pl.ds(pl.multiple_of(t * 256, 256), 256)]
        along_x, along_y, along_z = v[0:1], v[1:2], v[2:3]
        radius = jnp.sqrt(along_x * along_x + along_y * along_y + along_z * along_z)
        ux = along_x / radius
        uy = along_y / radius
        uz = along_z / radius
        ratio = radius / cutoff_radius
        flat = 1.0 - ratio * ratio
        envelope = flat * flat
        spot = lax.broadcasted_iota(jnp.int32, (1, 128), 1)
        alive = jnp.concatenate(
            [(spot < fill_ref[2 * t + j]).astype(F32) for j in range(2)], axis=1
        )
        rows = [
            envelope,
            root_three * ux * envelope,
            root_three * uy * envelope,
            root_three * uz * envelope,
            root_fifteen * ux * uy * envelope,
            root_fifteen * uy * uz * envelope,
            root_five / 2.0 * (3.0 * uz * uz - 1.0) * envelope,
            root_fifteen * ux * uz * envelope,
            root_fifteen / 2.0 * (ux * ux - uy * uy) * envelope,
            alive,
        ]
        for m, row in enumerate(rows):
            hs[t, m : m + 1, :] = row

    each(NTP, harmonics)

    def make_onehot(b):
        atoms = lax.broadcasted_iota(jnp.int32, (128, 128), 0)
        onehot[b] = (atoms == cen_ref[pl.ds(b, 1), :]).astype(F32).astype(BF16)

    each(32, make_onehot)

    groups = [slice(0, 8), slice(8, 14)]
    spans = [pl.ds(0, 8), pl.ds(8, 6)]

    def quad(g, kind, k, half=None):
        part = slice(None) if half is None else pl.ds(2 * half, 2)
        if kind == 0:
            return g1.at[core, (by + SIDE - k) % SIDE, part, spans[g]]
        return g2.at[core, (ax + SIDE - k) % SIDE, part, spans[g]]

    def sib_copy(g, kind, k, half=None):
        ref = quad(g, kind, k, half)
        slot = k if half is None else 2 + 2 * half
        return remote(
            ref, ref, sib_send.at[g, kind, slot], sib_recv.at[g, kind, slot], dom, sib
        )

    def second_peer(kind, k):
        return (y_peer, x_peer)[kind](k)

    first = []
    second = []
    across = []
    env_row = by * other + ax * core
    env_copies = []
    for g in range(2):
        for slot in range(groups[g].start, groups[g].stop):
            one_arrival(slot)
        tiles = ring[groups[g]]
        g1[pl.ds(core, 1), pl.ds(by, 1), pl.ds(ax, 1), groups[g]] = tiles[:, 0][None, None, None]
        g2[pl.ds(core, 1), pl.ds(ax, 1), pl.ds(by, 1), groups[g]] = tiles[:, 1][None, None, None]
        copies = []
        for k in (2, 1, 3):
            one = g1.at[core, by, ax, spans[g]]
            copies.append(remote(one, one, a_send.at[g, 0, k], a_recv.at[g, 0, k], x_peer(k), me))
            two = g2.at[core, ax, by, spans[g]]
            copies.append(remote(two, two, a_send.at[g, 1, k], a_recv.at[g, 1, k], y_peer(k), me))
        for copy in copies:
            copy.start()
        first.append(copies)
        if g == 0:
            each(15, lambda q: lat_copy(q).start())
        if g == 1:
            tile_copies[14].wait_recv()
            for n in range(7):
                for c in range(2):
                    chip = (z + DEPTH - NEAR_Z[n]) % DEPTH
                    ge[pl.ds(core, 1), pl.ds(2 * chip + c, 1), pl.ds(env_row, 1)] = ring[
                        2 * n + c, 2
                    ][None, None, None]
            for c in range(2):
                ge[pl.ds(core, 1), pl.ds(2 * z + c, 1), pl.ds(env_row, 1)] = ring[14 + c, 2][
                    None, None, None
                ]
            for k in (2, 1, 3):
                three = ge.at[core, :, env_row]
                to = (ax + k * core) % SIDE * SIDE + (by + k * other) % SIDE
                env_copies.append(remote(three, three, e_send.at[k], e_recv.at[k], to, me))
            for copy in env_copies:
                copy.start()
        for copy in copies:
            copy.wait_recv()
        copies = {}
        for k in (1, 3):
            for kind in range(2):
                mine = quad(g, kind, 0)
                copies[kind, k] = remote(
                    mine, mine, b_send.at[g, kind, k], b_recv.at[g, kind, k],
                    second_peer(kind, k), me,
                )
                copies[kind, k].start()
        second.append(copies)
        for kind in range(2):
            copy = sib_copy(g, kind, 0)
            copy.start()
            across.append(copy)

    def make_slots(d):
        found = [jnp.int32(32)] * 4
        for b in range(32):
            hit = dest_ref[b] == d
            found = [jnp.where(hit, new, old) for new, old in zip([b] + found[:3], found)]
        for s in range(4):
            slots[4 * d + s] = found[s]

    relays = []
    for g in range(2):
        copies = {}
        for half, k in enumerate((1, 3)):
            for kind in range(2):
                second[g][kind, k].wait_recv()
                theirs = quad(g, kind, k, half)
                copies[kind, half] = remote(
                    theirs, theirs, b_send.at[g, kind, 2 * half], b_recv.at[g, kind, 2 * half],
                    second_peer(kind, k), me,
                )
                copies[kind, half].start()
        relays.append(copies)
        for k in (1, 3):
            for kind in range(2):
                copy = sib_copy(g, kind, k)
                copy.start()
                across.append(copy)
        if g == 0:
            each(NDOM, make_slots)
            sums[32] = jnp.zeros((144, 128), F32)
            same = lax.broadcasted_iota(jnp.int32, (16, 16), 0) == lax.broadcasted_iota(
                jnp.int32, (16, 16), 1
            )
            gain = jnp.zeros((16, 128), F32)
            for s in range(4):
                column = jnp.sum(jnp.where(same, gain_ref[s : s + 1, :], 0.0), axis=1, keepdims=True)
                gain = gain + jnp.where(spec_ref[...] == s, column, 0.0)
    for copy in env_copies:
        copy.wait_recv()
    last = remote(ge.at[core], ge.at[core], own_send.at[2], own_recv.at[2], dom, sib)
    last.start()
    across.append(last)
    each(15, lambda q: lat_copy(q).wait_recv())
    for n in range(4):
        block = x_in[4 * n : 4 * n + 4].reshape(256, 256).astype(F32)
        x_t[:, 256 * n : 256 * n + 256] = block.T.astype(BF16)
    for g in range(2):
        for half in range(2):
            for kind in range(2):
                relays[g][kind, half].wait_recv()
                copy = sib_copy(g, kind, 2, half)
                copy.start()
                across.append(copy)

    def sib_arrivals(kind):
        own_copies[kind].wait_recv()
        for g in range(2):
            for k in (0, 1, 3):
                sib_copy(g, kind, k).wait_recv()
            for half in range(2):
                sib_copy(g, kind, 2, half).wait_recv()

    sib_arrivals(0)

    def first_layer(r):
        tiles = jnp.concatenate(
            [g1[c, b, r].reshape(224, 128) for b in range(SIDE) for c in range(2)], axis=1
        )
        rows = pl.ds(pl.multiple_of(16 * r, 16), 16)
        matrix = jnp.concatenate([tiles, own1[0, rows, :], own1[1, rows, :]], axis=0)
        v = dot(x_t[...], matrix, ((1,), (1,)))
        hid[r] = (v / (1.0 + jnp.exp(-v))).astype(BF16)

    each(SIDE, first_layer)
    sib_arrivals(1)
    for b in range(SIDE):
        lanes = slice(256 * b, 256 * b + 256)
        update = jnp.zeros((256, 256), F32)
        for r in range(SIDE):
            tiles = jnp.concatenate([g2[c, r, b].reshape(224, 128) for c in range(2)], axis=1)
            rows = slice(16 * r, 16 * r + 16)
            matrix = jnp.concatenate([tiles, own2[0, rows, lanes], own2[1, rows, lanes]], axis=0)
            update = update + dot(hid[r], matrix, ((1,), (0,)))
        lnt[:, lanes] = (x_t[:, lanes].astype(F32) + update).astype(BF16)

    last.wait_recv()
    matrix = jnp.concatenate([ge[c].reshape(1024, 128) for c in range(2)], axis=1)
    env_weights = dot(lnt[...], matrix, ((1,), (0,)))
    ws[...] = env_weights.T.astype(BF16).reshape(16, 16, 256)
    each(15, lambda q: w_copy(q).start())
    wt[pl.ds(me, 1)] = ws[pl.ds(me, 1)]

    for b in range(SIDE):
        block = lnt[:, 256 * b : 256 * b + 256].astype(F32).T.astype(BF16)
        ln[4 * b : 4 * b + 4] = block.reshape(4, 64, 256)
    def block_sums(t):
        w = wt[t].astype(F32)
        h = hs[t]
        for j in range(2):
            lanes = slice(128 * j, 128 * j + 128)
            wj = w[:, lanes]
            alive = h[9:10, lanes]
            contrib = jnp.concatenate(
                [((h[m : m + 1, lanes] * wj) * alive).astype(BF16) for m in range(9)], axis=0
            )
            sums[2 * t + j] = dot(contrib, onehot[2 * t + j], ((1,), (1,)))

    each(15, lambda q: w_copy(q).wait_recv())
    each(NTP, block_sums, unroll=4)

    def domain_sum(d):
        total = sums[slots[4 * d]] + sums[slots[4 * d + 1]]
        return total + (sums[slots[4 * d + 2]] + sums[slots[4 * d + 3]])

    def q_copy(part, q):
        out, into = ((p_low, in_low), (p_high, in_high))[part]
        to = dom_far(q)
        return remote(
            out.at[to], into.at[dom], q_send.at[part, q], q_recv.at[part, q], to, me
        )

    def t_copy(part, q):
        ref = (table_low, table_high)[part]
        return remote(
            ref.at[dom], ref.at[dom], t_send.at[part, q], t_recv.at[part, q], dom_far(q), me
        )

    for q in range(NDOM - 1):
        to = dom_far(q)
        total = domain_sum(to).astype(BF16)
        p_low[pl.ds(to, 1)] = total[None, :64]
        p_high[pl.ds(to, 1)] = total[None, 64:]
        q_copy(0, q).start()
    for q in range(NDOM - 1):
        q_copy(1, q).start()
    own = pltpu.make_async_copy(
        ln.at[me], ln_out.at[:, pl.ds(pl.multiple_of(me * 256, 256), 256)], pre_sem.at[6]
    )
    own.start()
    each(15, lambda q: ln_copy(q).start())
    total = domain_sum(dom)
    in_low[pl.ds(dom, 1)] = jnp.zeros((1, 64, 128), BF16)
    in_high[pl.ds(dom, 1)] = jnp.zeros((1, 80, 128), BF16)
    for part in range(2):
        into, ref = ((in_low, table_low), (in_high, table_high))[part]
        rows = (slice(0, 64), slice(64, 144))[part]
        comps = (slice(0, 4), slice(4, 9))[part]
        for q in range(NDOM - 1):
            q_copy(part, q).wait_recv()

        acc = total[rows]
        for d in range(NDOM):
            acc = acc + into[d].astype(F32)
        env = acc.reshape(-1, 16, 128) * gain[None] * env_factor
        ref[pl.ds(dom, 1)] = env.reshape(1, -1, 128).astype(BF16)
        for q in range(NDOM - 1):
            t_copy(part, q).start()
        env_out[comps] = env

    def finish(t, part):
        w = wt[t].astype(F32)
        h = hs[t]
        ref = (table_low, table_high)[part]
        base = (0, 4)[part]
        spans_of = (((0,), (1, 2, 3)), ((4, 5, 6, 7, 8),))[part]
        parts = [[] for _ in spans_of]
        for j in range(2):
            lanes = slice(128 * j, 128 * j + 128)
            env_edge = dot(ref[dest_ref[2 * t + j]], onehot[2 * t + j], ((1,), (0,)))
            for l, comps in enumerate(spans_of):
                degree = None
                for m in comps:
                    term = env_edge[16 * (m - base) : 16 * (m - base) + 16] * h[m : m + 1, lanes]
                    degree = term if degree is None else degree + term
                parts[l].append(degree * w[:, lanes] * h[9:10, lanes])
        for l in range(len(spans_of)):
            inv_out[(0, 2)[part] + l, :, pl.ds(pl.multiple_of(t * 256, 256), 256)] = (
                jnp.concatenate(parts[l], axis=1)
            )

    for part in range(2):
        for q in range(NDOM - 1):
            t_copy(part, q).wait_recv()
        each(NTP, lambda t: finish(t, part), unroll=4)

    own.wait()
    each(15, lambda q: ln_copy(q).wait_recv())
    for copy in tile_copies + own_copies + first[0] + first[1] + env_copies:
        copy.wait_send()
    for copy in across:
        copy.wait_send()
    for copies in second + relays:
        for copy in copies.values():
            copy.wait_send()
    for make in (lat_copy, w_copy, ln_copy):
        each(15, lambda q: make(q).wait_send())
    for part in range(2):
        for q in range(NDOM - 1):
            q_copy(part, q).wait_send()
            t_copy(part, q).wait_send()


def write_out(ln_in, env_in, inv_in, ln_out, env_out, inv_out, ln, env, inv, sem_in, sem_out):
    parts = [(env_in, env, env_out)]
    for n in range(2):
        rows = pl.ds(32 * n, 32)
        parts.append((ln_in.at[rows], ln.at[rows], ln_out.at[rows]))
    for l in range(3):
        parts.append((inv_in.at[l], inv.at[l], inv_out.at[l]))
    reads = [
        pltpu.make_async_copy(src, mid, sem_in.at[n]) for n, (src, mid, _) in enumerate(parts)
    ]
    writes = [
        pltpu.make_async_copy(mid, dst, sem_out.at[n]) for n, (_, mid, dst) in enumerate(parts)
    ]
    for copy in reads:
        copy.start()
    for read, write in zip(reads, writes):
        read.wait()
        write.start()
    for copy in writes:
        copy.wait()


def on_device(
    latent, w_first, w_second, w_env, edge_vec, centers, block_dest, block_fill, species,
    species_gain,
):
    vmem = pl.BlockSpec(memory_space=pltpu.VMEM)
    hbm = pl.BlockSpec(memory_space=pltpu.HBM)
    dma = pltpu.SemaphoreType.DMA
    shapes = (
        jax.ShapeDtypeStruct((64, 4096), BF16),
        jax.ShapeDtypeStruct((9, 16, 128), F32),
        jax.ShapeDtypeStruct((3, 16, 4096), F32),
    )
    results = pl.pallas_call(
        kernel,
        out_shape=shapes,
        in_specs=[hbm] * 10,
        out_specs=(vmem, vmem, vmem),
        scratch_shapes=[
            pltpu.SMEM((32,), jnp.int32),
            pltpu.SMEM((32,), jnp.int32),
            pltpu.VMEM((3, 4096), F32),
            pltpu.VMEM((32, 128), jnp.int32),
            pltpu.VMEM((1, 128), jnp.int32),
            pltpu.VMEM((4, 16), F32),
            pltpu.VMEM((2, 3, 16, 128), BF16),
            pltpu.VMEM((16, 3, 16, 128), BF16),
            pltpu.VMEM((2, 64, 1024), BF16),
            pltpu.VMEM((2, 64, 1024), BF16),
            pltpu.VMEM((2, 4, 4, 14, 16, 128), BF16),
            pltpu.VMEM((2, 4, 4, 14, 16, 128), BF16),
            pltpu.VMEM((2, 16, 4, 16, 128), BF16),
            pltpu.VMEM((16, 64, 256), BF16),
            pltpu.VMEM((256, 1024), BF16),
            pltpu.VMEM((4, 256, 256), BF16),
            pltpu.VMEM((256, 1024), BF16),
            pltpu.VMEM((16, 64, 256), BF16),
            pltpu.VMEM((16, 16, 256), BF16),
            pltpu.VMEM((16, 16, 256), BF16),
            pltpu.VMEM((16, 16, 256), F32),
            pltpu.VMEM((32, 128, 128), BF16),
            pltpu.SMEM((64,), jnp.int32),
            pltpu.VMEM((33, 144, 128), F32),
            pltpu.VMEM((16, 64, 128), BF16),
            pltpu.VMEM((16, 80, 128), BF16),
            pltpu.VMEM((16, 64, 128), BF16),
            pltpu.VMEM((16, 80, 128), BF16),
            pltpu.VMEM((16, 64, 128), BF16),
            pltpu.VMEM((16, 80, 128), BF16),
            dma((16,)),
            dma((15,)), dma((15,)), dma((15,)), dma((15,)), dma((3,)), dma((3,)),
            dma((2, 2, 4)), dma((2, 2, 4)), dma((2, 2, 4)), dma((2, 2, 4)), dma((4,)), dma((4,)),
            dma((2, 2, 5)), dma((2, 2, 5)),
            dma((15,)), dma((15,)), dma((15,)), dma((15,)),
            dma((2, 15)), dma((2, 15)), dma((2, 15)), dma((2, 15)),
        ],
        compiler_params=pltpu.CompilerParams(
            collective_id=0, has_side_effects=True, vmem_limit_bytes=60 * 1024 * 1024
        ),
        cost_estimate=pl.CostEstimate(
            flops=2 * 10**9, bytes_accessed=4 * 10**6, transcendentals=300000
        ),
        name="allegro",
    )(
        block_dest.reshape(32), block_fill, latent, w_first.T, w_second, w_env, edge_vec,
        centers.reshape(32, 128), species.reshape(1, 128), species_gain,
    )
    return pl.pallas_call(
        write_out,
        out_shape=shapes,
        in_specs=[hbm] * 3,
        out_specs=(hbm,) * 3,
        scratch_shapes=[
            pltpu.VMEM((64, 4096), BF16),
            pltpu.VMEM((9, 16, 128), F32),
            pltpu.VMEM((3, 16, 4096), F32),
            dma((6,)),
            dma((6,)),
        ],
        compiler_params=pltpu.CompilerParams(vmem_limit_bytes=60 * 1024 * 1024),
        name="write_out",
    )(*results)


def solution(mesh):
    in_specs = (
        P("tp", "dom"),
        P(None, "tp"),
        P("tp", None),
        P("tp", None),
        P(None, "dom"),
        P("dom"),
        P("dom", None),
        P("dom"),
        P("dom"),
        P(None, "tp"),
    )
    out_specs = (P("tp", "dom"), P(None, "tp", "dom"), P(None, "tp", "dom"))
    return jax.shard_map(
        on_device, mesh=mesh, in_specs=in_specs, out_specs=out_specs, check_vma=False
    )
```

```python
import math

import jax
import jax.numpy as jnp
from jax import lax
from jax.experimental import pallas as pl
from jax.experimental.pallas import tpu as pltpu
from jax.sharding import PartitionSpec as P

MESH = pl.DeviceIdType.MESH
F32 = jnp.float32
BF16 = jnp.bfloat16

root_three = math.sqrt(3.0)
root_five = math.sqrt(5.0)
root_fifteen = math.sqrt(15.0)
cutoff_radius = 6.0
env_factor = 0.25

SIDE = 4
NDOM = 16
NTP = 16
DEPTH = 8
HALF = DEPTH // 2
NEAR_Z = (6, 2, 7, 1, 4, 5, 3)
FAR = sorted(
    [(dx, dy) for dx in range(SIDE) for dy in range(SIDE) if dx or dy],
    key=lambda d: -min(d[0], SIDE - d[0]) - min(d[1], SIDE - d[1]),
)


def dot(left, right, dims):
    return lax.dot_general(left, right, (dims, ((), ())), preferred_element_type=F32)


def kernel(
    dest, fill, latent, w1, w2, we, ev, cen, spec, gains,
    ln_out, env_out, inv_out,
    dest_ref, fill_ref, ev_ref, cen_ref, spec_ref, gain_ref,
    pieces, ring, own1, own2, g1, g2, ge, x_in, x_t, hid, lnt, ln, ws, wt, hs, onehot, slots,
    sums, p_low, p_high, in_low, in_high, table_low, table_high,
    pre_sem, lat_send, lat_recv, one_send, one_recv, own_send, own_recv,
    a_send, a_recv, b_send, b_recv, e_send, e_recv,
    sib_send, sib_recv, w_send, w_recv, ln_send, ln_recv, q_send, q_recv, t_send, t_recv,
):
    dom = lax.axis_index("dom")
    me = lax.axis_index("tp")
    ax = dom // SIDE
    by = dom % SIDE
    core = me % 2
    other = 1 - core
    z = me // 2
    sib = 2 * z + other

    def tp_far(q):
        s = q // 2
        dz = HALF + (s + 1) // 2 * (1 - 2 * (s % 2))
        return 2 * ((z + dz) % DEPTH) + (core + 1 + q) % 2

    def dom_far(q):
        dx, dy = FAR[q]
        return (ax + dx) % SIDE * SIDE + (by + dy) % SIDE

    def x_peer(k):
        return (ax + k) % SIDE * SIDE + by

    def y_peer(k):
        return ax * SIDE + (by + k) % SIDE

    def remote(src, dst, send, recv, to_dom, to_tp):
        return pltpu.make_async_remote_copy(
            src_ref=src, dst_ref=dst, send_sem=send, recv_sem=recv,
            device_id=(to_dom, to_tp), device_id_type=MESH,
        )

    def each(count, act, unroll=1):
        def body(q, carry):
            act(q)
            return carry

        lax.fori_loop(0, count, body, 0, unroll=unroll)

    pre = [
        pltpu.make_async_copy(
            latent.at[:, pl.ds(pl.multiple_of(me * 256, 256), 256)], x_in.at[me], pre_sem.at[7]
        ),
        pltpu.make_async_copy(w1, own1.at[core], pre_sem.at[8]),
        pltpu.make_async_copy(w2, own2.at[core], pre_sem.at[9]),
    ]
    for half in range(2):
        lanes = pl.ds(pl.multiple_of(by * 256 + 128 * half, 128), 128)
        for i, matrix in enumerate([w1, w2]):
            pre.append(
                pltpu.make_async_copy(
                    matrix.at[pl.ds(ax * 16, 16), lanes],
                    pieces.at[half, i], pre_sem.at[2 * i + half],
                )
            )
        pre.append(
            pltpu.make_async_copy(
                we.at[pl.ds((by, ax)[half] * 16, 16), pl.ds(128 * half, 128)],
                pieces.at[half, 2], pre_sem.at[4 + half],
            )
        )
    for copy in pre:
        copy.start()

    small = [
        pltpu.make_async_copy(src, dst, pre_sem.at[10 + i])
        for i, (src, dst) in enumerate(
            [
                (dest, dest_ref), (fill, fill_ref), (ev, ev_ref), (cen, cen_ref),
                (spec, spec_ref), (gains, gain_ref),
            ]
        )
    ]
    for copy in small:
        copy.start()
    barrier = pltpu.get_barrier_semaphore()

    def greet_tp(q):
        pl.semaphore_signal(barrier, inc=1, device_id=(dom, tp_far(q)), device_id_type=MESH)

    each(NTP - 1, greet_tp)
    for q in range(NDOM - 1):
        pl.semaphore_signal(barrier, inc=1, device_id=(dom_far(q), me), device_id_type=MESH)
    for copy in pre:
        copy.wait()
    ring[pl.ds(14 + core, 1)] = pieces[pl.ds(core, 1)]
    pl.semaphore_wait(barrier, NTP - 1 + NDOM - 1)

    def one_copy(n, c):
        to = 2 * ((z + NEAR_Z[n]) % DEPTH) + c
        return remote(
            pieces.at[c], ring.at[2 * n + core], one_send.at[2 * n + c],
            one_recv.at[2 * n + core], dom, to,
        )

    def one_arrival(slot):
        remote(
            pieces.at[0], ring.at[slot], one_send.at[slot], one_recv.at[slot], dom, sib
        ).wait_recv()

    tile_copies = [one_copy(n, c) for n in range(7) for c in range(2)]
    tile_copies.append(
        remote(
            pieces.at[other], ring.at[14 + core], one_send.at[14], one_recv.at[14], dom, sib
        )
    )
    own_copies = [
        remote(ref.at[core], ref.at[core], own_send.at[i], own_recv.at[i], dom, sib)
        for i, ref in enumerate([own1, own2])
    ]
    for copy in tile_copies + own_copies:
        copy.start()

    def lat_copy(q):
        to = tp_far(q)
        return remote(
            latent.at[:, pl.ds(pl.multiple_of(to * 256, 256), 256)], x_in.at[me],
            lat_send.at[q], lat_recv.at[q], dom, to,
        )

    def w_copy(q):
        to = tp_far(q)
        return remote(ws.at[to], wt.at[me], w_send.at[q], w_recv.at[q], dom, to)

    def ln_copy(q):
        to = tp_far(q)
        return remote(
            ln.at[to], ln_out.at[:, pl.ds(pl.multiple_of(me * 256, 256), 256)],
            ln_send.at[q], ln_recv.at[q], dom, to,
        )

    for copy in small:
        copy.wait()

    def harmonics(t):
        v = ev_ref[:, pl.ds(pl.multiple_of(t * 256, 256), 256)]
        along_x, along_y, along_z = v[0:1], v[1:2], v[2:3]
        radius = jnp.sqrt(along_x * along_x + along_y * along_y + along_z * along_z)
        ux = along_x / radius
        uy = along_y / radius
        uz = along_z / radius
        ratio = radius / cutoff_radius
        flat = 1.0 - ratio * ratio
        envelope = flat * flat
        spot = lax.broadcasted_iota(jnp.int32, (1, 128), 1)
        alive = jnp.concatenate(
            [(spot < fill_ref[2 * t + j]).astype(F32) for j in range(2)], axis=1
        )
        rows = [
            envelope,
            root_three * ux * envelope,
            root_three * uy * envelope,
            root_three * uz * envelope,
            root_fifteen * ux * uy * envelope,
            root_fifteen * uy * uz * envelope,
            root_five / 2.0 * (3.0 * uz * uz - 1.0) * envelope,
            root_fifteen * ux * uz * envelope,
            root_fifteen / 2.0 * (ux * ux - uy * uy) * envelope,
            alive,
        ]
        for m, row in enumerate(rows):
            hs[t, m : m + 1, :] = row

    each(NTP, harmonics)

    def make_onehot(b):
        atoms = lax.broadcasted_iota(jnp.int32, (128, 128), 0)
        onehot[b] = (atoms == cen_ref[pl.ds(b, 1), :]).astype(F32).astype(BF16)

    each(32, make_onehot)

    groups = [slice(0, 8), slice(8, 14)]
    spans = [pl.ds(0, 8), pl.ds(8, 6)]

    def quad(g, kind, k, half=None):
        part = slice(None) if half is None else pl.ds(2 * half, 2)
        if kind == 0:
            return g1.at[core, (by + SIDE - k) % SIDE, part, spans[g]]
        return g2.at[core, (ax + SIDE - k) % SIDE, part, spans[g]]

    def sib_copy(g, kind, k, half=None):
        ref = quad(g, kind, k, half)
        slot = k if half is None else 2 + 2 * half
        return remote(
            ref, ref, sib_send.at[g, kind, slot], sib_recv.at[g, kind, slot], dom, sib
        )

    def second_peer(kind, k):
        return (y_peer, x_peer)[kind](k)

    first = []
    second = []
    across = []
    env_row = by * other + ax * core
    env_copies = []
    for g in range(2):
        for slot in range(groups[g].start, groups[g].stop):
            one_arrival(slot)
        tiles = ring[groups[g]]
        g1[pl.ds(core, 1), pl.ds(by, 1), pl.ds(ax, 1), groups[g]] = tiles[:, 0][None, None, None]
        g2[pl.ds(core, 1), pl.ds(ax, 1), pl.ds(by, 1), groups[g]] = tiles[:, 1][None, None, None]
        copies = []
        for k in (2, 1, 3):
            one = g1.at[core, by, ax, spans[g]]
            copies.append(remote(one, one, a_send.at[g, 0, k], a_recv.at[g, 0, k], x_peer(k), me))
            two = g2.at[core, ax, by, spans[g]]
            copies.append(remote(two, two, a_send.at[g, 1, k], a_recv.at[g, 1, k], y_peer(k), me))
        for copy in copies:
            copy.start()
        first.append(copies)
        if g == 0:
            each(15, lambda q: lat_copy(q).start())
        if g == 1:
            tile_copies[14].wait_recv()
            for n in range(7):
                for c in range(2):
                    chip = (z + DEPTH - NEAR_Z[n]) % DEPTH
                    ge[pl.ds(core, 1), pl.ds(2 * chip + c, 1), pl.ds(env_row, 1)] = ring[
                        2 * n + c, 2
                    ][None, None, None]
            for c in range(2):
                ge[pl.ds(core, 1), pl.ds(2 * z + c, 1), pl.ds(env_row, 1)] = ring[14 + c, 2][
                    None, None, None
                ]
            for k in (2, 1, 3):
                three = ge.at[core, :, env_row]
                to = (ax + k * core) % SIDE * SIDE + (by + k * other) % SIDE
                env_copies.append(remote(three, three, e_send.at[k], e_recv.at[k], to, me))
            for copy in env_copies:
                copy.start()
        for copy in copies:
            copy.wait_recv()
        copies = {}
        for k in (1, 3):
            for kind in range(2):
                mine = quad(g, kind, 0)
                copies[kind, k] = remote(
                    mine, mine, b_send.at[g, kind, k], b_recv.at[g, kind, k],
                    second_peer(kind, k), me,
                )
                copies[kind, k].start()
        second.append(copies)
        for kind in range(2):
            copy = sib_copy(g, kind, 0)
            copy.start()
            across.append(copy)

    def make_slots(d):
        found = [jnp.int32(32)] * 4
        for b in range(32):
            hit = dest_ref[b] == d
            found = [jnp.where(hit, new, old) for new, old in zip([b] + found[:3], found)]
        for s in range(4):
            slots[4 * d + s] = found[s]

    relays = []
    for g in range(2):
        copies = {}
        for half, k in enumerate((1, 3)):
            for kind in range(2):
                second[g][kind, k].wait_recv()
                theirs = quad(g, kind, k, half)
                copies[kind, half] = remote(
                    theirs, theirs, b_send.at[g, kind, 2 * half], b_recv.at[g, kind, 2 * half],
                    second_peer(kind, k), me,
                )
                copies[kind, half].start()
        relays.append(copies)
        for k in (1, 3):
            for kind in range(2):
                copy = sib_copy(g, kind, k)
                copy.start()
                across.append(copy)
        if g == 0:
            each(NDOM, make_slots)
            sums[32] = jnp.zeros((144, 128), F32)
            same = lax.broadcasted_iota(jnp.int32, (16, 16), 0) == lax.broadcasted_iota(
                jnp.int32, (16, 16), 1
            )
            gain = jnp.zeros((16, 128), F32)
            for s in range(4):
                column = jnp.sum(jnp.where(same, gain_ref[s : s + 1, :], 0.0), axis=1, keepdims=True)
                gain = gain + jnp.where(spec_ref[...] == s, column, 0.0)
    for copy in env_copies:
        copy.wait_recv()
    last = remote(ge.at[core], ge.at[core], own_send.at[2], own_recv.at[2], dom, sib)
    last.start()
    across.append(last)
    each(15, lambda q: lat_copy(q).wait_recv())
    for n in range(4):
        block = x_in[4 * n : 4 * n + 4].reshape(256, 256).astype(F32)
        x_t[:, 256 * n : 256 * n + 256] = block.T.astype(BF16)
    for g in range(2):
        for half in range(2):
            for kind in range(2):
                relays[g][kind, half].wait_recv()
                copy = sib_copy(g, kind, 2, half)
                copy.start()
                across.append(copy)

    def sib_arrivals(kind):
        own_copies[kind].wait_recv()
        for g in range(2):
            for k in (0, 1, 3):
                sib_copy(g, kind, k).wait_recv()
            for half in range(2):
                sib_copy(g, kind, 2, half).wait_recv()

    sib_arrivals(0)

    def first_layer(r):
        tiles = jnp.concatenate(
            [g1[c, b, r].reshape(224, 128) for b in range(SIDE) for c in range(2)], axis=1
        )
        rows = pl.ds(pl.multiple_of(16 * r, 16), 16)
        matrix = jnp.concatenate([tiles, own1[0, rows, :], own1[1, rows, :]], axis=0)
        v = dot(x_t[...], matrix, ((1,), (1,)))
        hid[r] = (v / (1.0 + jnp.exp(-v))).astype(BF16)

    each(SIDE, first_layer)
    sib_arrivals(1)
    for b in range(SIDE):
        lanes = slice(256 * b, 256 * b + 256)
        update = jnp.zeros((256, 256), F32)
        for r in range(SIDE):
            tiles = jnp.concatenate([g2[c, r, b].reshape(224, 128) for c in range(2)], axis=1)
            rows = slice(16 * r, 16 * r + 16)
            matrix = jnp.concatenate([tiles, own2[0, rows, lanes], own2[1, rows, lanes]], axis=0)
            update = update + dot(hid[r], matrix, ((1,), (0,)))
        lnt[:, lanes] = (x_t[:, lanes].astype(F32) + update).astype(BF16)

    last.wait_recv()
    matrix = jnp.concatenate([ge[c].reshape(1024, 128) for c in range(2)], axis=1)
    env_weights = dot(lnt[...], matrix, ((1,), (0,)))
    ws[...] = env_weights.T.astype(BF16).reshape(16, 16, 256)
    each(15, lambda q: w_copy(q).start())
    wt[pl.ds(me, 1)] = ws[pl.ds(me, 1)]

    for b in range(SIDE):
        block = lnt[:, 256 * b : 256 * b + 256].astype(F32).T.astype(BF16)
        ln[4 * b : 4 * b + 4] = block.reshape(4, 64, 256)
    def block_sums(t):
        w = wt[t].astype(F32)
        h = hs[t]
        for j in range(2):
            lanes = slice(128 * j, 128 * j + 128)
            wj = w[:, lanes]
            alive = h[9:10, lanes]
            contrib = jnp.concatenate(
                [((h[m : m + 1, lanes] * wj) * alive).astype(BF16) for m in range(9)], axis=0
            )
            sums[2 * t + j] = dot(contrib, onehot[2 * t + j], ((1,), (1,)))

    each(15, lambda q: w_copy(q).wait_recv())
    each(NTP, block_sums, unroll=8)

    def domain_sum(d):
        total = sums[slots[4 * d]] + sums[slots[4 * d + 1]]
        return total + (sums[slots[4 * d + 2]] + sums[slots[4 * d + 3]])

    def q_copy(part, q):
        out, into = ((p_low, in_low), (p_high, in_high))[part]
        to = dom_far(q)
        return remote(
            out.at[to], into.at[dom], q_send.at[part, q], q_recv.at[part, q], to, me
        )

    def t_copy(part, q):
        ref = (table_low, table_high)[part]
        return remote(
            ref.at[dom], ref.at[dom], t_send.at[part, q], t_recv.at[part, q], dom_far(q), me
        )

    for q in range(NDOM - 1):
        to = dom_far(q)
        total = domain_sum(to).astype(BF16)
        p_low[pl.ds(to, 1)] = total[None, :64]
        p_high[pl.ds(to, 1)] = total[None, 64:]
        q_copy(0, q).start()
    for q in range(NDOM - 1):
        q_copy(1, q).start()
    own = pltpu.make_async_copy(
        ln.at[me], ln_out.at[:, pl.ds(pl.multiple_of(me * 256, 256), 256)], pre_sem.at[6]
    )
    own.start()
    each(15, lambda q: ln_copy(q).start())
    total = domain_sum(dom)
    in_low[pl.ds(dom, 1)] = jnp.zeros((1, 64, 128), BF16)
    in_high[pl.ds(dom, 1)] = jnp.zeros((1, 80, 128), BF16)
    for part in range(2):
        into, ref = ((in_low, table_low), (in_high, table_high))[part]
        rows = (slice(0, 64), slice(64, 144))[part]
        comps = (slice(0, 4), slice(4, 9))[part]
        for q in range(NDOM - 1):
            q_copy(part, q).wait_recv()

        acc = total[rows]
        for d in range(NDOM):
            acc = acc + into[d].astype(F32)
        env = acc.reshape(-1, 16, 128) * gain[None] * env_factor
        ref[pl.ds(dom, 1)] = env.reshape(1, -1, 128).astype(BF16)
        for q in range(NDOM - 1):
            t_copy(part, q).start()
        env_out[comps] = env

    def finish(t, part):
        w = wt[t].astype(F32)
        h = hs[t]
        ref = (table_low, table_high)[part]
        base = (0, 4)[part]
        spans_of = (((0,), (1, 2, 3)), ((4, 5, 6, 7, 8),))[part]
        parts = [[] for _ in spans_of]
        for j in range(2):
            lanes = slice(128 * j, 128 * j + 128)
            env_edge = dot(ref[dest_ref[2 * t + j]], onehot[2 * t + j], ((1,), (0,)))
            for l, comps in enumerate(spans_of):
                degree = None
                for m in comps:
                    term = env_edge[16 * (m - base) : 16 * (m - base) + 16] * h[m : m + 1, lanes]
                    degree = term if degree is None else degree + term
                parts[l].append(degree * w[:, lanes] * h[9:10, lanes])
        for l in range(len(spans_of)):
            inv_out[(0, 2)[part] + l, :, pl.ds(pl.multiple_of(t * 256, 256), 256)] = (
                jnp.concatenate(parts[l], axis=1)
            )

    for part in range(2):
        for q in range(NDOM - 1):
            t_copy(part, q).wait_recv()
        each(NTP, lambda t: finish(t, part), unroll=8)

    own.wait()
    each(15, lambda q: ln_copy(q).wait_recv())
    for copy in tile_copies + own_copies + first[0] + first[1] + env_copies:
        copy.wait_send()
    for copy in across:
        copy.wait_send()
    for copies in second + relays:
        for copy in copies.values():
            copy.wait_send()
    for make in (lat_copy, w_copy, ln_copy):
        each(15, lambda q: make(q).wait_send())
    for part in range(2):
        for q in range(NDOM - 1):
            q_copy(part, q).wait_send()
            t_copy(part, q).wait_send()


def write_out(ln_in, env_in, inv_in, ln_out, env_out, inv_out, ln, env, inv, sem_in, sem_out):
    parts = [(env_in, env, env_out)]
    for n in range(2):
        rows = pl.ds(32 * n, 32)
        parts.append((ln_in.at[rows], ln.at[rows], ln_out.at[rows]))
    for l in range(3):
        parts.append((inv_in.at[l], inv.at[l], inv_out.at[l]))
    reads = [
        pltpu.make_async_copy(src, mid, sem_in.at[n]) for n, (src, mid, _) in enumerate(parts)
    ]
    writes = [
        pltpu.make_async_copy(mid, dst, sem_out.at[n]) for n, (_, mid, dst) in enumerate(parts)
    ]
    for copy in reads:
        copy.start()
    for read, write in zip(reads, writes):
        read.wait()
        write.start()
    for copy in writes:
        copy.wait()


def on_device(
    latent, w_first, w_second, w_env, edge_vec, centers, block_dest, block_fill, species,
    species_gain,
):
    vmem = pl.BlockSpec(memory_space=pltpu.VMEM)
    hbm = pl.BlockSpec(memory_space=pltpu.HBM)
    dma = pltpu.SemaphoreType.DMA
    shapes = (
        jax.ShapeDtypeStruct((64, 4096), BF16),
        jax.ShapeDtypeStruct((9, 16, 128), F32),
        jax.ShapeDtypeStruct((3, 16, 4096), F32),
    )
    results = pl.pallas_call(
        kernel,
        out_shape=shapes,
        in_specs=[hbm] * 10,
        out_specs=(vmem, vmem, vmem),
        scratch_shapes=[
            pltpu.SMEM((32,), jnp.int32),
            pltpu.SMEM((32,), jnp.int32),
            pltpu.VMEM((3, 4096), F32),
            pltpu.VMEM((32, 128), jnp.int32),
            pltpu.VMEM((1, 128), jnp.int32),
            pltpu.VMEM((4, 16), F32),
            pltpu.VMEM((2, 3, 16, 128), BF16),
            pltpu.VMEM((16, 3, 16, 128), BF16),
            pltpu.VMEM((2, 64, 1024), BF16),
            pltpu.VMEM((2, 64, 1024), BF16),
            pltpu.VMEM((2, 4, 4, 14, 16, 128), BF16),
            pltpu.VMEM((2, 4, 4, 14, 16, 128), BF16),
            pltpu.VMEM((2, 16, 4, 16, 128), BF16),
            pltpu.VMEM((16, 64, 256), BF16),
            pltpu.VMEM((256, 1024), BF16),
            pltpu.VMEM((4, 256, 256), BF16),
            pltpu.VMEM((256, 1024), BF16),
            pltpu.VMEM((16, 64, 256), BF16),
            pltpu.VMEM((16, 16, 256), BF16),
            pltpu.VMEM((16, 16, 256), BF16),
            pltpu.VMEM((16, 16, 256), F32),
            pltpu.VMEM((32, 128, 128), BF16),
            pltpu.SMEM((64,), jnp.int32),
            pltpu.VMEM((33, 144, 128), F32),
            pltpu.VMEM((16, 64, 128), BF16),
            pltpu.VMEM((16, 80, 128), BF16),
            pltpu.VMEM((16, 64, 128), BF16),
            pltpu.VMEM((16, 80, 128), BF16),
            pltpu.VMEM((16, 64, 128), BF16),
            pltpu.VMEM((16, 80, 128), BF16),
            dma((16,)),
            dma((15,)), dma((15,)), dma((15,)), dma((15,)), dma((3,)), dma((3,)),
            dma((2, 2, 4)), dma((2, 2, 4)), dma((2, 2, 4)), dma((2, 2, 4)), dma((4,)), dma((4,)),
            dma((2, 2, 5)), dma((2, 2, 5)),
            dma((15,)), dma((15,)), dma((15,)), dma((15,)),
            dma((2, 15)), dma((2, 15)), dma((2, 15)), dma((2, 15)),
        ],
        compiler_params=pltpu.CompilerParams(
            collective_id=0, has_side_effects=True, vmem_limit_bytes=60 * 1024 * 1024
        ),
        cost_estimate=pl.CostEstimate(
            flops=2 * 10**9, bytes_accessed=4 * 10**6, transcendentals=300000
        ),
        name="allegro",
    )(
        block_dest.reshape(32), block_fill, latent, w_first.T, w_second, w_env, edge_vec,
        centers.reshape(32, 128), species.reshape(1, 128), species_gain,
    )
    return pl.pallas_call(
        write_out,
        out_shape=shapes,
        in_specs=[hbm] * 3,
        out_specs=(hbm,) * 3,
        scratch_shapes=[
            pltpu.VMEM((64, 4096), BF16),
            pltpu.VMEM((9, 16, 128), F32),
            pltpu.VMEM((3, 16, 4096), F32),
            dma((6,)),
            dma((6,)),
        ],
        compiler_params=pltpu.CompilerParams(vmem_limit_bytes=60 * 1024 * 1024),
        name="write_out",
    )(*results)


def solution(mesh):
    in_specs = (
        P("tp", "dom"),
        P(None, "tp"),
        P("tp", None),
        P("tp", None),
        P(None, "dom"),
        P("dom"),
        P("dom", None),
        P("dom"),
        P("dom"),
        P(None, "tp"),
    )
    out_specs = (P("tp", "dom"), P(None, "tp", "dom"), P(None, "tp", "dom"))
    return jax.shard_map(
        on_device, mesh=mesh, in_specs=in_specs, out_specs=out_specs, check_vma=False
    )
```

```python
import math

import jax
import jax.numpy as jnp
from jax import lax
from jax.experimental import pallas as pl
from jax.experimental.pallas import tpu as pltpu
from jax.sharding import PartitionSpec as P

MESH = pl.DeviceIdType.MESH
F32 = jnp.float32
BF16 = jnp.bfloat16

root_three = math.sqrt(3.0)
root_five = math.sqrt(5.0)
root_fifteen = math.sqrt(15.0)
cutoff_radius = 6.0
env_factor = 0.25

SIDE = 4
NDOM = 16
NTP = 16
DEPTH = 8
HALF = DEPTH // 2
NEAR_Z = (6, 2, 7, 1, 4, 5, 3)
FAR = sorted(
    [(dx, dy) for dx in range(SIDE) for dy in range(SIDE) if dx or dy],
    key=lambda d: -min(d[0], SIDE - d[0]) - min(d[1], SIDE - d[1]),
)


def dot(left, right, dims):
    return lax.dot_general(left, right, (dims, ((), ())), preferred_element_type=F32)


def kernel(
    dest, fill, latent, w1, w2, we, ev, cen, spec, gains,
    ln_out, env_out, inv_out,
    dest_ref, fill_ref, ev_ref, cen_ref, spec_ref, gain_ref,
    pieces, ring, own1, own2, g1, g2, ge, x_in, x_t, hid, lnt, ln, ws, wt, hs, onehot, slots,
    sums, p_low, p_high, in_low, in_high, table_low, table_high,
    pre_sem, lat_send, lat_recv, one_send, one_recv, own_send, own_recv,
    a_send, a_recv, b_send, b_recv, e_send, e_recv,
    sib_send, sib_recv, w_send, w_recv, ln_send, ln_recv, q_send, q_recv, t_send, t_recv,
):
    dom = lax.axis_index("dom")
    me = lax.axis_index("tp")
    ax = dom // SIDE
    by = dom % SIDE
    core = me % 2
    other = 1 - core
    z = me // 2
    sib = 2 * z + other

    def tp_far(q):
        s = q // 2
        dz = HALF + (s + 1) // 2 * (1 - 2 * (s % 2))
        return 2 * ((z + dz) % DEPTH) + (core + 1 + q) % 2

    def dom_far(q):
        dx, dy = FAR[q]
        return (ax + dx) % SIDE * SIDE + (by + dy) % SIDE

    def x_peer(k):
        return (ax + k) % SIDE * SIDE + by

    def y_peer(k):
        return ax * SIDE + (by + k) % SIDE

    def remote(src, dst, send, recv, to_dom, to_tp):
        return pltpu.make_async_remote_copy(
            src_ref=src, dst_ref=dst, send_sem=send, recv_sem=recv,
            device_id=(to_dom, to_tp), device_id_type=MESH,
        )

    def each(count, act, unroll=1):
        def body(q, carry):
            act(q)
            return carry

        lax.fori_loop(0, count, body, 0, unroll=unroll)

    pre = [
        pltpu.make_async_copy(
            latent.at[:, pl.ds(pl.multiple_of(me * 256, 256), 256)], x_in.at[me], pre_sem.at[7]
        ),
        pltpu.make_async_copy(w1, own1.at[core], pre_sem.at[8]),
        pltpu.make_async_copy(w2, own2.at[core], pre_sem.at[9]),
    ]
    for half in range(2):
        lanes = pl.ds(pl.multiple_of(by * 256 + 128 * half, 128), 128)
        for i, matrix in enumerate([w1, w2]):
            pre.append(
                pltpu.make_async_copy(
                    matrix.at[pl.ds(ax * 16, 16), lanes],
                    pieces.at[half, i], pre_sem.at[2 * i + half],
                )
            )
        pre.append(
            pltpu.make_async_copy(
                we.at[pl.ds((by, ax)[half] * 16, 16), pl.ds(128 * half, 128)],
                pieces.at[half, 2], pre_sem.at[4 + half],
            )
        )
    for copy in pre:
        copy.start()

    small = [
        pltpu.make_async_copy(src, dst, pre_sem.at[10 + i])
        for i, (src, dst) in enumerate(
            [
                (dest, dest_ref), (fill, fill_ref), (ev, ev_ref), (cen, cen_ref),
                (spec, spec_ref), (gains, gain_ref),
            ]
        )
    ]
    for copy in small:
        copy.start()
    barrier = pltpu.get_barrier_semaphore()

    def greet_tp(q):
        pl.semaphore_signal(barrier, inc=1, device_id=(dom, tp_far(q)), device_id_type=MESH)

    each(NTP - 1, greet_tp, unroll=NTP - 1)
    for q in range(NDOM - 1):
        pl.semaphore_signal(barrier, inc=1, device_id=(dom_far(q), me), device_id_type=MESH)
    for copy in pre:
        copy.wait()
    ring[pl.ds(14 + core, 1)] = pieces[pl.ds(core, 1)]
    pl.semaphore_wait(barrier, NTP - 1 + NDOM - 1)

    def one_copy(n, c):
        to = 2 * ((z + NEAR_Z[n]) % DEPTH) + c
        return remote(
            pieces.at[c], ring.at[2 * n + core], one_send.at[2 * n + c],
            one_recv.at[2 * n + core], dom, to,
        )

    def one_arrival(slot):
        remote(
            pieces.at[0], ring.at[slot], one_send.at[slot], one_recv.at[slot], dom, sib
        ).wait_recv()

    tile_copies = [one_copy(n, c) for n in range(7) for c in range(2)]
    tile_copies.append(
        remote(
            pieces.at[other], ring.at[14 + core], one_send.at[14], one_recv.at[14], dom, sib
        )
    )
    own_copies = [
        remote(ref.at[core], ref.at[core], own_send.at[i], own_recv.at[i], dom, sib)
        for i, ref in enumerate([own1, own2])
    ]
    for copy in tile_copies + own_copies:
        copy.start()

    def lat_copy(q):
        to = tp_far(q)
        return remote(
            latent.at[:, pl.ds(pl.multiple_of(to * 256, 256), 256)], x_in.at[me],
            lat_send.at[q], lat_recv.at[q], dom, to,
        )

    def w_copy(q):
        to = tp_far(q)
        return remote(ws.at[to], wt.at[me], w_send.at[q], w_recv.at[q], dom, to)

    def ln_copy(q):
        to = tp_far(q)
        return remote(
            ln.at[to], ln_out.at[:, pl.ds(pl.multiple_of(me * 256, 256), 256)],
            ln_send.at[q], ln_recv.at[q], dom, to,
        )

    for copy in small:
        copy.wait()

    def harmonics(t):
        v = ev_ref[:, pl.ds(pl.multiple_of(t * 256, 256), 256)]
        along_x, along_y, along_z = v[0:1], v[1:2], v[2:3]
        radius = jnp.sqrt(along_x * along_x + along_y * along_y + along_z * along_z)
        ux = along_x / radius
        uy = along_y / radius
        uz = along_z / radius
        ratio = radius / cutoff_radius
        flat = 1.0 - ratio * ratio
        envelope = flat * flat
        spot = lax.broadcasted_iota(jnp.int32, (1, 128), 1)
        alive = jnp.concatenate(
            [(spot < fill_ref[2 * t + j]).astype(F32) for j in range(2)], axis=1
        )
        rows = [
            envelope,
            root_three * ux * envelope,
            root_three * uy * envelope,
            root_three * uz * envelope,
            root_fifteen * ux * uy * envelope,
            root_fifteen * uy * uz * envelope,
            root_five / 2.0 * (3.0 * uz * uz - 1.0) * envelope,
            root_fifteen * ux * uz * envelope,
            root_fifteen / 2.0 * (ux * ux - uy * uy) * envelope,
            alive,
        ]
        for m, row in enumerate(rows):
            hs[t, m : m + 1, :] = row

    each(NTP, harmonics)

    def make_onehot(b):
        atoms = lax.broadcasted_iota(jnp.int32, (128, 128), 0)
        onehot[b] = (atoms == cen_ref[pl.ds(b, 1), :]).astype(F32).astype(BF16)

    each(32, make_onehot)

    groups = [slice(0, 8), slice(8, 14)]
    spans = [pl.ds(0, 8), pl.ds(8, 6)]

    def quad(g, kind, k, half=None):
        part = slice(None) if half is None else pl.ds(2 * half, 2)
        if kind == 0:
            return g1.at[core, (by + SIDE - k) % SIDE, part, spans[g]]
        return g2.at[core, (ax + SIDE - k) % SIDE, part, spans[g]]

    def sib_copy(g, kind, k, half=None):
        ref = quad(g, kind, k, half)
        slot = k if half is None else 2 + 2 * half
        return remote(
            ref, ref, sib_send.at[g, kind, slot], sib_recv.at[g, kind, slot], dom, sib
        )

    def second_peer(kind, k):
        return (y_peer, x_peer)[kind](k)

    first = []
    second = []
    across = []
    env_row = by * other + ax * core
    env_copies = []
    for g in range(2):
        for slot in range(groups[g].start, groups[g].stop):
            one_arrival(slot)
        tiles = ring[groups[g]]
        g1[pl.ds(core, 1), pl.ds(by, 1), pl.ds(ax, 1), groups[g]] = tiles[:, 0][None, None, None]
        g2[pl.ds(core, 1), pl.ds(ax, 1), pl.ds(by, 1), groups[g]] = tiles[:, 1][None, None, None]
        copies = []
        for k in (2, 1, 3):
            one = g1.at[core, by, ax, spans[g]]
            copies.append(remote(one, one, a_send.at[g, 0, k], a_recv.at[g, 0, k], x_peer(k), me))
            two = g2.at[core, ax, by, spans[g]]
            copies.append(remote(two, two, a_send.at[g, 1, k], a_recv.at[g, 1, k], y_peer(k), me))
        for copy in copies:
            copy.start()
        first.append(copies)
        if g == 0:
            each(15, lambda q: lat_copy(q).start())
        if g == 1:
            tile_copies[14].wait_recv()
            for n in range(7):
                for c in range(2):
                    chip = (z + DEPTH - NEAR_Z[n]) % DEPTH
                    ge[pl.ds(core, 1), pl.ds(2 * chip + c, 1), pl.ds(env_row, 1)] = ring[
                        2 * n + c, 2
                    ][None, None, None]
            for c in range(2):
                ge[pl.ds(core, 1), pl.ds(2 * z + c, 1), pl.ds(env_row, 1)] = ring[14 + c, 2][
                    None, None, None
                ]
            for k in (2, 1, 3):
                three = ge.at[core, :, env_row]
                to = (ax + k * core) % SIDE * SIDE + (by + k * other) % SIDE
                env_copies.append(remote(three, three, e_send.at[k], e_recv.at[k], to, me))
            for copy in env_copies:
                copy.start()
        for copy in copies:
            copy.wait_recv()
        copies = {}
        for k in (1, 3):
            for kind in range(2):
                mine = quad(g, kind, 0)
                copies[kind, k] = remote(
                    mine, mine, b_send.at[g, kind, k], b_recv.at[g, kind, k],
                    second_peer(kind, k), me,
                )
                copies[kind, k].start()
        second.append(copies)
        for kind in range(2):
            copy = sib_copy(g, kind, 0)
            copy.start()
            across.append(copy)

    def make_slots(d):
        found = [jnp.int32(32)] * 4
        for b in range(32):
            hit = dest_ref[b] == d
            found = [jnp.where(hit, new, old) for new, old in zip([b] + found[:3], found)]
        for s in range(4):
            slots[4 * d + s] = found[s]

    relays = []
    for g in range(2):
        copies = {}
        for half, k in enumerate((1, 3)):
            for kind in range(2):
                second[g][kind, k].wait_recv()
                theirs = quad(g, kind, k, half)
                copies[kind, half] = remote(
                    theirs, theirs, b_send.at[g, kind, 2 * half], b_recv.at[g, kind, 2 * half],
                    second_peer(kind, k), me,
                )
                copies[kind, half].start()
        relays.append(copies)
        for k in (1, 3):
            for kind in range(2):
                copy = sib_copy(g, kind, k)
                copy.start()
                across.append(copy)
        if g == 0:
            each(NDOM, make_slots)
            sums[32] = jnp.zeros((144, 128), F32)
            same = lax.broadcasted_iota(jnp.int32, (16, 16), 0) == lax.broadcasted_iota(
                jnp.int32, (16, 16), 1
            )
            gain = jnp.zeros((16, 128), F32)
            for s in range(4):
                column = jnp.sum(jnp.where(same, gain_ref[s : s + 1, :], 0.0), axis=1, keepdims=True)
                gain = gain + jnp.where(spec_ref[...] == s, column, 0.0)
    for copy in env_copies:
        copy.wait_recv()
    last = remote(ge.at[core], ge.at[core], own_send.at[2], own_recv.at[2], dom, sib)
    last.start()
    across.append(last)
    each(15, lambda q: lat_copy(q).wait_recv())
    for n in range(4):
        block = x_in[4 * n : 4 * n + 4].reshape(256, 256).astype(F32)
        x_t[:, 256 * n : 256 * n + 256] = block.T.astype(BF16)
    for g in range(2):
        for half in range(2):
            for kind in range(2):
                relays[g][kind, half].wait_recv()
                copy = sib_copy(g, kind, 2, half)
                copy.start()
                across.append(copy)

    def sib_arrivals(kind):
        own_copies[kind].wait_recv()
        for g in range(2):
            for k in (0, 1, 3):
                sib_copy(g, kind, k).wait_recv()
            for half in range(2):
                sib_copy(g, kind, 2, half).wait_recv()

    sib_arrivals(0)

    def first_layer(r):
        tiles = jnp.concatenate(
            [g1[c, b, r].reshape(224, 128) for b in range(SIDE) for c in range(2)], axis=1
        )
        rows = pl.ds(pl.multiple_of(16 * r, 16), 16)
        matrix = jnp.concatenate([tiles, own1[0, rows, :], own1[1, rows, :]], axis=0)
        v = dot(x_t[...], matrix, ((1,), (1,)))
        hid[r] = (v / (1.0 + jnp.exp(-v))).astype(BF16)

    each(SIDE, first_layer)
    sib_arrivals(1)
    for b in range(SIDE):
        lanes = slice(256 * b, 256 * b + 256)
        update = jnp.zeros((256, 256), F32)
        for r in range(SIDE):
            tiles = jnp.concatenate([g2[c, r, b].reshape(224, 128) for c in range(2)], axis=1)
            rows = slice(16 * r, 16 * r + 16)
            matrix = jnp.concatenate([tiles, own2[0, rows, lanes], own2[1, rows, lanes]], axis=0)
            update = update + dot(hid[r], matrix, ((1,), (0,)))
        lnt[:, lanes] = (x_t[:, lanes].astype(F32) + update).astype(BF16)

    last.wait_recv()
    matrix = jnp.concatenate([ge[c].reshape(1024, 128) for c in range(2)], axis=1)
    env_weights = dot(lnt[...], matrix, ((1,), (0,)))
    ws[...] = env_weights.T.astype(BF16).reshape(16, 16, 256)
    each(15, lambda q: w_copy(q).start(), unroll=15)
    wt[pl.ds(me, 1)] = ws[pl.ds(me, 1)]

    for b in range(SIDE):
        block = lnt[:, 256 * b : 256 * b + 256].astype(F32).T.astype(BF16)
        ln[4 * b : 4 * b + 4] = block.reshape(4, 64, 256)
    def block_sums(t):
        w = wt[t].astype(F32)
        h = hs[t]
        for j in range(2):
            lanes = slice(128 * j, 128 * j + 128)
            wj = w[:, lanes]
            alive = h[9:10, lanes]
            contrib = jnp.concatenate(
                [((h[m : m + 1, lanes] * wj) * alive).astype(BF16) for m in range(9)], axis=0
            )
            sums[2 * t + j] = dot(contrib, onehot[2 * t + j], ((1,), (1,)))

    each(15, lambda q: w_copy(q).wait_recv(), unroll=15)
    each(NTP, block_sums, unroll=8)

    def domain_sum(d):
        total = sums[slots[4 * d]] + sums[slots[4 * d + 1]]
        return total + (sums[slots[4 * d + 2]] + sums[slots[4 * d + 3]])

    def q_copy(part, q):
        out, into = ((p_low, in_low), (p_high, in_high))[part]
        to = dom_far(q)
        return remote(
            out.at[to], into.at[dom], q_send.at[part, q], q_recv.at[part, q], to, me
        )

    def t_copy(part, q):
        ref = (table_low, table_high)[part]
        return remote(
            ref.at[dom], ref.at[dom], t_send.at[part, q], t_recv.at[part, q], dom_far(q), me
        )

    for q in range(NDOM - 1):
        to = dom_far(q)
        total = domain_sum(to).astype(BF16)
        p_low[pl.ds(to, 1)] = total[None, :64]
        p_high[pl.ds(to, 1)] = total[None, 64:]
        q_copy(0, q).start()
    for q in range(NDOM - 1):
        q_copy(1, q).start()
    own = pltpu.make_async_copy(
        ln.at[me], ln_out.at[:, pl.ds(pl.multiple_of(me * 256, 256), 256)], pre_sem.at[6]
    )
    own.start()
    each(15, lambda q: ln_copy(q).start())
    total = domain_sum(dom)
    in_low[pl.ds(dom, 1)] = jnp.zeros((1, 64, 128), BF16)
    in_high[pl.ds(dom, 1)] = jnp.zeros((1, 80, 128), BF16)
    for part in range(2):
        into, ref = ((in_low, table_low), (in_high, table_high))[part]
        rows = (slice(0, 64), slice(64, 144))[part]
        comps = (slice(0, 4), slice(4, 9))[part]
        for q in range(NDOM - 1):
            q_copy(part, q).wait_recv()

        acc = total[rows]
        for d in range(NDOM):
            acc = acc + into[d].astype(F32)
        env = acc.reshape(-1, 16, 128) * gain[None] * env_factor
        ref[pl.ds(dom, 1)] = env.reshape(1, -1, 128).astype(BF16)
        for q in range(NDOM - 1):
            t_copy(part, q).start()
        env_out[comps] = env

    def finish(t, part):
        w = wt[t].astype(F32)
        h = hs[t]
        ref = (table_low, table_high)[part]
        base = (0, 4)[part]
        spans_of = (((0,), (1, 2, 3)), ((4, 5, 6, 7, 8),))[part]
        parts = [[] for _ in spans_of]
        for j in range(2):
            lanes = slice(128 * j, 128 * j + 128)
            env_edge = dot(ref[dest_ref[2 * t + j]], onehot[2 * t + j], ((1,), (0,)))
            for l, comps in enumerate(spans_of):
                degree = None
                for m in comps:
                    term = env_edge[16 * (m - base) : 16 * (m - base) + 16] * h[m : m + 1, lanes]
                    degree = term if degree is None else degree + term
                parts[l].append(degree * w[:, lanes] * h[9:10, lanes])
        for l in range(len(spans_of)):
            inv_out[(0, 2)[part] + l, :, pl.ds(pl.multiple_of(t * 256, 256), 256)] = (
                jnp.concatenate(parts[l], axis=1)
            )

    for part in range(2):
        for q in range(NDOM - 1):
            t_copy(part, q).wait_recv()
        each(NTP, lambda t: finish(t, part), unroll=8)

    own.wait()
    each(15, lambda q: ln_copy(q).wait_recv())
    for copy in tile_copies + own_copies + first[0] + first[1] + env_copies:
        copy.wait_send()
    for copy in across:
        copy.wait_send()
    for copies in second + relays:
        for copy in copies.values():
            copy.wait_send()
    for make in (lat_copy, w_copy, ln_copy):
        each(15, lambda q: make(q).wait_send())
    for part in range(2):
        for q in range(NDOM - 1):
            q_copy(part, q).wait_send()
            t_copy(part, q).wait_send()


def write_out(ln_in, env_in, inv_in, ln_out, env_out, inv_out, ln, env, inv, sem_in, sem_out):
    parts = [(env_in, env, env_out)]
    for n in range(2):
        rows = pl.ds(32 * n, 32)
        parts.append((ln_in.at[rows], ln.at[rows], ln_out.at[rows]))
    for l in range(3):
        parts.append((inv_in.at[l], inv.at[l], inv_out.at[l]))
    reads = [
        pltpu.make_async_copy(src, mid, sem_in.at[n]) for n, (src, mid, _) in enumerate(parts)
    ]
    writes = [
        pltpu.make_async_copy(mid, dst, sem_out.at[n]) for n, (_, mid, dst) in enumerate(parts)
    ]
    for copy in reads:
        copy.start()
    for read, write in zip(reads, writes):
        read.wait()
        write.start()
    for copy in writes:
        copy.wait()


def on_device(
    latent, w_first, w_second, w_env, edge_vec, centers, block_dest, block_fill, species,
    species_gain,
):
    vmem = pl.BlockSpec(memory_space=pltpu.VMEM)
    hbm = pl.BlockSpec(memory_space=pltpu.HBM)
    dma = pltpu.SemaphoreType.DMA
    shapes = (
        jax.ShapeDtypeStruct((64, 4096), BF16),
        jax.ShapeDtypeStruct((9, 16, 128), F32),
        jax.ShapeDtypeStruct((3, 16, 4096), F32),
    )
    results = pl.pallas_call(
        kernel,
        out_shape=shapes,
        in_specs=[hbm] * 10,
        out_specs=(vmem, vmem, vmem),
        scratch_shapes=[
            pltpu.SMEM((32,), jnp.int32),
            pltpu.SMEM((32,), jnp.int32),
            pltpu.VMEM((3, 4096), F32),
            pltpu.VMEM((32, 128), jnp.int32),
            pltpu.VMEM((1, 128), jnp.int32),
            pltpu.VMEM((4, 16), F32),
            pltpu.VMEM((2, 3, 16, 128), BF16),
            pltpu.VMEM((16, 3, 16, 128), BF16),
            pltpu.VMEM((2, 64, 1024), BF16),
            pltpu.VMEM((2, 64, 1024), BF16),
            pltpu.VMEM((2, 4, 4, 14, 16, 128), BF16),
            pltpu.VMEM((2, 4, 4, 14, 16, 128), BF16),
            pltpu.VMEM((2, 16, 4, 16, 128), BF16),
            pltpu.VMEM((16, 64, 256), BF16),
            pltpu.VMEM((256, 1024), BF16),
            pltpu.VMEM((4, 256, 256), BF16),
            pltpu.VMEM((256, 1024), BF16),
            pltpu.VMEM((16, 64, 256), BF16),
            pltpu.VMEM((16, 16, 256), BF16),
            pltpu.VMEM((16, 16, 256), BF16),
            pltpu.VMEM((16, 16, 256), F32),
            pltpu.VMEM((32, 128, 128), BF16),
            pltpu.SMEM((64,), jnp.int32),
            pltpu.VMEM((33, 144, 128), F32),
            pltpu.VMEM((16, 64, 128), BF16),
            pltpu.VMEM((16, 80, 128), BF16),
            pltpu.VMEM((16, 64, 128), BF16),
            pltpu.VMEM((16, 80, 128), BF16),
            pltpu.VMEM((16, 64, 128), BF16),
            pltpu.VMEM((16, 80, 128), BF16),
            dma((16,)),
            dma((15,)), dma((15,)), dma((15,)), dma((15,)), dma((3,)), dma((3,)),
            dma((2, 2, 4)), dma((2, 2, 4)), dma((2, 2, 4)), dma((2, 2, 4)), dma((4,)), dma((4,)),
            dma((2, 2, 5)), dma((2, 2, 5)),
            dma((15,)), dma((15,)), dma((15,)), dma((15,)),
            dma((2, 15)), dma((2, 15)), dma((2, 15)), dma((2, 15)),
        ],
        compiler_params=pltpu.CompilerParams(
            collective_id=0, has_side_effects=True, vmem_limit_bytes=60 * 1024 * 1024
        ),
        cost_estimate=pl.CostEstimate(
            flops=2 * 10**9, bytes_accessed=4 * 10**6, transcendentals=300000
        ),
        name="allegro",
    )(
        block_dest.reshape(32), block_fill, latent, w_first.T, w_second, w_env, edge_vec,
        centers.reshape(32, 128), species.reshape(1, 128), species_gain,
    )
    return pl.pallas_call(
        write_out,
        out_shape=shapes,
        in_specs=[hbm] * 3,
        out_specs=(hbm,) * 3,
        scratch_shapes=[
            pltpu.VMEM((64, 4096), BF16),
            pltpu.VMEM((9, 16, 128), F32),
            pltpu.VMEM((3, 16, 4096), F32),
            dma((6,)),
            dma((6,)),
        ],
        compiler_params=pltpu.CompilerParams(vmem_limit_bytes=60 * 1024 * 1024),
        name="write_out",
    )(*results)


def solution(mesh):
    in_specs = (
        P("tp", "dom"),
        P(None, "tp"),
        P("tp", None),
        P("tp", None),
        P(None, "dom"),
        P("dom"),
        P("dom", None),
        P("dom"),
        P("dom"),
        P(None, "tp"),
    )
    out_specs = (P("tp", "dom"), P(None, "tp", "dom"), P(None, "tp", "dom"))
    return jax.shard_map(
        on_device, mesh=mesh, in_specs=in_specs, out_specs=out_specs, check_vma=False
    )
```
